32 devices in a mesh: groups: 2 (over x), kx: 16 (over z, y, core).
Axes of the slice: x: 2, y: 2, z: 4, core: 2. Of those that a mesh axis runs over, the one named last changes fastest.
Arguments:
- latent: bfloat16 [2560, 16, 128], P(('groups', 'kx')), parts along dimension 0, may hold values from -6 to 6
- cond_lists: int32 [2560, 3], P(('groups', 'kx')), parts along dimension 0, may hold values from 0 to 1279, as said below
- cond_weights: bfloat16 [2560, 3, 128, 128], P(('groups', 'kx')), parts along dimension 0, may hold values from -0.3125 to 0.3125
- precision_factor: bfloat16 [2560, 128, 128], P(('groups', 'kx')), parts along dimension 0, may hold values from -0.5 to 0.5
Outputs:
- gradient: float32 [2560, 16, 128], P(('groups', 'kx')), parts along dimension 0
The draws below stay inside these ranges and needn't reach their ends.
There are 2 independent parts, one for each index of `groups`. The reference program is written for one: setup_inputs(seed, part) draws one part's arguments, and reference() takes and returns one part's arrays. A program takes and returns all parts, laid end to end along the dimension named above; each array names one. Nothing has to cross between parts.
Inputs may be any that keep to these rules, and one draw needn't show every extreme that they name: `cond_lists`: leaf block l belongs to index l // 80 of kx. An entry of a leaf block of index d names a leaf block of index d, d - 1, d - 2, d - 4 or d - 8, never its own leaf block. For each o of 1, 2, 4, 8 with d - o not negative, exactly 30 of the 240 entries of index d name leaf blocks of index d - o; all others name leaf blocks of index d.
All inputs are finite; a program needn't handle non-finite values.
Results may differ from the reference program's by a relative error of at most 0.0037.
Values may be sent and summed in bfloat16 or wider, within the bound.
No kernel may reach another device: no remote copies, remote signals or barrier semaphores. Data moves between devices by JAX's collectives and lax.ppermute only.
A program may use at most 64 MiB of HBM per device.

```python
import jax
import jax.numpy as jnp
from jax import lax

B = 128
S = 16
LEAF_DEV = 80
LEAVES = 1280
N_KX = 16


def draw_cond_lists(key, part):
    key = jax.random.fold_in(key, 11)
    key_order, key_local = jax.random.split(key)
    slots = 3 * LEAF_DEV
    capacity = 3 * LEAF_DEV // 8
    slot_ids = jnp.arange(slots, dtype=jnp.int32)
    pattern = jnp.where(slot_ids < capacity, 1, jnp.where(slot_ids < 2 * capacity, 2, jnp.where(slot_ids < 3 * capacity, 4, jnp.where(slot_ids < 4 * capacity, 8, 0)))).astype(jnp.int32)
    orders = jax.vmap(lambda k: jax.random.permutation(k, slots))(jax.random.split(key_order, N_KX))
    offsets = pattern[orders]
    device_ids = jnp.arange(N_KX, dtype=jnp.int32)[:, None]
    offsets = jnp.where(device_ids - offsets >= 0, offsets, 0)
    owners = device_ids - offsets
    local_ids = jax.random.randint(key_local, (N_KX, slots), 0, LEAF_DEV, dtype=jnp.int32)
    own_leaf = slot_ids[None, :] // 3
    clash = (owners == device_ids) & (local_ids == own_leaf)
    local_ids = jnp.where(clash, (local_ids + 1) % LEAF_DEV, local_ids)
    return (owners * LEAF_DEV + local_ids).reshape(N_KX * LEAF_DEV, 3).astype(jnp.int32)


def shard_levels(own_key, shape, pieces, smallest, top_value):
    gain = 1.0
    for axis_at, shards_of in pieces:
        heights = jax.random.uniform(jax.random.fold_in(jax.random.fold_in(own_key, 6), axis_at), (shards_of,), jnp.float32, smallest / len(pieces), top_value / len(pieces))
        gain = gain * jnp.repeat(jnp.exp(heights), shape[axis_at] // shards_of).reshape((-1,) + (1,) * (len(shape) - 1 - axis_at))
    return gain


def centred(own_key, shape, deviation, limit, cuts=(), held_as=jnp.bfloat16):
    drawn = deviation * jax.random.normal(own_key, shape, jnp.float32)
    if cuts:
        drawn = drawn * shard_levels(own_key, shape, cuts, -0.22, 0.18)
    return jnp.clip(drawn, -limit, limit).astype(held_as)


def setup_inputs(seed: int = 0, part: int = 0) -> dict:
    seeds = jax.random.split(jax.random.key(seed), 5)
    part_keys = jax.random.split(jax.random.fold_in(seeds[4], part), 5)
    return {
        "latent": centred(part_keys[0], (LEAVES, S, B), 1.0, 6.0, ((0, 16),)),
        "cond_lists": draw_cond_lists(jax.random.fold_in(jax.random.fold_in(seeds[4], part), 71), part),
        "cond_weights": centred(part_keys[2], (LEAVES, 3, B, B), (3 * B) ** -0.5, 0.3125, ((0, 16),)),
        "precision_factor": centred(part_keys[3], (LEAVES, B, B), B ** -0.5, 0.5, ((0, 16),)),
    }


def reference(latent, cond_lists, cond_weights, precision_factor):
    block_count = LEAVES // LEAF_DEV
    fetched = latent[cond_lists.reshape(-1)].reshape(LEAVES, 3, S, B)

    def one_block(items):
        own_rows, near_rows, weights, factor = items
        mean_part = jnp.einsum('gksb,gkba->gsa', near_rows.astype(jnp.float32), weights.astype(jnp.float32))
        residual_low = (own_rows.astype(jnp.float32) - mean_part).astype(jnp.bfloat16)
        innovation = jnp.einsum('gsb,gba->gsa', residual_low.astype(jnp.float32), factor.astype(jnp.float32)).astype(jnp.bfloat16)
        back_full = jnp.einsum('gsa,gba->gsb', innovation.astype(jnp.float32), factor.astype(jnp.float32))
        back_low = back_full.astype(jnp.bfloat16)
        term_all = jnp.einsum('gsa,gkba->gksb', back_low.astype(jnp.float32), weights.astype(jnp.float32))
        return back_full, term_all

    back_full, term_all = lax.map(one_block, (
        latent.reshape(block_count, LEAF_DEV, S, B),
        fetched.reshape(block_count, LEAF_DEV, 3, S, B),
        cond_weights.reshape(block_count, LEAF_DEV, 3, B, B),
        precision_factor.reshape(block_count, LEAF_DEV, B, B)))
    back_full = back_full.reshape(LEAVES, S, B)
    term_all = term_all.reshape(LEAVES * 3, S, B)
    gradient = (-back_full).at[cond_lists.reshape(-1).astype(jnp.int32)].add(term_all)
    return gradient
```

```python
import functools

import jax
import jax.numpy as jnp
from jax import lax
from jax.experimental import pallas as pl
from jax.experimental.pallas import tpu as pltpu
from jax.sharding import PartitionSpec as P

SLOTS = 32
CHUNK = 8
VMEM, SMEM, ANY = pltpu.VMEM, pltpu.SMEM, pl.ANY


def index_kernel(capacity, lists_ref, asked_ref, source_ref, target_ref):
    leaf_dev, fan = lists_ref.shape
    me = lax.axis_index("kx")
    behind = me * leaf_dev - lists_ref[...]
    kind = (
        (behind > 0).astype(jnp.int32)
        + (behind > leaf_dev).astype(jnp.int32)
        + (behind > 2 * leaf_dev).astype(jnp.int32)
        + (behind > 4 * leaf_dev).astype(jnp.int32)
    )
    reach = jnp.where(kind == 4, 8, jnp.where(kind == 3, 4, kind))
    row = reach * leaf_dev - behind
    eye = (
        lax.broadcasted_iota(jnp.int32, (leaf_dev, leaf_dev), 0)
        == lax.broadcasted_iota(jnp.int32, (leaf_dev, leaf_dev), 1)
    ).astype(jnp.bfloat16)
    before = (
        lax.broadcasted_iota(jnp.int32, (leaf_dev, leaf_dev), 0)
        < lax.broadcasted_iota(jnp.int32, (leaf_dev, leaf_dev), 1)
    ).astype(jnp.bfloat16)

    def turned(x):
        return lax.dot_general(
            x.astype(jnp.float32).astype(jnp.bfloat16), eye, (((0,), (0,)), ((), ())),
            preferred_element_type=jnp.float32,
        )

    kind_t = turned(kind)
    row_t = turned(row)
    source = row_t
    target = row_t
    slot = lax.broadcasted_iota(jnp.int32, (SLOTS, leaf_dev), 0).astype(jnp.float32)
    for o in range(1, 5):
        mask = kind_t == float(o)
        ones = mask.astype(jnp.float32)
        within = jnp.dot(ones.astype(jnp.bfloat16), before, preferred_element_type=jnp.float32)
        totals = jnp.sum(ones, axis=1, keepdims=True)
        base = jnp.zeros((1, 1), jnp.float32)
        asked = jnp.zeros((1, SLOTS), jnp.float32)
        for k in range(fan):
            rank = within[k : k + 1] + base
            base = base + totals[k : k + 1]
            hit = (jnp.where(mask[k : k + 1], rank, -1.0) == slot).astype(jnp.float32)
            asked = asked + lax.dot_general(
                row_t[k : k + 1].astype(jnp.bfloat16), hit.astype(jnp.bfloat16),
                (((1,), (1,)), ((), ())), preferred_element_type=jnp.float32,
            )
            place = leaf_dev + (o - 1) * capacity + rank
            near = row_t[k : k + 1] + leaf_dev if o == 3 else place + leaf_dev
            target_ref[k : k + 1] = jnp.where(
                mask[k : k + 1], place,
                target[k : k + 1] if o == 1 else target_ref[k : k + 1].astype(jnp.float32),
            ).astype(jnp.int32)
            source_ref[k : k + 1] = jnp.where(
                mask[k : k + 1], near,
                source[k : k + 1] if o == 1 else source_ref[k : k + 1].astype(jnp.float32),
            ).astype(jnp.int32)
        asked_ref[:, (o - 1) * SLOTS : o * SLOTS] = asked.astype(jnp.int32)


def serve_kernel(capacity, all_asked, latent, before, out8, out2, out1):
    me = lax.axis_index("kx")
    last = lax.axis_size("kx") - 1
    ahead = jnp.minimum(me + 4, last)
    across = lax.bitwise_xor(me, 2)
    low = lax.bitwise_and(me, 3)
    around = me - low + lax.bitwise_and(low + 1, 3)

    def pick(slots, rows, out, reader):
        def one(r, carry):
            out[r] = rows[all_asked[reader, slots * SLOTS + r]]
            return carry
        lax.fori_loop(0, capacity, one, 0, unroll=6)

    pick(3, before, out8, ahead)

    @pl.when(lax.bitwise_and(me, 2) == 0)
    def _():
        pick(1, latent, out2, across)

    @pl.when(lax.bitwise_and(me, 2) != 0)
    def _():
        pick(1, before, out2, across)

    @pl.when(low != 3)
    def _():
        pick(0, latent, out1, around)

    @pl.when(low == 3)
    def _():
        pick(0, before, out1, around)


def leaf_kernel(
    capacity, source, target, latent, from4, from8, from2, from1, weights, factor,
    grad, out1, out2, out4, out8, near, acc, w_v, f_v, row_sem, w_sem, f_sem,
):
    leaf_dev = latent.shape[0]
    fan, width = weights.shape[1], weights.shape[2]
    chunks = leaf_dev // CHUNK
    starts = (0, leaf_dev, 2 * leaf_dev, 2 * leaf_dev + capacity, 2 * leaf_dev + 3 * capacity)
    row_copies = [
        pltpu.make_async_copy(rows, near.at[pl.ds(at, rows.shape[0])], row_sem.at[n])
        for n, (rows, at) in enumerate(zip((latent, from4, from1, from2, from8), starts))
    ]

    def weight_copy(c):
        part = pl.ds(c * CHUNK, CHUNK)
        return pltpu.make_async_copy(weights.at[part], w_v.at[part], w_sem.at[c])

    def factor_copy(c):
        part = pl.ds(c * CHUNK, CHUNK)
        return pltpu.make_async_copy(factor.at[part], f_v.at[part], f_sem.at[c])

    for copy in row_copies:
        copy.start()
    for c in range(chunks):
        weight_copy(c).start()
        factor_copy(c).start()
    acc[...] = jnp.zeros_like(acc)
    for copy in row_copies:
        copy.wait()
    by_rows = (((1,), (1,)), ((), ()))

    def chunk(c, carry):
        weight_copy(c).wait()
        factor_copy(c).wait()
        leaves = [c * CHUNK + u for u in range(CHUNK)]
        resid, innov, back, term = [], [], [], []
        for i in leaves:
            rows = jnp.concatenate([near[source[k, i]] for k in range(fan)], axis=1)
            mean = jnp.dot(
                rows, w_v[i].reshape(fan * width, width), preferred_element_type=jnp.float32
            )
            resid.append((near[i].astype(jnp.float32) - mean).astype(jnp.bfloat16))
        for i, x in zip(leaves, resid):
            innov.append(
                jnp.dot(x, f_v[i], preferred_element_type=jnp.float32).astype(jnp.bfloat16)
            )
        for i, x in zip(leaves, innov):
            back.append(
                lax.dot_general(x, f_v[i], by_rows, preferred_element_type=jnp.float32)
            )
        for i, x in zip(leaves, back):
            term.append(lax.dot_general(
                x.astype(jnp.bfloat16), w_v[i].reshape(fan * width, width), by_rows,
                preferred_element_type=jnp.float32,
            ))
        for i, x in zip(leaves, back):
            acc[i] = acc[i] - x
        for i, x in zip(leaves, term):
            for k in range(fan):
                j = target[k, i]
                acc[j] = acc[j] + x[:, k * width : (k + 1) * width]
        return carry

    lax.fori_loop(0, chunks, chunk, 0)
    grad[...] = acc[pl.ds(0, leaf_dev)]
    for n, out in enumerate((out1, out2, out4, out8)):
        out[...] = acc[pl.ds(leaf_dev + n * capacity, capacity)].astype(out.dtype)


def add_kernel(capacity, all_asked, part, back1, back2, back4, back8, out):
    me = lax.axis_index("kx")
    last = lax.axis_size("kx") - 1
    out[...] = part[...]
    for n, (reach, rows) in enumerate(((1, back1), (2, back2), (4, back4), (8, back8))):
        asker = jnp.minimum(me + reach, last)

        def one(r, carry):
            j = all_asked[asker, n * SLOTS + r]
            out[j] = out[j] + rows[r].astype(jnp.float32)
            return carry

        lax.fori_loop(0, capacity, one, 0, unroll=6)


def per_device(latent, cond_lists, cond_weights, precision_factor):
    devices = lax.axis_size("kx")
    leaf_dev, samples, width = latent.shape
    fan = cond_lists.shape[1]
    capacity = fan * leaf_dev // 8
    spec = pl.BlockSpec
    some_rows = jax.ShapeDtypeStruct((capacity, samples, width), jnp.bfloat16)
    vmem, smem, anywhere = spec(memory_space=VMEM), spec(memory_space=SMEM), spec(memory_space=ANY)

    from4 = lax.ppermute(latent, "kx", [(i, i + 4) for i in range(devices - 4)])
    asked, source, target = pl.pallas_call(
        functools.partial(index_kernel, capacity),
        out_shape=(
            jax.ShapeDtypeStruct((1, 4 * SLOTS), jnp.int32),
            jax.ShapeDtypeStruct((fan, leaf_dev), jnp.int32),
            jax.ShapeDtypeStruct((fan, leaf_dev), jnp.int32),
        ),
        in_specs=[vmem],
        out_specs=(vmem, vmem, vmem),
        name="index",
    )(cond_lists)
    all_asked = lax.all_gather(asked, "kx", axis=0, tiled=True)
    serve8, serve2, serve1 = pl.pallas_call(
        functools.partial(serve_kernel, capacity),
        out_shape=(some_rows,) * 3,
        in_specs=[smem, vmem, vmem],
        out_specs=(vmem,) * 3,
        name="serve",
    )(all_asked, latent, from4)
    from8 = lax.ppermute(serve8, "kx", [(i, i + 4) for i in range(4, devices - 4)])
    from2 = lax.ppermute(serve2, "kx", [(i, i ^ 2) for i in range(devices)])
    from1 = lax.ppermute(serve1, "kx", [(i, i // 4 * 4 + (i + 1) % 4) for i in range(devices)])
    part, out1, out2, out4, out8 = pl.pallas_call(
        functools.partial(leaf_kernel, capacity),
        out_shape=(jax.ShapeDtypeStruct(latent.shape, jnp.float32),) + (some_rows,) * 4,
        in_specs=[smem, smem] + [anywhere] * 7,
        out_specs=(vmem,) * 5,
        scratch_shapes=[
            VMEM((2 * leaf_dev + 4 * capacity, samples, width), jnp.bfloat16),
            VMEM((leaf_dev + 4 * capacity, samples, width), jnp.float32),
            VMEM(cond_weights.shape, jnp.bfloat16),
            VMEM(precision_factor.shape, jnp.bfloat16),
            pltpu.SemaphoreType.DMA((5,)),
            pltpu.SemaphoreType.DMA((leaf_dev // CHUNK,)),
            pltpu.SemaphoreType.DMA((leaf_dev // CHUNK,)),
        ],
        compiler_params=pltpu.CompilerParams(vmem_limit_bytes=24 * 2**20),
        name="leaves",
    )(source, target, latent, from4, from8, from2, from1, cond_weights, precision_factor)
    returned = [
        lax.ppermute(x, "kx", [(i, i - reach) for i in range(reach, devices)])
        for reach, x in ((8, out8), (4, out4), (2, out2), (1, out1))
    ]
    return pl.pallas_call(
        functools.partial(add_kernel, capacity),
        out_shape=jax.ShapeDtypeStruct(latent.shape, jnp.float32),
        in_specs=[smem] + [vmem] * 5,
        out_specs=vmem,
        name="add",
    )(all_asked, part, *returned[::-1])


def solution(mesh):
    return jax.shard_map(
        per_device,
        mesh=mesh,
        in_specs=(
            P(("groups", "kx"), None, None),
            P(("groups", "kx"), None),
            P(("groups", "kx"), None, None, None),
            P(("groups", "kx"), None, None),
        ),
        out_specs=P(("groups", "kx"), None, None),
        check_vma=False,
    )
```

```python
import functools

import jax
import jax.numpy as jnp
from jax import lax
from jax.experimental import pallas as pl
from jax.experimental.pallas import tpu as pltpu
from jax.sharding import PartitionSpec as P

SLOTS = 32
LEAVES = 16
ROWS = 15
MIB = 2**20
BY_ROWS = (((1,), (1,)), ((), ()))
VMEM, SMEM, HBM = pltpu.VMEM, pltpu.SMEM, pltpu.HBM


def index_kernel(lists, latent, asked, slots, home, held, sem):
    fan, leaf_dev = lists.shape
    fetch = pltpu.make_async_copy(latent, held, sem)
    fetch.start()
    me = lax.axis_index("kx")
    behind = me * leaf_dev - lists[...]
    kind = (
        (behind > 0).astype(jnp.int32)
        + (behind > leaf_dev).astype(jnp.int32)
        + (behind > 2 * leaf_dev).astype(jnp.int32)
        + (behind > 4 * leaf_dev).astype(jnp.int32)
    )
    reach = jnp.where(kind == 4, 8, jnp.where(kind == 3, 4, kind))
    row = reach * leaf_dev - behind
    home[...] = jnp.where(kind == 0, row, leaf_dev)

    def grid(shape, dim):
        return lax.broadcasted_iota(jnp.int32, shape, dim)

    def low(x):
        return x.astype(jnp.float32).astype(jnp.bfloat16)

    every = 4 * fan
    mask = jnp.concatenate([(kind == o).astype(jnp.float32) for o in range(1, 5)], axis=0)
    earlier = low(grid((leaf_dev, leaf_dev), 0) < grid((leaf_dev, leaf_dev), 1))
    a, b = grid((every, every), 0), grid((every, every), 1)
    above = (b < a)
    for o in range(1, 4):
        above = above & ((a < o * fan) | (b >= o * fan))
    within = jnp.dot(low(mask), earlier, preferred_element_type=jnp.float32)
    base = jnp.sum(
        jnp.dot(low(above), low(mask), preferred_element_type=jnp.float32), axis=1, keepdims=True
    )
    place = jnp.where(mask > 0.0, within + base, -1.0)
    slot = grid((SLOTS, leaf_dev), 0).astype(jnp.float32)
    leaf = grid((1, leaf_dev), 1).astype(jnp.float32)
    ones = jnp.ones((1, leaf_dev), jnp.float32)
    total = jnp.zeros((8, 4 * SLOTS), jnp.float32)
    for k in range(fan):
        hit = jnp.concatenate(
            [(place[o * fan + k : o * fan + k + 1] == slot).astype(jnp.float32) for o in range(4)],
            axis=0,
        )
        facts = jnp.concatenate(
            [row[k : k + 1].astype(jnp.float32), leaf, k * ones, ones]
            + [jnp.zeros((4, leaf_dev), jnp.float32)], axis=0,
        )
        total = total + lax.dot_general(
            low(facts), low(hit), BY_ROWS, preferred_element_type=jnp.float32
        )
    asked[...] = total[0:1].astype(jnp.int32)
    slots[0:1] = jnp.where(total[3:4] > 0.0, total[1:2], float(leaf_dev)).astype(jnp.int32)
    slots[1:2] = total[2:3].astype(jnp.int32)
    fetch.wait()


def local_kernel(home, latent, weights, factor, left, held_w, held_f, near, w_sem, f_sem):
    leaf_dev = latent.shape[0]
    fan, width = weights.shape[1], weights.shape[2]

    def fetch(c):
        part = pl.ds(c * LEAVES, LEAVES)
        return pltpu.make_async_copy(weights.at[part], held_w.at[part], w_sem.at[c])

    fetch_factor = pltpu.make_async_copy(factor, held_f, f_sem)
    for c in range(leaf_dev // LEAVES):
        fetch(c).start()
    fetch_factor.start()
    near[pl.ds(0, leaf_dev)] = latent[...]
    near[leaf_dev] = jnp.zeros(latent.shape[1:], latent.dtype)

    def some(c, carry):
        fetch(c).wait()
        for u in range(LEAVES):
            i = c * LEAVES + u
            rows = jnp.concatenate([near[home[k, i]] for k in range(fan)], axis=1)
            mean = jnp.dot(
                rows, held_w[i].reshape(fan * width, width), preferred_element_type=jnp.float32
            )
            left[i] = latent[i].astype(jnp.float32) - mean
        return carry

    lax.fori_loop(0, leaf_dev // LEAVES, some, 0)
    fetch_factor.wait()


def serve_kernel(capacity, ask8, ask2, ask1, latent, before, out8, out2, out1, heard):
    me = lax.axis_index("kx")
    for n, ask in enumerate((ask8, ask2, ask1)):
        for lane in range(4 * SLOTS):
            heard[n, lane] = ask[0, lane]

    def pick(o, ask, rows, out):
        for r in range(capacity):
            out[r] = rows[ask[0, o * SLOTS + r]]

    pick(3, ask8, before, out8)
    for o, ask, out, bits in ((1, ask2, out2, 2), (0, ask1, out1, 3)):
        relays = lax.bitwise_and(me, bits) == bits

        @pl.when(relays)
        def _():
            pick(o, ask, before, out)

        @pl.when(jnp.logical_not(relays))
        def _():
            pick(o, ask, latent, out)


def remote_kernel(
    capacity, asked, slots, left, before, from8, from2, from1, weights, factor,
    back, out8, out4, out2, out1, resid, low,
):
    leaf_dev = left.shape[0]
    resid[pl.ds(0, leaf_dev)] = left[...]
    resid[leaf_dev] = jnp.zeros(left.shape[1:], left.dtype)
    low[leaf_dev] = jnp.zeros(left.shape[1:], low.dtype)

    def asker(o, r):
        i = slots[0, o * SLOTS + r]
        return i, jnp.minimum(i, leaf_dev - 1), slots[1, o * SLOTS + r]

    for o, rows in ((2, before), (3, from8), (1, from2), (0, from1)):
        def some(c, carry):
            means = []
            for u in range(ROWS):
                r = c * ROWS + u
                i, held, k = asker(o, r)
                x = rows[asked[0, o * SLOTS + r]] if o == 2 else rows[r]
                means.append((i, jnp.dot(
                    x, weights[held, k], preferred_element_type=jnp.float32
                )))
            for i, mean in means:
                resid[i] = resid[i] - mean
            return carry

        lax.fori_loop(0, capacity // ROWS, some, 0)

    def leaves(c, carry):
        every = [c * LEAVES + u for u in range(LEAVES)]
        innov = [
            jnp.dot(
                resid[i].astype(jnp.bfloat16), factor[i], preferred_element_type=jnp.float32
            ).astype(jnp.bfloat16)
            for i in every
        ]
        for i, x in zip(every, innov):
            y = lax.dot_general(x, factor[i], BY_ROWS, preferred_element_type=jnp.float32)
            back[i] = y
            low[i] = y.astype(jnp.bfloat16)
        return carry

    lax.fori_loop(0, leaf_dev // LEAVES, leaves, 0)
    for o, out in ((3, out8), (2, out4), (1, out2), (0, out1)):
        def terms(c, carry):
            for u in range(ROWS):
                r = c * ROWS + u
                i, held, k = asker(o, r)
                out[r] = lax.dot_general(
                    low[i], weights[held, k], BY_ROWS, preferred_element_type=jnp.float32
                ).astype(out.dtype)
            return carry

        lax.fori_loop(0, capacity // ROWS, terms, 0)


def home_kernel(home, back, weights, part, acc):
    leaf_dev = back.shape[0]
    fan, width = weights.shape[1], weights.shape[2]
    acc[pl.ds(0, leaf_dev)] = -back[...]
    acc[leaf_dev] = jnp.zeros(back.shape[1:], back.dtype)

    def some(c, carry):
        every = [c * LEAVES + u for u in range(LEAVES)]
        terms = [
            lax.dot_general(
                back[i].astype(jnp.bfloat16), weights[i].reshape(fan * width, width), BY_ROWS,
                preferred_element_type=jnp.float32,
            )
            for i in every
        ]
        for i, x in zip(every, terms):
            for k in range(fan):
                j = home[k, i]
                acc[j] = acc[j] + x[:, k * width : (k + 1) * width]
        return carry

    lax.fori_loop(0, leaf_dev // LEAVES, some, 0)
    part[...] = acc[pl.ds(0, leaf_dev)]


def add_kernel(capacity, ask8, ask2, ask1, far, part, back8, back4, back2, back1, out):
    me = lax.axis_index("kx")
    out[...] = part[...]

    def add(o, lane, rows):
        for r in range(capacity):
            j = lane(o * SLOTS + r)
            out[j] = out[j] + rows[r].astype(jnp.float32)

    beyond2 = lax.bitwise_and(me, 2) == 2
    beyond1 = lax.bitwise_and(me, 3) == 3
    add(3, lambda at: far[0, at], back8)
    add(2, lambda at: ask8[0, at], back4)
    add(1, lambda at: jnp.where(beyond2, far[1, at], ask2[0, at]), back2)
    add(0, lambda at: jnp.where(beyond1, far[2, at], ask1[0, at]), back1)


def call(body, name, out_shape, ins, outs, limit, flops=0, moved=0, scratch=()):
    spec = lambda space: pl.BlockSpec(memory_space=space)
    return pl.pallas_call(
        body,
        out_shape=out_shape,
        in_specs=[spec(space) for space in ins],
        out_specs=tuple(spec(space) for space in outs),
        scratch_shapes=scratch,
        compiler_params=pltpu.CompilerParams(vmem_limit_bytes=limit * MIB),
        cost_estimate=pl.CostEstimate(flops=flops, bytes_accessed=moved, transcendentals=0),
        name=name,
    )


def in_hbm(x):
    return pltpu.with_memory_space_constraint(x, HBM)


def per_device(latent, cond_lists, cond_weights, precision_factor):
    devices = lax.axis_size("kx")
    leaf_dev, samples, width = latent.shape
    fan = cond_lists.shape[1]
    capacity = fan * leaf_dev // 8
    everyone = range(devices)
    shape = jax.ShapeDtypeStruct
    some_rows = shape((capacity, samples, width), jnp.bfloat16)
    all_rows = shape(latent.shape, jnp.float32)
    one_list = shape((1, 4 * SLOTS), jnp.int32)
    heavy = cond_weights.size * 2

    def passed(x, route):
        return lax.ppermute(x, "kx", route)

    before = passed(latent, [(i, i + 4) for i in everyone if i + 4 < devices])
    asked, slots, home, held_l = call(
        index_kernel, "index",
        (
            one_list, shape((2, 4 * SLOTS), jnp.int32), shape((fan, leaf_dev), jnp.int32),
            shape(latent.shape, latent.dtype),
        ),
        [VMEM, HBM], [VMEM] * 4, 4, moved=2 * MIB, scratch=[pltpu.SemaphoreType.DMA],
    )(in_hbm(cond_lists.T), in_hbm(latent))
    ask8 = passed(asked, [(i, i - 4) for i in everyone if i >= 4])
    ask2 = passed(asked, [(i, i ^ 2) for i in everyone])
    ask1 = passed(asked, [(i, i // 4 * 4 + (i + 3) % 4) for i in everyone])
    left, held_w, held_f = call(
        local_kernel, "local",
        (
            all_rows, shape(cond_weights.shape, jnp.bfloat16),
            shape(precision_factor.shape, jnp.bfloat16),
        ),
        [SMEM, VMEM, HBM, HBM], [VMEM] * 3, 16, moved=heavy,
        scratch=[
            VMEM((leaf_dev + 8, samples, width), jnp.bfloat16),
            pltpu.SemaphoreType.DMA((leaf_dev // LEAVES,)),
            pltpu.SemaphoreType.DMA,
        ],
    )(home, held_l, in_hbm(cond_weights), in_hbm(precision_factor))
    serve8, serve2, serve1, heard = call(
        functools.partial(serve_kernel, capacity), "serve",
        (some_rows,) * 3 + (shape((3, 4 * SLOTS), jnp.int32),),
        [SMEM] * 3 + [VMEM] * 2, [VMEM] * 3 + [SMEM], 4, moved=4 * MIB,
    )(ask8, ask2, ask1, held_l, before)
    from8 = passed(serve8, [(i, i + 4) for i in everyone if i >= 4 and i + 4 < devices])
    from2 = passed(serve2, [(i, i ^ 2) for i in everyone])
    from1 = passed(serve1, [(i, i // 4 * 4 + (i + 1) % 4) for i in everyone])
    far = passed(heard, [(i, i - 4) for i in everyone if i >= 4])
    back, out8, out4, out2, out1 = call(
        functools.partial(remote_kernel, capacity), "remote",
        (all_rows,) + (some_rows,) * 4, [SMEM] * 2 + [VMEM] * 7, [VMEM] * 5, 18,
        moved=2 * heavy,
        scratch=[
            VMEM((leaf_dev + 8, samples, width), jnp.float32),
            VMEM((leaf_dev + 8, samples, width), jnp.bfloat16),
        ],
    )(asked, slots, left, before, from8, from2, from1, held_w, held_f)
    returned = [
        passed(x, [(i, i - reach) for i in everyone if i >= reach])
        for reach, x in ((8, out8), (4, out4), (2, out2), (1, out1))
    ]
    (part,) = call(
        home_kernel, "home", (all_rows,), [SMEM, VMEM, VMEM], [VMEM], 16,
        moved=heavy, scratch=[VMEM((leaf_dev + 8, samples, width), jnp.float32)],
    )(home, back, held_w)
    (gradient,) = call(
        functools.partial(add_kernel, capacity), "add", (all_rows,),
        [SMEM] * 4 + [VMEM] * 5, [VMEM], 6, moved=4 * MIB,
    )(ask8, ask2, ask1, far, part, *returned)
    return gradient


def solution(mesh):
    return jax.shard_map(
        per_device,
        mesh=mesh,
        in_specs=(
            P(("groups", "kx"), None, None),
            P(("groups", "kx"), None),
            P(("groups", "kx"), None, None, None),
            P(("groups", "kx"), None, None),
        ),
        out_specs=P(("groups", "kx"), None, None),
        check_vma=False,
    )
```

```python
import functools

import jax
import jax.numpy as jnp
from jax import lax
from jax.experimental import pallas as pl
from jax.experimental.pallas import tpu as pltpu
from jax.sharding import PartitionSpec as P

SLOTS = 32
LEAVES = 16
MIB = 2**20
BY_ROWS = (((1,), (1,)), ((), ()))
VMEM, SMEM, HBM = pltpu.VMEM, pltpu.SMEM, pltpu.HBM


def index_kernel(lists, asked, slots, close, home):
    fan, leaf_dev = lists.shape
    me = lax.axis_index("kx")
    behind = me * leaf_dev - lists[...]
    kind = (
        (behind > 0).astype(jnp.int32)
        + (behind > leaf_dev).astype(jnp.int32)
        + (behind > 2 * leaf_dev).astype(jnp.int32)
        + (behind > 4 * leaf_dev).astype(jnp.int32)
    )
    reach = jnp.where(kind == 4, 8, jnp.where(kind == 3, 4, kind))
    row = reach * leaf_dev - behind
    home[...] = jnp.where(kind == 0, row, leaf_dev)
    close[...] = jnp.where(kind == 0, row, jnp.where(kind == 3, row + leaf_dev, 2 * leaf_dev))

    def grid(shape, dim):
        return lax.broadcasted_iota(jnp.int32, shape, dim)

    def low(x):
        return x.astype(jnp.float32).astype(jnp.bfloat16)

    every = 4 * fan
    mask = jnp.concatenate([(kind == o).astype(jnp.float32) for o in range(1, 5)], axis=0)
    earlier = low(grid((leaf_dev, leaf_dev), 0) < grid((leaf_dev, leaf_dev), 1))
    a, b = grid((every, every), 0), grid((every, every), 1)
    above = (b < a)
    for o in range(1, 4):
        above = above & ((a < o * fan) | (b >= o * fan))
    within = jnp.dot(low(mask), earlier, preferred_element_type=jnp.float32)
    base = jnp.sum(
        jnp.dot(low(above), low(mask), preferred_element_type=jnp.float32), axis=1, keepdims=True
    )
    place = jnp.where(mask > 0.0, within + base, -1.0)
    slot = grid((SLOTS, leaf_dev), 0).astype(jnp.float32)
    leaf = grid((1, leaf_dev), 1).astype(jnp.float32)
    ones = jnp.ones((1, leaf_dev), jnp.float32)
    total = jnp.zeros((8, 4 * SLOTS), jnp.float32)
    for k in range(fan):
        hit = jnp.concatenate(
            [(place[o * fan + k : o * fan + k + 1] == slot).astype(jnp.float32) for o in range(4)],
            axis=0,
        )
        facts = jnp.concatenate(
            [row[k : k + 1].astype(jnp.float32), leaf, k * ones, ones]
            + [jnp.zeros((4, leaf_dev), jnp.float32)], axis=0,
        )
        total = total + lax.dot_general(
            low(facts), low(hit), BY_ROWS, preferred_element_type=jnp.float32
        )
    asked[...] = total[0:1].astype(jnp.int32)
    slots[0:1] = jnp.where(total[3:4] > 0.0, total[1:2], float(leaf_dev)).astype(jnp.int32)
    slots[1:2] = total[2:3].astype(jnp.int32)


def beside(xs):
    return jnp.concatenate(xs, axis=1)


def below(xs):
    return jnp.concatenate(xs, axis=0)


def paired(x, y, left, right, by_rows=False):
    samples = x.shape[0]
    if by_rows:
        wide = left.shape[0]
        both = lax.dot_general(
            below([x, y]), below([left, right]), BY_ROWS, preferred_element_type=jnp.float32
        )
    else:
        wide = left.shape[1]
        both = jnp.dot(below([x, y]), beside([left, right]), preferred_element_type=jnp.float32)
    return both[:samples, :wide], both[samples:, wide:]


def near_kernel(
    close, latent, before, weights, factor, left, held_w, held_f, rows, row_sem, w_sem, f_sem
):
    leaf_dev = latent.shape[0]
    fan, width = weights.shape[1], weights.shape[2]

    def fetch(c):
        part = pl.ds(c * LEAVES, LEAVES)
        return pltpu.make_async_copy(weights.at[part], held_w.at[part], w_sem.at[c])

    fetch_rows = pltpu.make_async_copy(latent, rows.at[pl.ds(0, leaf_dev)], row_sem)
    fetch_factor = pltpu.make_async_copy(factor, held_f, f_sem)
    fetch_rows.start()
    for c in range(leaf_dev // LEAVES):
        fetch(c).start()
    fetch_factor.start()
    rows[pl.ds(leaf_dev, leaf_dev)] = before[...]
    rows[2 * leaf_dev] = jnp.zeros(latent.shape[1:], latent.dtype)
    fetch_rows.wait()

    def some(c, carry):
        fetch(c).wait()
        for u in range(0, LEAVES, 2):
            i = c * LEAVES + u
            means = paired(
                beside([rows[close[k, i]] for k in range(fan)]),
                beside([rows[close[k, i + 1]] for k in range(fan)]),
                held_w[i].reshape(fan * width, width),
                held_w[i + 1].reshape(fan * width, width),
            )
            for j, mean in zip((i, i + 1), means):
                left[j] = rows[j].astype(jnp.float32) - mean
        return carry

    lax.fori_loop(0, leaf_dev // LEAVES, some, 0)
    fetch_factor.wait()


def remote_kernel(
    capacity, asked, slots, asked_row, left, from8, low2, high2, odd1, high1, low1,
    weights, factor, back, out8, out4, out2, out1, resid, low,
):
    leaf_dev = left.shape[0]
    resid[pl.ds(0, leaf_dev)] = left[...]
    resid[leaf_dev] = jnp.zeros(left.shape[1:], left.dtype)
    low[leaf_dev] = jnp.zeros(left.shape[1:], low.dtype)

    def asker(o, r):
        i = slots[0, o * SLOTS + r]
        return i, weights[jnp.minimum(i, leaf_dev - 1), slots[1, o * SLOTS + r]]

    for o, sources in ((3, (from8,)), (1, (low2, high2)), (0, (odd1, high1, low1))):
        def row(r):
            return functools.reduce(lax.add, [x[asked[0, o * SLOTS + r]] for x in sources])

        found = []
        for r in range(0, capacity, 2):
            (i, w), (j, v) = asker(o, r), asker(o, r + 1)
            found += zip((i, j), paired(row(r), row(r + 1), w, v))
        for i, mean in found:
            resid[i] = resid[i] - mean

    def leaves(c, carry):
        pairs = [c * LEAVES + u for u in range(0, LEAVES, 2)]
        innov = [
            paired(
                resid[i].astype(jnp.bfloat16), resid[i + 1].astype(jnp.bfloat16),
                factor[i], factor[i + 1],
            )
            for i in pairs
        ]
        for i, (x, y) in zip(pairs, innov):
            both = paired(
                x.astype(jnp.bfloat16), y.astype(jnp.bfloat16), factor[i], factor[i + 1], True
            )
            for j, z in zip((i, i + 1), both):
                back[j] = z
                low[j] = z.astype(jnp.bfloat16)
        return carry

    lax.fori_loop(0, leaf_dev // LEAVES, leaves, 0)
    listed = jnp.broadcast_to(asked_row[...].astype(jnp.float32), left.shape[1:])
    for o, out in ((3, out8), (2, out4), (1, out2), (0, out1)):
        for r in range(0, capacity, 2):
            (i, w), (j, v) = asker(o, r), asker(o, r + 1)
            for at, x in zip((r, r + 1), paired(low[i], low[j], w, v, True)):
                out[at] = x.astype(out.dtype)
        out[capacity] = listed.astype(out.dtype)


def home_kernel(home, back, weights, part, acc):
    leaf_dev = back.shape[0]
    fan, width = weights.shape[1], weights.shape[2]
    acc[pl.ds(0, leaf_dev)] = -back[...]
    acc[leaf_dev] = jnp.zeros(back.shape[1:], back.dtype)

    def some(c, carry):
        found = []
        for u in range(0, LEAVES, 2):
            i = c * LEAVES + u
            found += zip((i, i + 1), paired(
                back[i].astype(jnp.bfloat16), back[i + 1].astype(jnp.bfloat16),
                weights[i].reshape(fan * width, width),
                weights[i + 1].reshape(fan * width, width), True,
            ))
        for i, x in found:
            for k in range(fan):
                j = home[k, i]
                acc[j] = acc[j] + x[:, k * width : (k + 1) * width]
        return carry

    lax.fori_loop(0, leaf_dev // LEAVES, some, 0)
    part[...] = acc[pl.ds(0, leaf_dev)]


def add_kernel(capacity, part, back8, back4, back2, back1, out, listed, wanted, sem):
    returned = ((3, back8), (2, back4), (1, back2), (0, back1))
    for o, rows in returned:
        listed[o : o + 1] = rows[capacity].astype(jnp.float32)[0:1].astype(jnp.int32)
    fetch = pltpu.make_async_copy(listed, wanted, sem)
    fetch.start()
    out[...] = part[...]
    fetch.wait()
    for o, rows in returned:
        for r in range(capacity):
            j = wanted[o, o * SLOTS + r]
            out[j] = out[j] + rows[r].astype(jnp.float32)


def call(body, name, out_shape, ins, outs, limit, flops=0, moved=0, scratch=()):
    spec = lambda space: pl.BlockSpec(memory_space=space)
    return pl.pallas_call(
        body,
        out_shape=out_shape,
        in_specs=[spec(space) for space in ins],
        out_specs=tuple(spec(space) for space in outs),
        scratch_shapes=scratch,
        compiler_params=pltpu.CompilerParams(vmem_limit_bytes=limit * MIB),
        cost_estimate=pl.CostEstimate(flops=flops, bytes_accessed=moved, transcendentals=0),
        name=name,
    )


def in_hbm(x):
    return pltpu.with_memory_space_constraint(x, HBM)


def per_device(latent, cond_lists, cond_weights, precision_factor):
    devices = lax.axis_size("kx")
    leaf_dev, samples, width = latent.shape
    fan = cond_lists.shape[1]
    capacity = fan * leaf_dev // 8
    everyone = range(devices)
    shape = jax.ShapeDtypeStruct
    sent = shape((capacity + 1, samples, width), jnp.bfloat16)
    all_rows = shape(latent.shape, jnp.float32)
    one_list = shape((1, 4 * SLOTS), jnp.int32)
    indices = shape((fan, leaf_dev), jnp.int32)
    heavy = cond_weights.size * 2

    def passed(x, step, chosen=lambda i: True):
        return lax.ppermute(
            x, "kx", [(i, i + step) for i in everyone if 0 <= i + step < devices and chosen(i)]
        )

    before = passed(latent, 4)
    low2 = passed(latent, 2, lambda i: i % 4 < 2)
    odd1 = passed(latent, 1, lambda i: i % 2 == 0)
    high1 = passed(low2, -1, lambda i: i % 4 == 3)
    asked, slots, close, home = call(
        index_kernel, "index", (one_list, shape((2, 4 * SLOTS), jnp.int32), indices, indices),
        [VMEM], [VMEM] * 4, 4, moved=2 * MIB,
    )(in_hbm(cond_lists.T))
    high2 = passed(before, -2, lambda i: i % 4 >= 2)
    from8 = passed(before, 4, lambda i: i >= 4)
    low1 = passed(high2, -1, lambda i: i % 4 == 1)
    left, held_w, held_f = call(
        near_kernel, "near",
        (
            all_rows, shape(cond_weights.shape, jnp.bfloat16),
            shape(precision_factor.shape, jnp.bfloat16),
        ),
        [SMEM, HBM, VMEM, HBM, HBM], [VMEM] * 3, 16, moved=heavy,
        scratch=[
            VMEM((2 * leaf_dev + 8, samples, width), jnp.bfloat16),
            pltpu.SemaphoreType.DMA,
            pltpu.SemaphoreType.DMA((leaf_dev // LEAVES,)),
            pltpu.SemaphoreType.DMA,
        ],
    )(close, in_hbm(latent), before, in_hbm(cond_weights), in_hbm(precision_factor))
    back, out8, out4, out2, out1 = call(
        functools.partial(remote_kernel, capacity), "remote",
        (all_rows,) + (sent,) * 4, [SMEM] * 2 + [VMEM] * 10, [VMEM] * 5, 18,
        moved=heavy,
        scratch=[
            VMEM((leaf_dev + 8, samples, width), jnp.float32),
            VMEM((leaf_dev + 8, samples, width), jnp.bfloat16),
        ],
    )(asked, slots, asked, left, from8, low2, high2, odd1, high1, low1, held_w, held_f)
    returned = [passed(x, -reach) for reach, x in ((8, out8), (4, out4), (2, out2), (1, out1))]
    (part,) = call(
        home_kernel, "home", (all_rows,), [SMEM, VMEM, VMEM], [VMEM], 16,
        moved=heavy, scratch=[VMEM((leaf_dev + 8, samples, width), jnp.float32)],
    )(home, back, held_w)
    (gradient,) = call(
        functools.partial(add_kernel, capacity), "add", (all_rows,), [VMEM] * 5, [VMEM], 6,
        moved=4 * MIB,
        scratch=[
            VMEM((4, 4 * SLOTS), jnp.int32), SMEM((4, 4 * SLOTS), jnp.int32),
            pltpu.SemaphoreType.DMA,
        ],
    )(part, *returned)
    return gradient


def solution(mesh):
    return jax.shard_map(
        per_device,
        mesh=mesh,
        in_specs=(
            P(("groups", "kx"), None, None),
            P(("groups", "kx"), None),
            P(("groups", "kx"), None, None, None),
            P(("groups", "kx"), None, None),
        ),
        out_specs=P(("groups", "kx"), None, None),
        check_vma=False,
    )
```

```python
import functools

import jax
import jax.numpy as jnp
from jax import lax
from jax.experimental import pallas as pl
from jax.experimental.pallas import tpu as pltpu
from jax.sharding import PartitionSpec as P

SLOTS = 32
LEAVES = 16
MIB = 2**20
BY_ROWS = (((1,), (1,)), ((), ()))
VMEM, SMEM, HBM, ANY = pltpu.VMEM, pltpu.SMEM, pltpu.HBM, pl.ANY


def index_kernel(lists, asked, slots, home):
    fan, leaf_dev = lists.shape
    me = lax.axis_index("kx")
    behind = me * leaf_dev - lists[...]
    kind = (
        (behind > 0).astype(jnp.int32)
        + (behind > leaf_dev).astype(jnp.int32)
        + (behind > 2 * leaf_dev).astype(jnp.int32)
        + (behind > 4 * leaf_dev).astype(jnp.int32)
    )
    reach = jnp.where(kind == 4, 8, jnp.where(kind == 3, 4, kind))
    row = reach * leaf_dev - behind
    home[...] = jnp.where(kind == 0, row, leaf_dev)

    def grid(shape, dim):
        return lax.broadcasted_iota(jnp.int32, shape, dim)

    def low(x):
        return x.astype(jnp.float32).astype(jnp.bfloat16)

    every = 4 * fan
    mask = jnp.concatenate([(kind == o).astype(jnp.float32) for o in range(1, 5)], axis=0)
    earlier = low(grid((leaf_dev, leaf_dev), 0) < grid((leaf_dev, leaf_dev), 1))
    a, b = grid((every, every), 0), grid((every, every), 1)
    above = (b < a)
    for o in range(1, 4):
        above = above & ((a < o * fan) | (b >= o * fan))
    within = jnp.dot(low(mask), earlier, preferred_element_type=jnp.float32)
    base = jnp.sum(
        jnp.dot(low(above), low(mask), preferred_element_type=jnp.float32), axis=1, keepdims=True
    )
    place = jnp.where(mask > 0.0, within + base, -1.0)
    slot = grid((SLOTS, leaf_dev), 0).astype(jnp.float32)
    leaf = grid((1, leaf_dev), 1).astype(jnp.float32)
    ones = jnp.ones((1, leaf_dev), jnp.float32)
    total = jnp.zeros((8, 4 * SLOTS), jnp.float32)
    for k in range(fan):
        hit = jnp.concatenate(
            [(place[o * fan + k : o * fan + k + 1] == slot).astype(jnp.float32) for o in range(4)],
            axis=0,
        )
        facts = jnp.concatenate(
            [row[k : k + 1].astype(jnp.float32), leaf, k * ones, ones]
            + [jnp.zeros((4, leaf_dev), jnp.float32)], axis=0,
        )
        total = total + lax.dot_general(
            low(facts), low(hit), BY_ROWS, preferred_element_type=jnp.float32
        )
    asked[...] = total[0:1].astype(jnp.int32)
    slots[0:1] = jnp.where(total[3:4] > 0.0, total[1:2], float(leaf_dev)).astype(jnp.int32)
    slots[1:2] = total[2:3].astype(jnp.int32)


def beside(xs):
    return jnp.concatenate(xs, axis=1)


def below(xs):
    return jnp.concatenate(xs, axis=0)


def paired(x, y, left, right, by_rows=False):
    samples = x.shape[0]
    if by_rows:
        wide = left.shape[0]
        both = lax.dot_general(
            below([x, y]), below([left, right]), BY_ROWS, preferred_element_type=jnp.float32
        )
    else:
        wide = left.shape[1]
        both = jnp.dot(below([x, y]), beside([left, right]), preferred_element_type=jnp.float32)
    return both[:samples, :wide], both[samples:, wide:]


def local_kernel(home, latent, weights, left, held_w, held_l, rows, row_sem, w_sem):
    leaf_dev = latent.shape[0]
    fan, width = weights.shape[1], weights.shape[2]

    def fetch(c):
        part = pl.ds(c * LEAVES, LEAVES)
        return pltpu.make_async_copy(weights.at[part], held_w.at[part], w_sem.at[c])

    fetch_rows = pltpu.make_async_copy(latent, held_l, row_sem)
    fetch_rows.start()
    for c in range(leaf_dev // LEAVES):
        fetch(c).start()
    fetch_rows.wait()
    rows[pl.ds(0, leaf_dev)] = held_l[...]
    rows[leaf_dev] = jnp.zeros(latent.shape[1:], latent.dtype)

    def some(c, carry):
        fetch(c).wait()
        for u in range(0, LEAVES, 2):
            i = c * LEAVES + u
            means = paired(
                beside([rows[home[k, i]] for k in range(fan)]),
                beside([rows[home[k, i + 1]] for k in range(fan)]),
                held_w[i].reshape(fan * width, width),
                held_w[i + 1].reshape(fan * width, width),
            )
            for j, mean in zip((i, i + 1), means):
                left[j] = rows[j].astype(jnp.float32) - mean
        return carry

    lax.fori_loop(0, leaf_dev // LEAVES, some, 0)


def serve_kernel(capacity, ask8, ask2, ask1, latent, before, left, out8, out2, out1):
    me = lax.axis_index("kx")
    def pick(o, ask, rows, out):
        for r in range(capacity):
            out[r] = rows[ask[0, o * SLOTS + r]]

    pick(3, ask8, before, out8)
    for o, ask, out, bits in ((1, ask2, out2, 2), (0, ask1, out1, 3)):
        relays = lax.bitwise_and(me, bits) == bits

        @pl.when(relays)
        def _():
            pick(o, ask, before, out)

        @pl.when(jnp.logical_not(relays))
        def _():
            pick(o, ask, latent, out)


def remote_kernel(
    capacity, asked, slots, asked_row, left, before, from8, from2, from1,
    weights, factor, back, out8, out4, out2, out1, resid, low, held_f, f_sem,
):
    leaf_dev = left.shape[0]
    fetch = pltpu.make_async_copy(factor, held_f, f_sem)
    fetch.start()
    resid[pl.ds(0, leaf_dev)] = left[...]
    resid[leaf_dev] = jnp.zeros(left.shape[1:], left.dtype)
    low[leaf_dev] = jnp.zeros(left.shape[1:], low.dtype)

    def asker(o, r):
        i = slots[0, o * SLOTS + r]
        return i, weights[jnp.minimum(i, leaf_dev - 1), slots[1, o * SLOTS + r]]

    for o, rows in ((2, before), (3, from8), (1, from2), (0, from1)):
        found = []
        for r in range(0, capacity, 2):
            (i, w), (j, v) = asker(o, r), asker(o, r + 1)
            at = (asked[0, o * SLOTS + r], asked[0, o * SLOTS + r + 1]) if o == 2 else (r, r + 1)
            found += zip((i, j), paired(rows[at[0]], rows[at[1]], w, v))
        for i, mean in found:
            resid[i] = resid[i] - mean

    fetch.wait()

    def leaves(c, carry):
        pairs = [c * LEAVES + u for u in range(0, LEAVES, 2)]
        innov = [
            paired(
                resid[i].astype(jnp.bfloat16), resid[i + 1].astype(jnp.bfloat16),
                held_f[i], held_f[i + 1],
            )
            for i in pairs
        ]
        for i, (x, y) in zip(pairs, innov):
            both = paired(
                x.astype(jnp.bfloat16), y.astype(jnp.bfloat16), held_f[i], held_f[i + 1], True
            )
            for j, z in zip((i, i + 1), both):
                back[j] = z
                low[j] = z.astype(jnp.bfloat16)
        return carry

    lax.fori_loop(0, leaf_dev // LEAVES, leaves, 0)
    listed = jnp.broadcast_to(asked_row[...].astype(jnp.float32), left.shape[1:])
    for o, out in ((3, out8), (2, out4), (1, out2), (0, out1)):
        for r in range(0, capacity, 2):
            (i, w), (j, v) = asker(o, r), asker(o, r + 1)
            for at, x in zip((r, r + 1), paired(low[i], low[j], w, v, True)):
                out[at] = x.astype(out.dtype)
        out[capacity] = listed.astype(out.dtype)


def home_kernel(home, back, weights, part, acc):
    leaf_dev = back.shape[0]
    fan, width = weights.shape[1], weights.shape[2]
    acc[pl.ds(0, leaf_dev)] = -back[...]
    acc[leaf_dev] = jnp.zeros(back.shape[1:], back.dtype)

    def some(c, carry):
        found = []
        for u in range(0, LEAVES, 2):
            i = c * LEAVES + u
            found += zip((i, i + 1), paired(
                back[i].astype(jnp.bfloat16), back[i + 1].astype(jnp.bfloat16),
                weights[i].reshape(fan * width, width),
                weights[i + 1].reshape(fan * width, width), True,
            ))
        for i, x in found:
            for k in range(fan):
                j = home[k, i]
                acc[j] = acc[j] + x[:, k * width : (k + 1) * width]
        return carry

    lax.fori_loop(0, leaf_dev // LEAVES, some, 0)
    part[...] = acc[pl.ds(0, leaf_dev)]


def add_kernel(capacity, part, back8, back4, back2, back1, out, listed, wanted, sem):
    returned = ((3, back8), (2, back4), (1, back2), (0, back1))
    for o, rows in returned:
        listed[o : o + 1] = rows[capacity].astype(jnp.float32)[0:1].astype(jnp.int32)
    fetch = pltpu.make_async_copy(listed, wanted, sem)
    fetch.start()
    out[...] = part[...]
    fetch.wait()
    for o, rows in returned:
        for r in range(capacity):
            j = wanted[o, o * SLOTS + r]
            out[j] = out[j] + rows[r].astype(jnp.float32)


def call(body, name, out_shape, ins, outs, limit, flops=0, moved=0, scratch=()):
    spec = lambda space: pl.BlockSpec(memory_space=space)
    return pl.pallas_call(
        body,
        out_shape=out_shape,
        in_specs=[spec(space) for space in ins],
        out_specs=tuple(spec(space) for space in outs),
        scratch_shapes=scratch,
        compiler_params=pltpu.CompilerParams(vmem_limit_bytes=limit * MIB),
        cost_estimate=pl.CostEstimate(flops=flops, bytes_accessed=moved, transcendentals=0),
        name=name,
    )


def placed(x, space):
    return pltpu.with_memory_space_constraint(x, space)


def per_device(latent, cond_lists, cond_weights, precision_factor):
    devices = lax.axis_size("kx")
    leaf_dev, samples, width = latent.shape
    fan = cond_lists.shape[1]
    capacity = fan * leaf_dev // 8
    everyone = range(devices)
    shape = jax.ShapeDtypeStruct
    some_rows = shape((capacity, samples, width), jnp.bfloat16)
    sent = shape((capacity + 1, samples, width), jnp.bfloat16)
    all_rows = shape(latent.shape, jnp.float32)
    one_list = shape((1, 4 * SLOTS), jnp.int32)
    heavy = cond_weights.size * 2

    def passed(x, route):
        return lax.ppermute(x, "kx", route)

    before = passed(latent, [(i, i + 4) for i in everyone if i + 4 < devices])
    asked, slots, home = call(
        index_kernel, "index",
        (one_list, shape((2, 4 * SLOTS), jnp.int32), shape((fan, leaf_dev), jnp.int32)),
        [VMEM], [VMEM] * 3, 4, moved=2 * MIB,
    )(placed(cond_lists.T, HBM))
    ask8 = passed(asked, [(i, i - 4) for i in everyone if i >= 4])
    ask2 = passed(asked, [(i, i ^ 2) for i in everyone])
    ask1 = passed(asked, [(i, i // 4 * 4 + (i + 3) % 4) for i in everyone])
    left, held_w, held_l = call(
        local_kernel, "local",
        (all_rows, shape(cond_weights.shape, jnp.bfloat16), shape(latent.shape, jnp.bfloat16)),
        [SMEM, HBM, HBM], [VMEM] * 3, 14, moved=heavy,
        scratch=[
            VMEM((leaf_dev + 8, samples, width), jnp.bfloat16),
            pltpu.SemaphoreType.DMA, pltpu.SemaphoreType.DMA((leaf_dev // LEAVES,)),
        ],
    )(home, placed(latent, HBM), placed(cond_weights, HBM))
    serve8, serve2, serve1 = call(
        functools.partial(serve_kernel, capacity), "serve", (some_rows,) * 3,
        [SMEM] * 3 + [VMEM] * 2 + [ANY], [VMEM] * 3, 4, moved=4 * MIB,
    )(ask8, ask2, ask1, held_l, before, left)
    from8 = passed(serve8, [(i, i + 4) for i in everyone if i >= 4 and i + 4 < devices])
    from2 = passed(serve2, [(i, i ^ 2) for i in everyone])
    from1 = passed(serve1, [(i, i // 4 * 4 + (i + 1) % 4) for i in everyone])
    back, out8, out4, out2, out1 = call(
        functools.partial(remote_kernel, capacity), "remote",
        (all_rows,) + (sent,) * 4, [SMEM] * 2 + [VMEM] * 7 + [HBM], [VMEM] * 5, 12, moved=heavy,
        scratch=[
            VMEM((leaf_dev + 8, samples, width), jnp.float32),
            VMEM((leaf_dev + 8, samples, width), jnp.bfloat16),
            VMEM(precision_factor.shape, jnp.bfloat16),
            pltpu.SemaphoreType.DMA,
        ],
    )(asked, slots, asked, left, before, from8, from2, from1, held_w, placed(precision_factor, HBM))
    returned = [
        passed(x, [(i, i - reach) for i in everyone if i >= reach])
        for reach, x in ((8, out8), (4, out4), (2, out2), (1, out1))
    ]
    (part,) = call(
        home_kernel, "home", (all_rows,), [SMEM, VMEM, VMEM], [VMEM], 6, moved=heavy,
        scratch=[VMEM((leaf_dev + 8, samples, width), jnp.float32)],
    )(home, back, held_w)
    (gradient,) = call(
        functools.partial(add_kernel, capacity), "add", (all_rows,), [VMEM] * 5, [VMEM], 6,
        moved=4 * MIB,
        scratch=[
            VMEM((4, 4 * SLOTS), jnp.int32), SMEM((4, 4 * SLOTS), jnp.int32),
            pltpu.SemaphoreType.DMA,
        ],
    )(part, *returned)
    return gradient


def solution(mesh):
    return jax.shard_map(
        per_device,
        mesh=mesh,
        in_specs=(
            P(("groups", "kx"), None, None),
            P(("groups", "kx"), None),
            P(("groups", "kx"), None, None, None),
            P(("groups", "kx"), None, None),
        ),
        out_specs=P(("groups", "kx"), None, None),
        check_vma=False,
    )
```

```python
import functools

import jax
import jax.numpy as jnp
from jax import lax
from jax.experimental import pallas as pl
from jax.experimental.pallas import tpu as pltpu
from jax.sharding import PartitionSpec as P

SLOTS = 32
CHUNK = 8
LEAVES = 16
MIB = 2**20
BY_ROWS = (((1,), (1,)), ((), ()))
VMEM, SMEM, HBM, ANY = pltpu.VMEM, pltpu.SMEM, pltpu.HBM, pl.ANY


def index_kernel(lists, asked, slots, home):
    fan, leaf_dev = lists.shape
    me = lax.axis_index("kx")
    behind = me * leaf_dev - lists[...]
    kind = (
        (behind > 0).astype(jnp.int32)
        + (behind > leaf_dev).astype(jnp.int32)
        + (behind > 2 * leaf_dev).astype(jnp.int32)
        + (behind > 4 * leaf_dev).astype(jnp.int32)
    )
    reach = jnp.where(kind == 4, 8, jnp.where(kind == 3, 4, kind))
    row = reach * leaf_dev - behind
    home[...] = jnp.where(kind == 0, row, leaf_dev)

    def grid(shape, dim):
        return lax.broadcasted_iota(jnp.int32, shape, dim)

    def low(x):
        return x.astype(jnp.float32).astype(jnp.bfloat16)

    every = 4 * fan
    mask = jnp.concatenate([(kind == o).astype(jnp.float32) for o in range(1, 5)], axis=0)
    earlier = low(grid((leaf_dev, leaf_dev), 0) < grid((leaf_dev, leaf_dev), 1))
    a, b = grid((every, every), 0), grid((every, every), 1)
    above = (b < a)
    for o in range(1, 4):
        above = above & ((a < o * fan) | (b >= o * fan))
    within = jnp.dot(low(mask), earlier, preferred_element_type=jnp.float32)
    base = jnp.sum(
        jnp.dot(low(above), low(mask), preferred_element_type=jnp.float32), axis=1, keepdims=True
    )
    place = jnp.where(mask > 0.0, within + base, -1.0)
    slot = grid((SLOTS, leaf_dev), 0).astype(jnp.float32)
    leaf = grid((1, leaf_dev), 1).astype(jnp.float32)
    ones = jnp.ones((1, leaf_dev), jnp.float32)
    total = jnp.zeros((8, 4 * SLOTS), jnp.float32)
    for k in range(fan):
        hit = jnp.concatenate(
            [(place[o * fan + k : o * fan + k + 1] == slot).astype(jnp.float32) for o in range(4)],
            axis=0,
        )
        facts = jnp.concatenate(
            [row[k : k + 1].astype(jnp.float32), leaf, k * ones, ones]
            + [jnp.zeros((4, leaf_dev), jnp.float32)], axis=0,
        )
        total = total + lax.dot_general(
            low(facts), low(hit), BY_ROWS, preferred_element_type=jnp.float32
        )
    asked[...] = total[0:1].astype(jnp.int32)
    slots[0:1] = jnp.where(total[3:4] > 0.0, total[1:2], float(leaf_dev)).astype(jnp.int32)
    slots[1:2] = total[2:3].astype(jnp.int32)


def beside(xs):
    return jnp.concatenate(xs, axis=1)


def below(xs):
    return jnp.concatenate(xs, axis=0)


def paired(x, y, left, right, by_rows=False):
    samples = x.shape[0]
    if by_rows:
        wide = left.shape[0]
        both = lax.dot_general(
            below([x, y]), below([left, right]), BY_ROWS, preferred_element_type=jnp.float32
        )
    else:
        wide = left.shape[1]
        both = jnp.dot(below([x, y]), beside([left, right]), preferred_element_type=jnp.float32)
    return both[:samples, :wide], both[samples:, wide:]


def local_means(leaves, home, rows, weights, left, first):
    fan, width = weights.shape[1], weights.shape[2]
    for i in leaves:
        means = paired(
            beside([rows[home[k, i]] for k in range(fan)]),
            beside([rows[home[k, i + 1]] for k in range(fan)]),
            weights[i].reshape(fan * width, width),
            weights[i + 1].reshape(fan * width, width),
        )
        for j, mean in zip((i, i + 1), means):
            left[j - first] = rows[j].astype(jnp.float32) - mean


def early_kernel(home, latent, weights, left, held_w, rows, row_sem, w_sem):
    leaf_dev = latent.shape[0]
    chunks, ahead = leaf_dev // CHUNK, 3

    def fetch(c):
        part = pl.ds(c * CHUNK, CHUNK)
        return pltpu.make_async_copy(weights.at[part], held_w.at[part], w_sem.at[c])

    fetch_rows = pltpu.make_async_copy(latent, rows.at[pl.ds(0, leaf_dev)], row_sem)
    fetch_rows.start()
    for c in range(ahead):
        fetch(c).start()
    rows[leaf_dev] = jnp.zeros(latent.shape[1:], latent.dtype)
    fetch_rows.wait()
    for c in range(chunks):
        fetch(c).wait()
        if c + ahead < chunks:
            fetch(c + ahead).start()
        if (c + 1) * CHUNK <= left.shape[0]:
            local_means(range(c * CHUNK, (c + 1) * CHUNK, 2), home, rows, held_w, left, 0)


def late_kernel(home, rows, before, weights, factor, left, held_f, f_sem):
    leaf_dev = weights.shape[0]
    fetch = pltpu.make_async_copy(factor, held_f, f_sem)
    fetch.start()
    first = leaf_dev - left.shape[0]
    local_means(range(first, leaf_dev, 2), home, rows, weights, left, first)
    fetch.wait()


def serve_kernel(capacity, ask8, ask2, ask1, latent, before, left, out8, out2, out1):
    me = lax.axis_index("kx")
    def pick(o, ask, rows, out):
        for r in range(capacity):
            out[r] = rows[ask[0, o * SLOTS + r]]

    pick(3, ask8, before, out8)
    for o, ask, out, bits in ((1, ask2, out2, 2), (0, ask1, out1, 3)):
        relays = lax.bitwise_and(me, bits) == bits

        @pl.when(relays)
        def _():
            pick(o, ask, before, out)

        @pl.when(jnp.logical_not(relays))
        def _():
            pick(o, ask, latent, out)


def asker(slots, weights, o, r):
    i = slots[0, o * SLOTS + r]
    return i, weights[jnp.minimum(i, weights.shape[0] - 1), slots[1, o * SLOTS + r]]


def remote_terms(capacity, slots, asked_row, low, weights, outs):
    listed = jnp.broadcast_to(asked_row[...].astype(jnp.float32), low.shape[1:])
    for o, out in outs:
        for r in range(0, capacity, 2):
            (i, w), (j, v) = asker(slots, weights, o, r), asker(slots, weights, o, r + 1)
            for at, x in zip((r, r + 1), paired(low[i], low[j], w, v, True)):
                out[at] = x.astype(out.dtype)
        out[capacity] = listed.astype(out.dtype)


def remote_kernel(
    capacity, asked, slots, asked_row, left, later, before, from8, from2, from1,
    weights, factor, back, low, out8, out4, out2, out1, resid,
):
    leaf_dev, half = back.shape[0], left.shape[0]
    resid[pl.ds(0, half)] = left[...]
    resid[pl.ds(half, leaf_dev - half)] = later[...]
    resid[leaf_dev] = jnp.zeros(left.shape[1:], left.dtype)
    low[leaf_dev] = jnp.zeros(left.shape[1:], low.dtype)

    for o, rows in ((2, before), (3, from8), (1, from2), (0, from1)):
        found = []
        for r in range(0, capacity, 2):
            (i, w), (j, v) = asker(slots, weights, o, r), asker(slots, weights, o, r + 1)
            at = (asked[0, o * SLOTS + r], asked[0, o * SLOTS + r + 1]) if o == 2 else (r, r + 1)
            found += zip((i, j), paired(rows[at[0]], rows[at[1]], w, v))
        for i, mean in found:
            resid[i] = resid[i] - mean

    def leaves(c, carry):
        pairs = [c * LEAVES + u for u in range(0, LEAVES, 2)]
        innov = [
            paired(
                resid[i].astype(jnp.bfloat16), resid[i + 1].astype(jnp.bfloat16),
                factor[i], factor[i + 1],
            )
            for i in pairs
        ]
        for i, (x, y) in zip(pairs, innov):
            both = paired(
                x.astype(jnp.bfloat16), y.astype(jnp.bfloat16), factor[i], factor[i + 1], True
            )
            for j, z in zip((i, i + 1), both):
                back[j] = z
                low[j] = z.astype(jnp.bfloat16)
        return carry

    lax.fori_loop(0, leaf_dev // LEAVES, leaves, 0)
    remote_terms(
        capacity, slots, asked_row, low, weights, ((3, out8), (2, out4), (1, out2), (0, out1))
    )


def home_kernel(home, back, low, weights, part, acc):
    leaf_dev = back.shape[0]
    fan, width = weights.shape[1], weights.shape[2]
    acc[pl.ds(0, leaf_dev)] = -back[...]
    acc[leaf_dev] = jnp.zeros(back.shape[1:], back.dtype)

    def some(c, carry):
        found = []
        for u in range(0, LEAVES, 2):
            i = c * LEAVES + u
            found += zip((i, i + 1), paired(
                low[i], low[i + 1],
                weights[i].reshape(fan * width, width),
                weights[i + 1].reshape(fan * width, width), True,
            ))
        for i, x in found:
            for k in range(fan):
                j = home[k, i]
                acc[j] = acc[j] + x[:, k * width : (k + 1) * width]
        return carry

    lax.fori_loop(0, leaf_dev // LEAVES, some, 0)
    part[...] = acc[pl.ds(0, leaf_dev)]


def add_kernel(capacity, offsets, part, *refs):
    returned, (out, listed, wanted, sem) = refs[: len(offsets)], refs[len(offsets) :]
    for n, (o, rows) in enumerate(zip(offsets, returned)):
        listed[n : n + 1] = rows[capacity].astype(jnp.float32)[0:1].astype(jnp.int32)
    fetch = pltpu.make_async_copy(listed, wanted, sem)
    fetch.start()
    out[...] = part[...]
    fetch.wait()
    for n, (o, rows) in enumerate(zip(offsets, returned)):
        for r in range(capacity):
            j = wanted[n, o * SLOTS + r]
            out[j] = out[j] + rows[r].astype(jnp.float32)


def call(body, name, out_shape, ins, outs, limit, flops=0, moved=0, scratch=()):
    spec = lambda space: pl.BlockSpec(memory_space=space)
    return pl.pallas_call(
        body,
        out_shape=out_shape,
        in_specs=[spec(space) for space in ins],
        out_specs=tuple(spec(space) for space in outs),
        scratch_shapes=scratch,
        compiler_params=pltpu.CompilerParams(vmem_limit_bytes=limit * MIB),
        cost_estimate=pl.CostEstimate(flops=flops, bytes_accessed=moved, transcendentals=0),
        name=name,
    )


def placed(x, space):
    return pltpu.with_memory_space_constraint(x, space)


def per_device(latent, cond_lists, cond_weights, precision_factor):
    devices = lax.axis_size("kx")
    leaf_dev, samples, width = latent.shape
    fan = cond_lists.shape[1]
    capacity = fan * leaf_dev // 8
    everyone = range(devices)
    shape = jax.ShapeDtypeStruct
    some_rows = shape((capacity, samples, width), jnp.bfloat16)
    sent = shape((capacity + 1, samples, width), jnp.bfloat16)
    all_rows = shape(latent.shape, jnp.float32)
    one_list = shape((1, 4 * SLOTS), jnp.int32)
    heavy = cond_weights.size * 2

    def passed(x, route):
        return lax.ppermute(x, "kx", route)

    before = passed(latent, [(i, i + 4) for i in everyone if i + 4 < devices])
    asked, slots, home = call(
        index_kernel, "index",
        (one_list, shape((2, 4 * SLOTS), jnp.int32), shape((fan, leaf_dev), jnp.int32)),
        [VMEM], [VMEM] * 3, 4, moved=2 * MIB,
    )(placed(cond_lists.T, HBM))
    ask8 = passed(asked, [(i, i - 4) for i in everyone if i >= 4])
    ask2 = passed(asked, [(i, i ^ 2) for i in everyone])
    ask1 = passed(asked, [(i, i // 4 * 4 + (i + 3) % 4) for i in everyone])
    half = leaf_dev // 2
    left, held_w, rows = call(
        early_kernel, "early",
        (
            shape((half, samples, width), jnp.float32), shape(cond_weights.shape, jnp.bfloat16),
            shape((leaf_dev + 8, samples, width), jnp.bfloat16),
        ),
        [SMEM, HBM, HBM], [VMEM] * 3, 14, moved=heavy // 2,
        scratch=[pltpu.SemaphoreType.DMA, pltpu.SemaphoreType.DMA((leaf_dev // CHUNK,))],
    )(home, placed(latent, HBM), placed(cond_weights, HBM))
    serve8, serve2, serve1 = call(
        functools.partial(serve_kernel, capacity), "serve", (some_rows,) * 3,
        [SMEM] * 3 + [VMEM] * 2 + [ANY], [VMEM] * 3, 4, moved=4 * MIB,
    )(ask8, ask2, ask1, rows, before, left)
    from8 = passed(serve8, [(i, i + 4) for i in everyone if i >= 4 and i + 4 < devices])
    from2 = passed(serve2, [(i, i ^ 2) for i in everyone])
    from1 = passed(serve1, [(i, i // 4 * 4 + (i + 1) % 4) for i in everyone])
    later, held_f = call(
        late_kernel, "late",
        (
            shape((leaf_dev - half, samples, width), jnp.float32),
            shape(precision_factor.shape, jnp.bfloat16),
        ),
        [SMEM, VMEM, ANY, VMEM, HBM], [VMEM] * 2, 8, moved=heavy // 2,
        scratch=[pltpu.SemaphoreType.DMA],
    )(home, rows, before, held_w, placed(precision_factor, HBM))
    back, low, out8, out4, out2, out1 = call(
        functools.partial(remote_kernel, capacity), "remote",
        (all_rows, shape((leaf_dev + 8, samples, width), jnp.bfloat16)) + (sent,) * 4,
        [SMEM] * 2 + [VMEM] * 9, [VMEM] * 6, 8, moved=heavy,
        scratch=[VMEM((leaf_dev + 8, samples, width), jnp.float32)],
    )(asked, slots, asked, left, later, before, from8, from2, from1, held_w, held_f)
    returned = [
        passed(x, [(i, i - reach) for i in everyone if i >= reach])
        for reach, x in ((8, out8), (4, out4), (2, out2), (1, out1))
    ]
    (part,) = call(
        home_kernel, "home", (all_rows,), [SMEM] + [VMEM] * 3, [VMEM], 6, moved=heavy,
        scratch=[VMEM((leaf_dev + 8, samples, width), jnp.float32)],
    )(home, back, low, held_w)
    lists = (4, 4 * SLOTS)
    (gradient,) = call(
        functools.partial(add_kernel, capacity, (3, 2, 1, 0)), "add", (all_rows,), [VMEM] * 5,
        [VMEM], 6, moved=4 * MIB,
        scratch=[VMEM(lists, jnp.int32), SMEM(lists, jnp.int32), pltpu.SemaphoreType.DMA],
    )(part, *returned)
    return gradient


def solution(mesh):
    return jax.shard_map(
        per_device,
        mesh=mesh,
        in_specs=(
            P(("groups", "kx"), None, None),
            P(("groups", "kx"), None),
            P(("groups", "kx"), None, None, None),
            P(("groups", "kx"), None, None),
        ),
        out_specs=P(("groups", "kx"), None, None),
        check_vma=False,
    )
```

```python
import functools

import jax
import jax.numpy as jnp
from jax import lax
from jax.experimental import pallas as pl
from jax.experimental.pallas import tpu as pltpu
from jax.sharding import PartitionSpec as P

SLOTS = 32
CHUNK = 8
LEAVES = 16
MIB = 2**20
BY_ROWS = (((1,), (1,)), ((), ()))
VMEM, SMEM, HBM, ANY = pltpu.VMEM, pltpu.SMEM, pltpu.HBM, pl.ANY


def index_kernel(lists, asked, slots, home):
    fan, leaf_dev = lists.shape
    me = lax.axis_index("kx")
    behind = me * leaf_dev - lists[...]
    kind = (
        (behind > 0).astype(jnp.int32)
        + (behind > leaf_dev).astype(jnp.int32)
        + (behind > 2 * leaf_dev).astype(jnp.int32)
        + (behind > 4 * leaf_dev).astype(jnp.int32)
    )
    reach = jnp.where(kind == 4, 8, jnp.where(kind == 3, 4, kind))
    row = reach * leaf_dev - behind
    home[...] = jnp.where(kind == 0, row, leaf_dev)

    def grid(shape, dim):
        return lax.broadcasted_iota(jnp.int32, shape, dim)

    def low(x):
        return x.astype(jnp.float32).astype(jnp.bfloat16)

    every = 4 * fan
    mask = jnp.concatenate([(kind == o).astype(jnp.float32) for o in range(1, 5)], axis=0)
    earlier = low(grid((leaf_dev, leaf_dev), 0) < grid((leaf_dev, leaf_dev), 1))
    a, b = grid((every, every), 0), grid((every, every), 1)
    above = (b < a)
    for o in range(1, 4):
        above = above & ((a < o * fan) | (b >= o * fan))
    within = jnp.dot(low(mask), earlier, preferred_element_type=jnp.float32)
    base = jnp.sum(
        jnp.dot(low(above), low(mask), preferred_element_type=jnp.float32), axis=1, keepdims=True
    )
    place = jnp.where(mask > 0.0, within + base, -1.0)
    slot = grid((SLOTS, leaf_dev), 0).astype(jnp.float32)
    leaf = grid((1, leaf_dev), 1).astype(jnp.float32)
    ones = jnp.ones((1, leaf_dev), jnp.float32)
    total = jnp.zeros((8, 4 * SLOTS), jnp.float32)
    for k in range(fan):
        hit = jnp.concatenate(
            [(place[o * fan + k : o * fan + k + 1] == slot).astype(jnp.float32) for o in range(4)],
            axis=0,
        )
        facts = jnp.concatenate(
            [row[k : k + 1].astype(jnp.float32), leaf, k * ones, ones]
            + [jnp.zeros((4, leaf_dev), jnp.float32)], axis=0,
        )
        total = total + lax.dot_general(
            low(facts), low(hit), BY_ROWS, preferred_element_type=jnp.float32
        )
    asked[...] = total[0:1].astype(jnp.int32)
    slots[0:1] = jnp.where(total[3:4] > 0.0, total[1:2], float(leaf_dev)).astype(jnp.int32)
    slots[1:2] = total[2:3].astype(jnp.int32)


def beside(xs):
    return jnp.concatenate(xs, axis=1)


def below(xs):
    return jnp.concatenate(xs, axis=0)


def paired(x, y, left, right, by_rows=False):
    samples = x.shape[0]
    if by_rows:
        wide = left.shape[0]
        both = lax.dot_general(
            below([x, y]), below([left, right]), BY_ROWS, preferred_element_type=jnp.float32
        )
    else:
        wide = left.shape[1]
        both = jnp.dot(below([x, y]), beside([left, right]), preferred_element_type=jnp.float32)
    return both[:samples, :wide], both[samples:, wide:]


def local_means(leaves, home, rows, weights, left, first):
    fan, width = weights.shape[1], weights.shape[2]
    for i in leaves:
        means = paired(
            beside([rows[home[k, i]] for k in range(fan)]),
            beside([rows[home[k, i + 1]] for k in range(fan)]),
            weights[i].reshape(fan * width, width),
            weights[i + 1].reshape(fan * width, width),
        )
        for j, mean in zip((i, i + 1), means):
            left[j - first] = rows[j].astype(jnp.float32) - mean


def fetches(weights, held, sem, first, leaves):
    parts = [(at, pl.ds(at, CHUNK)) for at in range(first, first + leaves, CHUNK)]
    return [
        (range(at, at + CHUNK, 2), pltpu.make_async_copy(weights.at[p], held.at[p], sem.at[n]))
        for n, (at, p) in enumerate(parts)
    ]


def early_kernel(home, latent, weights, left, held_w, rows, row_sem, w_sem):
    leaf_dev, half = latent.shape[0], left.shape[0]
    fetch_rows = pltpu.make_async_copy(latent, rows.at[pl.ds(0, leaf_dev)], row_sem)
    fetch_rows.start()
    parts = fetches(weights, held_w, w_sem, 0, half)
    for _, fetch in parts:
        fetch.start()
    rows[leaf_dev] = jnp.zeros(latent.shape[1:], latent.dtype)
    fetch_rows.wait()
    for leaves, fetch in parts:
        fetch.wait()
        local_means(leaves, home, rows, held_w, left, 0)


def late_kernel(
    home, rows, before, partly_held, weights, factor, left, held_w, held_f, w_sem, f_sem
):
    leaf_dev, half = weights.shape[0], left.shape[0]
    first = leaf_dev - half
    parts = fetches(weights, held_w, w_sem, first, half)
    for _, fetch in parts:
        fetch.start()
    fetch_factor = pltpu.make_async_copy(factor, held_f, f_sem)
    fetch_factor.start()
    for leaves, fetch in parts:
        fetch.wait()
        local_means(leaves, home, rows, held_w, left, first)
    fetch_factor.wait()


def serve_kernel(capacity, ask8, ask2, ask1, latent, before, left, out8, out2, out1):
    me = lax.axis_index("kx")
    def pick(o, ask, rows, out):
        for r in range(capacity):
            out[r] = rows[ask[0, o * SLOTS + r]]

    pick(3, ask8, before, out8)
    for o, ask, out, bits in ((1, ask2, out2, 2), (0, ask1, out1, 3)):
        relays = lax.bitwise_and(me, bits) == bits

        @pl.when(relays)
        def _():
            pick(o, ask, before, out)

        @pl.when(jnp.logical_not(relays))
        def _():
            pick(o, ask, latent, out)


def asker(slots, weights, o, r):
    i = slots[0, o * SLOTS + r]
    return i, weights[jnp.minimum(i, weights.shape[0] - 1), slots[1, o * SLOTS + r]]


def remote_terms(capacity, slots, asked_row, low, weights, outs):
    listed = jnp.broadcast_to(asked_row[...].astype(jnp.float32), low.shape[1:])
    for o, out in outs:
        for r in range(0, capacity, 2):
            (i, w), (j, v) = asker(slots, weights, o, r), asker(slots, weights, o, r + 1)
            for at, x in zip((r, r + 1), paired(low[i], low[j], w, v, True)):
                out[at] = x.astype(out.dtype)
        out[capacity] = listed.astype(out.dtype)


def remote_kernel(
    capacity, asked, slots, asked_row, left, later, before, from8, from2, from1,
    weights, factor, back, low, out8, out4, out2, out1, resid,
):
    leaf_dev, half = back.shape[0], left.shape[0]
    resid[pl.ds(0, half)] = left[...]
    resid[pl.ds(half, leaf_dev - half)] = later[...]
    resid[leaf_dev] = jnp.zeros(left.shape[1:], left.dtype)
    low[leaf_dev] = jnp.zeros(left.shape[1:], low.dtype)

    for o, rows in ((2, before), (3, from8), (1, from2), (0, from1)):
        found = []
        for r in range(0, capacity, 2):
            (i, w), (j, v) = asker(slots, weights, o, r), asker(slots, weights, o, r + 1)
            at = (asked[0, o * SLOTS + r], asked[0, o * SLOTS + r + 1]) if o == 2 else (r, r + 1)
            found += zip((i, j), paired(rows[at[0]], rows[at[1]], w, v))
        for i, mean in found:
            resid[i] = resid[i] - mean

    def leaves(c, carry):
        pairs = [c * LEAVES + u for u in range(0, LEAVES, 2)]
        innov = [
            paired(
                resid[i].astype(jnp.bfloat16), resid[i + 1].astype(jnp.bfloat16),
                factor[i], factor[i + 1],
            )
            for i in pairs
        ]
        for i, (x, y) in zip(pairs, innov):
            both = paired(
                x.astype(jnp.bfloat16), y.astype(jnp.bfloat16), factor[i], factor[i + 1], True
            )
            for j, z in zip((i, i + 1), both):
                back[j] = z
                low[j] = z.astype(jnp.bfloat16)
        return carry

    lax.fori_loop(0, leaf_dev // LEAVES, leaves, 0)
    remote_terms(
        capacity, slots, asked_row, low, weights, ((3, out8), (2, out4), (1, out2), (0, out1))
    )


def home_kernel(home, back, low, weights, part, acc):
    leaf_dev = back.shape[0]
    fan, width = weights.shape[1], weights.shape[2]
    acc[pl.ds(0, leaf_dev)] = -back[...]
    acc[leaf_dev] = jnp.zeros(back.shape[1:], back.dtype)

    def some(c, carry):
        found = []
        for u in range(0, LEAVES, 2):
            i = c * LEAVES + u
            found += zip((i, i + 1), paired(
                low[i], low[i + 1],
                weights[i].reshape(fan * width, width),
                weights[i + 1].reshape(fan * width, width), True,
            ))
        for i, x in found:
            for k in range(fan):
                j = home[k, i]
                acc[j] = acc[j] + x[:, k * width : (k + 1) * width]
        return carry

    lax.fori_loop(0, leaf_dev // LEAVES, some, 0)
    part[...] = acc[pl.ds(0, leaf_dev)]


def add_kernel(capacity, offsets, part, *refs):
    returned, (out, listed, wanted, sem) = refs[: len(offsets)], refs[len(offsets) :]
    for n, (o, rows) in enumerate(zip(offsets, returned)):
        listed[n : n + 1] = rows[capacity].astype(jnp.float32)[0:1].astype(jnp.int32)
    fetch = pltpu.make_async_copy(listed, wanted, sem)
    fetch.start()
    out[...] = part[...]
    fetch.wait()
    for n, (o, rows) in enumerate(zip(offsets, returned)):
        for r in range(capacity):
            j = wanted[n, o * SLOTS + r]
            out[j] = out[j] + rows[r].astype(jnp.float32)


def call(body, name, out_shape, ins, outs, limit, flops=0, moved=0, scratch=(), aliases={}):
    spec = lambda space: pl.BlockSpec(memory_space=space)
    return pl.pallas_call(
        body,
        out_shape=out_shape,
        in_specs=[spec(space) for space in ins],
        out_specs=tuple(spec(space) for space in outs),
        scratch_shapes=scratch,
        input_output_aliases=aliases,
        compiler_params=pltpu.CompilerParams(vmem_limit_bytes=limit * MIB),
        cost_estimate=pl.CostEstimate(flops=flops, bytes_accessed=moved, transcendentals=0),
        name=name,
    )


def placed(x, space):
    return pltpu.with_memory_space_constraint(x, space)


def per_device(latent, cond_lists, cond_weights, precision_factor):
    devices = lax.axis_size("kx")
    leaf_dev, samples, width = latent.shape
    fan = cond_lists.shape[1]
    capacity = fan * leaf_dev // 8
    everyone = range(devices)
    shape = jax.ShapeDtypeStruct
    some_rows = shape((capacity, samples, width), jnp.bfloat16)
    sent = shape((capacity + 1, samples, width), jnp.bfloat16)
    all_rows = shape(latent.shape, jnp.float32)
    one_list = shape((1, 4 * SLOTS), jnp.int32)
    heavy = cond_weights.size * 2

    def passed(x, route):
        return lax.ppermute(x, "kx", route)

    before = passed(latent, [(i, i + 4) for i in everyone if i + 4 < devices])
    asked, slots, home = call(
        index_kernel, "index",
        (one_list, shape((2, 4 * SLOTS), jnp.int32), shape((fan, leaf_dev), jnp.int32)),
        [VMEM], [VMEM] * 3, 4, moved=2 * MIB,
    )(placed(cond_lists.T, HBM))
    ask8 = passed(asked, [(i, i - 4) for i in everyone if i >= 4])
    ask2 = passed(asked, [(i, i ^ 2) for i in everyone])
    ask1 = passed(asked, [(i, i // 4 * 4 + (i + 3) % 4) for i in everyone])
    half = leaf_dev // 2
    left, held_w, rows = call(
        early_kernel, "early",
        (
            shape((half, samples, width), jnp.float32), shape(cond_weights.shape, jnp.bfloat16),
            shape((leaf_dev + 8, samples, width), jnp.bfloat16),
        ),
        [SMEM, HBM, HBM], [VMEM] * 3, 14, moved=heavy // 2,
        scratch=[pltpu.SemaphoreType.DMA, pltpu.SemaphoreType.DMA((half // CHUNK,))],
    )(home, placed(latent, HBM), placed(cond_weights, HBM))
    serve8, serve2, serve1 = call(
        functools.partial(serve_kernel, capacity), "serve", (some_rows,) * 3,
        [SMEM] * 3 + [VMEM] * 2 + [ANY], [VMEM] * 3, 4, moved=4 * MIB,
    )(ask8, ask2, ask1, rows, before, left)
    from8 = passed(serve8, [(i, i + 4) for i in everyone if i >= 4 and i + 4 < devices])
    from2 = passed(serve2, [(i, i ^ 2) for i in everyone])
    from1 = passed(serve1, [(i, i // 4 * 4 + (i + 1) % 4) for i in everyone])
    later, held_w, held_f = call(
        late_kernel, "late",
        (
            shape((leaf_dev - half, samples, width), jnp.float32),
            shape(cond_weights.shape, jnp.bfloat16), shape(precision_factor.shape, jnp.bfloat16),
        ),
        [SMEM, VMEM, ANY, VMEM, HBM, HBM], [VMEM] * 3, 14, moved=heavy // 2,
        scratch=[
            pltpu.SemaphoreType.DMA(((leaf_dev - half) // CHUNK,)), pltpu.SemaphoreType.DMA
        ],
        aliases={3: 1},
    )(home, rows, before, held_w, placed(cond_weights, HBM), placed(precision_factor, HBM))
    back, low, out8, out4, out2, out1 = call(
        functools.partial(remote_kernel, capacity), "remote",
        (all_rows, shape((leaf_dev + 8, samples, width), jnp.bfloat16)) + (sent,) * 4,
        [SMEM] * 2 + [VMEM] * 9, [VMEM] * 6, 8, moved=heavy,
        scratch=[VMEM((leaf_dev + 8, samples, width), jnp.float32)],
    )(asked, slots, asked, left, later, before, from8, from2, from1, held_w, held_f)
    returned = [
        passed(x, [(i, i - reach) for i in everyone if i >= reach])
        for reach, x in ((8, out8), (4, out4), (2, out2), (1, out1))
    ]
    (part,) = call(
        home_kernel, "home", (all_rows,), [SMEM] + [VMEM] * 3, [VMEM], 6, moved=heavy,
        scratch=[VMEM((leaf_dev + 8, samples, width), jnp.float32)],
    )(home, back, low, held_w)
    lists = (4, 4 * SLOTS)
    (gradient,) = call(
        functools.partial(add_kernel, capacity, (3, 2, 1, 0)), "add", (all_rows,), [VMEM] * 5,
        [VMEM], 6, moved=4 * MIB,
        scratch=[VMEM(lists, jnp.int32), SMEM(lists, jnp.int32), pltpu.SemaphoreType.DMA],
    )(part, *returned)
    return gradient


def solution(mesh):
    return jax.shard_map(
        per_device,
        mesh=mesh,
        in_specs=(
            P(("groups", "kx"), None, None),
            P(("groups", "kx"), None),
            P(("groups", "kx"), None, None, None),
            P(("groups", "kx"), None, None),
        ),
        out_specs=P(("groups", "kx"), None, None),
        check_vma=False,
    )
```

```python
import functools

import jax
import jax.numpy as jnp
from jax import lax
from jax.experimental import pallas as pl
from jax.experimental.pallas import tpu as pltpu
from jax.sharding import PartitionSpec as P

SLOTS = 32
CHUNK = 8
LEAVES = 16
MIB = 2**20
BY_ROWS = (((1,), (1,)), ((), ()))
VMEM, SMEM, HBM, ANY = pltpu.VMEM, pltpu.SMEM, pltpu.HBM, pl.ANY


def index_kernel(lists, asked, slots, home):
    fan, leaf_dev = lists.shape
    me = lax.axis_index("kx")
    behind = me * leaf_dev - lists[...]
    kind = (
        (behind > 0).astype(jnp.int32)
        + (behind > leaf_dev).astype(jnp.int32)
        + (behind > 2 * leaf_dev).astype(jnp.int32)
        + (behind > 4 * leaf_dev).astype(jnp.int32)
    )
    reach = jnp.where(kind == 4, 8, jnp.where(kind == 3, 4, kind))
    row = reach * leaf_dev - behind
    home[...] = jnp.where(kind == 0, row, leaf_dev)

    def grid(shape, dim):
        return lax.broadcasted_iota(jnp.int32, shape, dim)

    def low(x):
        return x.astype(jnp.float32).astype(jnp.bfloat16)

    every = 4 * fan
    mask = jnp.concatenate([(kind == o).astype(jnp.float32) for o in range(1, 5)], axis=0)
    earlier = low(grid((leaf_dev, leaf_dev), 0) < grid((leaf_dev, leaf_dev), 1))
    a, b = grid((every, every), 0), grid((every, every), 1)
    above = (b < a)
    for o in range(1, 4):
        above = above & ((a < o * fan) | (b >= o * fan))
    within = jnp.dot(low(mask), earlier, preferred_element_type=jnp.float32)
    base = jnp.sum(
        jnp.dot(low(above), low(mask), preferred_element_type=jnp.float32), axis=1, keepdims=True
    )
    place = jnp.where(mask > 0.0, within + base, -1.0)
    slot = grid((SLOTS, leaf_dev), 0).astype(jnp.float32)
    leaf = grid((1, leaf_dev), 1).astype(jnp.float32)
    ones = jnp.ones((1, leaf_dev), jnp.float32)
    total = jnp.zeros((8, 4 * SLOTS), jnp.float32)
    for k in range(fan):
        hit = jnp.concatenate(
            [(place[o * fan + k : o * fan + k + 1] == slot).astype(jnp.float32) for o in range(4)],
            axis=0,
        )
        facts = jnp.concatenate(
            [row[k : k + 1].astype(jnp.float32), leaf, k * ones, ones]
            + [jnp.zeros((4, leaf_dev), jnp.float32)], axis=0,
        )
        total = total + lax.dot_general(
            low(facts), low(hit), BY_ROWS, preferred_element_type=jnp.float32
        )
    asked[...] = total[0:1].astype(jnp.int32)
    slots[0:1] = jnp.where(total[3:4] > 0.0, total[1:2], float(leaf_dev)).astype(jnp.int32)
    slots[1:2] = total[2:3].astype(jnp.int32)


def beside(xs):
    return jnp.concatenate(xs, axis=1)


def below(xs):
    return jnp.concatenate(xs, axis=0)


def paired(x, y, left, right, by_rows=False):
    dims = BY_ROWS if by_rows else (((1,), (0,)), ((), ()))
    return tuple(
        lax.dot_general(rows, weights, dims, preferred_element_type=jnp.float32)
        for rows, weights in ((x, left), (y, right))
    )


def local_means(leaves, home, rows, weights, left, first):
    fan, width = weights.shape[1], weights.shape[2]
    for i in leaves:
        means = paired(
            beside([rows[home[k, i]] for k in range(fan)]),
            beside([rows[home[k, i + 1]] for k in range(fan)]),
            weights[i].reshape(fan * width, width),
            weights[i + 1].reshape(fan * width, width),
        )
        for j, mean in zip((i, i + 1), means):
            left[j - first] = rows[j].astype(jnp.float32) - mean


def fetches(weights, held, sem, first, leaves):
    parts = [(at, pl.ds(at, CHUNK)) for at in range(first, first + leaves, CHUNK)]
    return [
        (range(at, at + CHUNK, 2), pltpu.make_async_copy(weights.at[p], held.at[p], sem.at[n]))
        for n, (at, p) in enumerate(parts)
    ]


def early_kernel(home, latent, weights, left, held_w, rows, row_sem, w_sem):
    leaf_dev, half = latent.shape[0], left.shape[0]
    fetch_rows = pltpu.make_async_copy(latent, rows.at[pl.ds(0, leaf_dev)], row_sem)
    fetch_rows.start()
    parts = fetches(weights, held_w, w_sem, 0, half)
    for _, fetch in parts:
        fetch.start()
    rows[leaf_dev] = jnp.zeros(latent.shape[1:], latent.dtype)
    fetch_rows.wait()
    for leaves, fetch in parts:
        fetch.wait()
        local_means(leaves, home, rows, held_w, left, 0)


def late_kernel(
    home, rows, before, partly_held, weights, factor, left, held_w, held_f, w_sem, f_sem
):
    leaf_dev, half = weights.shape[0], left.shape[0]
    first = leaf_dev - half
    parts = fetches(weights, held_w, w_sem, first, half)
    for _, fetch in parts:
        fetch.start()
    fetch_factor = pltpu.make_async_copy(factor, held_f, f_sem)
    fetch_factor.start()
    for leaves, fetch in parts:
        fetch.wait()
        local_means(leaves, home, rows, held_w, left, first)
    fetch_factor.wait()


def serve_kernel(capacity, ask1, ask2, ask8, latent, before, left, out8, out2, out1):
    me = lax.axis_index("kx")
    def pick(o, ask, rows, out):
        for r in range(capacity):
            out[r] = rows[ask[0, o * SLOTS + r]]

    pick(3, ask8, before, out8)
    for o, ask, out, bits in ((1, ask2, out2, 2), (0, ask1, out1, 3)):
        relays = lax.bitwise_and(me, bits) == bits

        @pl.when(relays)
        def _():
            pick(o, ask, before, out)

        @pl.when(jnp.logical_not(relays))
        def _():
            pick(o, ask, latent, out)


def asker(slots, weights, o, r):
    i = slots[0, o * SLOTS + r]
    return i, weights[jnp.minimum(i, weights.shape[0] - 1), slots[1, o * SLOTS + r]]


def remote_terms(capacity, slots, asked_row, low, weights, outs):
    listed = jnp.broadcast_to(asked_row[...].astype(jnp.float32), low.shape[1:])
    for o, out in outs:
        for r in range(0, capacity, 2):
            (i, w), (j, v) = asker(slots, weights, o, r), asker(slots, weights, o, r + 1)
            for at, x in zip((r, r + 1), paired(low[i], low[j], w, v, True)):
                out[at] = x.astype(out.dtype)
        out[capacity] = listed.astype(out.dtype)


def remote_kernel(
    capacity, asked, slots, asked_row, left, later, before, from2, from1, from8,
    weights, factor, back, low, out8, out4, out2, out1, resid,
):
    leaf_dev, half = back.shape[0], left.shape[0]
    resid[pl.ds(0, half)] = left[...]
    resid[pl.ds(half, leaf_dev - half)] = later[...]
    resid[leaf_dev] = jnp.zeros(left.shape[1:], left.dtype)
    low[leaf_dev] = jnp.zeros(left.shape[1:], low.dtype)

    for o, rows in ((2, before), (3, from8), (1, from2), (0, from1)):
        found = []
        for r in range(0, capacity, 2):
            (i, w), (j, v) = asker(slots, weights, o, r), asker(slots, weights, o, r + 1)
            at = (asked[0, o * SLOTS + r], asked[0, o * SLOTS + r + 1]) if o == 2 else (r, r + 1)
            found += zip((i, j), paired(rows[at[0]], rows[at[1]], w, v))
        for i, mean in found:
            resid[i] = resid[i] - mean

    def leaves(c, carry):
        pairs = [c * LEAVES + u for u in range(0, LEAVES, 2)]
        innov = [
            paired(
                resid[i].astype(jnp.bfloat16), resid[i + 1].astype(jnp.bfloat16),
                factor[i], factor[i + 1],
            )
            for i in pairs
        ]
        for i, (x, y) in zip(pairs, innov):
            both = paired(
                x.astype(jnp.bfloat16), y.astype(jnp.bfloat16), factor[i], factor[i + 1], True
            )
            for j, z in zip((i, i + 1), both):
                back[j] = z
                low[j] = z.astype(jnp.bfloat16)
        return carry

    lax.fori_loop(0, leaf_dev // LEAVES, leaves, 0)
    remote_terms(
        capacity, slots, asked_row, low, weights, ((3, out8), (2, out4), (1, out2), (0, out1))
    )


def home_kernel(home, back, low, weights, part, acc):
    leaf_dev = back.shape[0]
    fan, width = weights.shape[1], weights.shape[2]
    acc[pl.ds(0, leaf_dev)] = -back[...]
    acc[leaf_dev] = jnp.zeros(back.shape[1:], back.dtype)

    def some(c, carry):
        found = []
        for u in range(0, LEAVES, 2):
            i = c * LEAVES + u
            found += zip((i, i + 1), paired(
                low[i], low[i + 1],
                weights[i].reshape(fan * width, width),
                weights[i + 1].reshape(fan * width, width), True,
            ))
        for i, x in found:
            for k in range(fan):
                j = home[k, i]
                acc[j] = acc[j] + x[:, k * width : (k + 1) * width]
        return carry

    lax.fori_loop(0, leaf_dev // LEAVES, some, 0)
    part[...] = acc[pl.ds(0, leaf_dev)]


def add_kernel(capacity, offsets, part, *refs):
    returned, (out, listed, wanted, sem) = refs[: len(offsets)], refs[len(offsets) :]
    for n, (o, rows) in enumerate(zip(offsets, returned)):
        listed[n : n + 1] = rows[capacity].astype(jnp.float32)[0:1].astype(jnp.int32)
    fetch = pltpu.make_async_copy(listed, wanted, sem)
    fetch.start()
    out[...] = part[...]
    fetch.wait()
    for n, (o, rows) in enumerate(zip(offsets, returned)):
        for r in range(capacity):
            j = wanted[n, o * SLOTS + r]
            out[j] = out[j] + rows[r].astype(jnp.float32)


def call(body, name, out_shape, ins, outs, limit, flops=0, moved=0, scratch=(), aliases={}):
    spec = lambda space: pl.BlockSpec(memory_space=space)
    return pl.pallas_call(
        body,
        out_shape=out_shape,
        in_specs=[spec(space) for space in ins],
        out_specs=tuple(spec(space) for space in outs),
        scratch_shapes=scratch,
        input_output_aliases=aliases,
        compiler_params=pltpu.CompilerParams(vmem_limit_bytes=limit * MIB),
        cost_estimate=pl.CostEstimate(flops=flops, bytes_accessed=moved, transcendentals=0),
        name=name,
    )


def placed(x, space):
    return pltpu.with_memory_space_constraint(x, space)


def per_device(latent, cond_lists, cond_weights, precision_factor):
    devices = lax.axis_size("kx")
    leaf_dev, samples, width = latent.shape
    fan = cond_lists.shape[1]
    capacity = fan * leaf_dev // 8
    everyone = range(devices)
    shape = jax.ShapeDtypeStruct
    some_rows = shape((capacity, samples, width), jnp.bfloat16)
    sent = shape((capacity + 1, samples, width), jnp.bfloat16)
    all_rows = shape(latent.shape, jnp.float32)
    one_list = shape((1, 4 * SLOTS), jnp.int32)
    heavy = cond_weights.size * 2

    def passed(x, route):
        return lax.ppermute(x, "kx", route)

    before = passed(latent, [(i, i + 4) for i in everyone if i + 4 < devices])
    asked, slots, home = call(
        index_kernel, "index",
        (one_list, shape((2, 4 * SLOTS), jnp.int32), shape((fan, leaf_dev), jnp.int32)),
        [VMEM], [VMEM] * 3, 4, moved=2 * MIB,
    )(placed(cond_lists.T, HBM))
    ask8 = passed(asked, [(i, i - 4) for i in everyone if i >= 4])
    ask2 = passed(asked, [(i, i ^ 2) for i in everyone])
    ask1 = passed(asked, [(i, i // 4 * 4 + (i + 3) % 4) for i in everyone])
    half = leaf_dev // 2
    left, held_w, rows = call(
        early_kernel, "early",
        (
            shape((half, samples, width), jnp.float32), shape(cond_weights.shape, jnp.bfloat16),
            shape((leaf_dev + 8, samples, width), jnp.bfloat16),
        ),
        [SMEM, HBM, HBM], [VMEM] * 3, 14, moved=heavy // 2,
        scratch=[pltpu.SemaphoreType.DMA, pltpu.SemaphoreType.DMA((half // CHUNK,))],
    )(home, placed(latent, HBM), placed(cond_weights, HBM))
    serve8, serve2, serve1 = call(
        functools.partial(serve_kernel, capacity), "serve", (some_rows,) * 3,
        [SMEM] * 3 + [VMEM] * 2 + [ANY], [VMEM] * 3, 4, moved=4 * MIB,
    )(ask1, ask2, ask8, rows, before, left)
    from8 = passed(serve8, [(i, i + 4) for i in everyone if i >= 4 and i + 4 < devices])
    from2 = passed(serve2, [(i, i ^ 2) for i in everyone])
    from1 = passed(serve1, [(i, i // 4 * 4 + (i + 1) % 4) for i in everyone])
    later, held_w, held_f = call(
        late_kernel, "late",
        (
            shape((leaf_dev - half, samples, width), jnp.float32),
            shape(cond_weights.shape, jnp.bfloat16), shape(precision_factor.shape, jnp.bfloat16),
        ),
        [SMEM, VMEM, ANY, VMEM, HBM, HBM], [VMEM] * 3, 14, moved=heavy // 2,
        scratch=[
            pltpu.SemaphoreType.DMA(((leaf_dev - half) // CHUNK,)), pltpu.SemaphoreType.DMA
        ],
        aliases={3: 1},
    )(home, rows, before, held_w, placed(cond_weights, HBM), placed(precision_factor, HBM))
    back, low, out8, out4, out2, out1 = call(
        functools.partial(remote_kernel, capacity), "remote",
        (all_rows, shape((leaf_dev + 8, samples, width), jnp.bfloat16)) + (sent,) * 4,
        [SMEM] * 2 + [VMEM] * 9, [VMEM] * 6, 8, moved=heavy,
        scratch=[VMEM((leaf_dev + 8, samples, width), jnp.float32)],
    )(asked, slots, asked, left, later, before, from2, from1, from8, held_w, held_f)
    returned = [
        passed(x, [(i, i - reach) for i in everyone if i >= reach])
        for reach, x in ((8, out8), (4, out4), (2, out2), (1, out1))
    ]
    (part,) = call(
        home_kernel, "home", (all_rows,), [SMEM] + [VMEM] * 3, [VMEM], 6, moved=heavy,
        scratch=[VMEM((leaf_dev + 8, samples, width), jnp.float32)],
    )(home, back, low, held_w)
    lists = (4, 4 * SLOTS)
    (gradient,) = call(
        functools.partial(add_kernel, capacity, (3, 2, 1, 0)), "add", (all_rows,), [VMEM] * 5,
        [VMEM], 6, moved=4 * MIB,
        scratch=[VMEM(lists, jnp.int32), SMEM(lists, jnp.int32), pltpu.SemaphoreType.DMA],
    )(part, *returned)
    return gradient


def solution(mesh):
    return jax.shard_map(
        per_device,
        mesh=mesh,
        in_specs=(
            P(("groups", "kx"), None, None),
            P(("groups", "kx"), None),
            P(("groups", "kx"), None, None, None),
            P(("groups", "kx"), None, None),
        ),
        out_specs=P(("groups", "kx"), None, None),
        check_vma=False,
    )
```

```python
import functools

import jax
import jax.numpy as jnp
from jax import lax
from jax.experimental import pallas as pl
from jax.experimental.pallas import tpu as pltpu
from jax.sharding import PartitionSpec as P

SLOTS = 32
CHUNK = 8
LEAVES = 16
MIB = 2**20
BY_ROWS = (((1,), (1,)), ((), ()))
VMEM, SMEM, HBM, ANY = pltpu.VMEM, pltpu.SMEM, pltpu.HBM, pl.ANY


def index_kernel(lists, asked, slots, home):
    fan, leaf_dev = lists.shape
    me = lax.axis_index("kx")
    behind = me * leaf_dev - lists[...]
    kind = (
        (behind > 0).astype(jnp.int32)
        + (behind > leaf_dev).astype(jnp.int32)
        + (behind > 2 * leaf_dev).astype(jnp.int32)
        + (behind > 4 * leaf_dev).astype(jnp.int32)
    )
    reach = jnp.where(kind == 4, 8, jnp.where(kind == 3, 4, kind))
    row = reach * leaf_dev - behind
    home[...] = jnp.where(kind == 0, row, leaf_dev)

    def grid(shape, dim):
        return lax.broadcasted_iota(jnp.int32, shape, dim)

    def low(x):
        return x.astype(jnp.float32).astype(jnp.bfloat16)

    every = 4 * fan
    mask = jnp.concatenate([(kind == o).astype(jnp.float32) for o in range(1, 5)], axis=0)
    earlier = low(grid((leaf_dev, leaf_dev), 0) < grid((leaf_dev, leaf_dev), 1))
    a, b = grid((every, every), 0), grid((every, every), 1)
    above = (b < a)
    for o in range(1, 4):
        above = above & ((a < o * fan) | (b >= o * fan))
    within = jnp.dot(low(mask), earlier, preferred_element_type=jnp.float32)
    base = jnp.sum(
        jnp.dot(low(above), low(mask), preferred_element_type=jnp.float32), axis=1, keepdims=True
    )
    place = jnp.where(mask > 0.0, within + base, -1.0)
    slot = grid((SLOTS, leaf_dev), 0).astype(jnp.float32)
    leaf = grid((1, leaf_dev), 1).astype(jnp.float32)
    ones = jnp.ones((1, leaf_dev), jnp.float32)
    total = jnp.zeros((8, 4 * SLOTS), jnp.float32)
    for k in range(fan):
        hit = jnp.concatenate(
            [(place[o * fan + k : o * fan + k + 1] == slot).astype(jnp.float32) for o in range(4)],
            axis=0,
        )
        facts = jnp.concatenate(
            [row[k : k + 1].astype(jnp.float32), leaf, k * ones, ones]
            + [jnp.zeros((4, leaf_dev), jnp.float32)], axis=0,
        )
        total = total + lax.dot_general(
            low(facts), low(hit), BY_ROWS, preferred_element_type=jnp.float32
        )
    asked[...] = total[0:1].astype(jnp.int32)
    slots[0:1] = jnp.where(total[3:4] > 0.0, total[1:2], float(leaf_dev)).astype(jnp.int32)
    slots[1:2] = total[2:3].astype(jnp.int32)


def beside(xs):
    return jnp.concatenate(xs, axis=1)


def below(xs):
    return jnp.concatenate(xs, axis=0)


def paired(x, y, left, right, by_rows=False):
    samples = x.shape[0]
    if by_rows:
        wide = left.shape[0]
        both = lax.dot_general(
            below([x, y]), below([left, right]), BY_ROWS, preferred_element_type=jnp.float32
        )
    else:
        wide = left.shape[1]
        both = jnp.dot(below([x, y]), beside([left, right]), preferred_element_type=jnp.float32)
    return both[:samples, :wide], both[samples:, wide:]


def local_means(home, rows, latent_rows, weights, held, left, sem, first):
    fan, width = weights.shape[1], weights.shape[2]
    leaves = left.shape[0]

    def fetch(c):
        part = pl.ds(first + c * CHUNK, CHUNK)
        return pltpu.make_async_copy(weights.at[part], held.at[part], sem.at[c])

    for c in range(leaves // CHUNK):
        fetch(c).start()
    latent_rows()

    def some(c, carry):
        fetch(c).wait()
        for u in range(CHUNK):
            i = first + c * CHUNK + u
            mean = jnp.dot(
                beside([rows[home[k, i]] for k in range(fan)]),
                held[i].reshape(fan * width, width), preferred_element_type=jnp.float32,
            )
            left[c * CHUNK + u] = rows[i].astype(jnp.float32) - mean
        return carry

    lax.fori_loop(0, leaves // CHUNK, some, 0)


def early_kernel(home, latent, weights, left, held_w, rows, row_sem, w_sem):
    leaf_dev = latent.shape[0]
    fetch_rows = pltpu.make_async_copy(latent, rows.at[pl.ds(0, leaf_dev)], row_sem)
    fetch_rows.start()

    def latent_rows():
        rows[leaf_dev] = jnp.zeros(latent.shape[1:], latent.dtype)
        fetch_rows.wait()

    local_means(home, rows, latent_rows, weights, held_w, left, w_sem, 0)


def late_kernel(
    home, rows, before, partly_held, weights, factor, left, held_w, held_f, w_sem, f_sem
):
    fetch_factor = pltpu.make_async_copy(factor, held_f, f_sem)
    first = weights.shape[0] - left.shape[0]
    local_means(home, rows, fetch_factor.start, weights, held_w, left, w_sem, first)
    fetch_factor.wait()


def serve_kernel(capacity, ask1, ask2, ask8, latent, before, left, out8, out2, out1):
    me = lax.axis_index("kx")
    def pick(o, ask, rows, out):
        for r in range(capacity):
            out[r] = rows[ask[0, o * SLOTS + r]]

    pick(3, ask8, before, out8)
    for o, ask, out, bits in ((1, ask2, out2, 2), (0, ask1, out1, 3)):
        relays = lax.bitwise_and(me, bits) == bits

        @pl.when(relays)
        def _():
            pick(o, ask, before, out)

        @pl.when(jnp.logical_not(relays))
        def _():
            pick(o, ask, latent, out)


def asker(slots, weights, o, r):
    i = slots[0, o * SLOTS + r]
    return i, weights[jnp.minimum(i, weights.shape[0] - 1), slots[1, o * SLOTS + r]]


def remote_terms(capacity, slots, asked_row, low, weights, outs):
    listed = jnp.broadcast_to(asked_row[...].astype(jnp.float32), low.shape[1:])
    for o, out in outs:
        for r in range(0, capacity, 2):
            (i, w), (j, v) = asker(slots, weights, o, r), asker(slots, weights, o, r + 1)
            for at, x in zip((r, r + 1), paired(low[i], low[j], w, v, True)):
                out[at] = x.astype(out.dtype)
        out[capacity] = listed.astype(out.dtype)


def remote_kernel(
    capacity, asked, slots, asked_row, left, later, before, from2, from8, from1,
    weights, factor, back, low, out8, out4, out2, out1, resid,
):
    leaf_dev, half = back.shape[0], left.shape[0]
    resid[pl.ds(0, half)] = left[...]
    resid[pl.ds(half, leaf_dev - half)] = later[...]
    resid[leaf_dev] = jnp.zeros(left.shape[1:], left.dtype)
    low[leaf_dev] = jnp.zeros(left.shape[1:], low.dtype)

    for o, rows in ((2, before), (3, from8), (1, from2), (0, from1)):
        found = []
        for r in range(0, capacity, 2):
            (i, w), (j, v) = asker(slots, weights, o, r), asker(slots, weights, o, r + 1)
            at = (asked[0, o * SLOTS + r], asked[0, o * SLOTS + r + 1]) if o == 2 else (r, r + 1)
            found += zip((i, j), paired(rows[at[0]], rows[at[1]], w, v))
        for i, mean in found:
            resid[i] = resid[i] - mean

    def leaves(c, carry):
        pairs = [c * LEAVES + u for u in range(0, LEAVES, 2)]
        innov = [
            paired(
                resid[i].astype(jnp.bfloat16), resid[i + 1].astype(jnp.bfloat16),
                factor[i], factor[i + 1],
            )
            for i in pairs
        ]
        for i, (x, y) in zip(pairs, innov):
            both = paired(
                x.astype(jnp.bfloat16), y.astype(jnp.bfloat16), factor[i], factor[i + 1], True
            )
            for j, z in zip((i, i + 1), both):
                back[j] = z
                low[j] = z.astype(jnp.bfloat16)
        return carry

    lax.fori_loop(0, leaf_dev // LEAVES, leaves, 0)
    remote_terms(
        capacity, slots, asked_row, low, weights, ((3, out8), (2, out4), (1, out2), (0, out1))
    )


def home_kernel(home, back, low, weights, part, acc):
    leaf_dev = back.shape[0]
    fan, width = weights.shape[1], weights.shape[2]
    acc[pl.ds(0, leaf_dev)] = -back[...]
    acc[leaf_dev] = jnp.zeros(back.shape[1:], back.dtype)

    def some(c, carry):
        found = []
        for u in range(LEAVES):
            i = c * LEAVES + u
            found.append((i, lax.dot_general(
                low[i], weights[i].reshape(fan * width, width), BY_ROWS,
                preferred_element_type=jnp.float32,
            )))
        for i, x in found:
            for k in range(fan):
                j = home[k, i]
                acc[j] = acc[j] + x[:, k * width : (k + 1) * width]
        return carry

    lax.fori_loop(0, leaf_dev // LEAVES, some, 0)
    part[...] = acc[pl.ds(0, leaf_dev)]


def add_kernel(capacity, offsets, part, *refs):
    returned, (out, listed, wanted, sem) = refs[: len(offsets)], refs[len(offsets) :]
    for n, (o, rows) in enumerate(zip(offsets, returned)):
        listed[n : n + 1] = rows[capacity].astype(jnp.float32)[0:1].astype(jnp.int32)
    fetch = pltpu.make_async_copy(listed, wanted, sem)
    fetch.start()
    out[...] = part[...]
    fetch.wait()
    for n, (o, rows) in enumerate(zip(offsets, returned)):
        for r in range(capacity):
            j = wanted[n, o * SLOTS + r]
            out[j] = out[j] + rows[r].astype(jnp.float32)


def call(body, name, out_shape, ins, outs, limit, flops=0, moved=0, scratch=(), aliases={}):
    spec = lambda space: pl.BlockSpec(memory_space=space)
    return pl.pallas_call(
        body,
        out_shape=out_shape,
        in_specs=[spec(space) for space in ins],
        out_specs=tuple(spec(space) for space in outs),
        scratch_shapes=scratch,
        input_output_aliases=aliases,
        compiler_params=pltpu.CompilerParams(vmem_limit_bytes=limit * MIB),
        cost_estimate=pl.CostEstimate(flops=flops, bytes_accessed=moved, transcendentals=0),
        name=name,
    )


def placed(x, space):
    return pltpu.with_memory_space_constraint(x, space)


def per_device(latent, cond_lists, cond_weights, precision_factor):
    devices = lax.axis_size("kx")
    leaf_dev, samples, width = latent.shape
    fan = cond_lists.shape[1]
    capacity = fan * leaf_dev // 8
    everyone = range(devices)
    shape = jax.ShapeDtypeStruct
    some_rows = shape((capacity, samples, width), jnp.bfloat16)
    sent = shape((capacity + 1, samples, width), jnp.bfloat16)
    all_rows = shape(latent.shape, jnp.float32)
    one_list = shape((1, 4 * SLOTS), jnp.int32)
    heavy = cond_weights.size * 2

    def passed(x, route):
        return lax.ppermute(x, "kx", route)

    before = passed(latent, [(i, i + 4) for i in everyone if i + 4 < devices])
    asked, slots, home = call(
        index_kernel, "index",
        (one_list, shape((2, 4 * SLOTS), jnp.int32), shape((fan, leaf_dev), jnp.int32)),
        [VMEM], [VMEM] * 3, 4, moved=2 * MIB,
    )(placed(cond_lists.T, HBM))
    ask8 = passed(asked, [(i, i - 4) for i in everyone if i >= 4])
    ask2 = passed(asked, [(i, i ^ 2) for i in everyone])
    ask1 = passed(asked, [(i, i // 4 * 4 + (i + 3) % 4) for i in everyone])
    half = leaf_dev // 2
    left, held_w, rows = call(
        early_kernel, "early",
        (
            shape((half, samples, width), jnp.float32), shape(cond_weights.shape, jnp.bfloat16),
            shape((leaf_dev + 8, samples, width), jnp.bfloat16),
        ),
        [SMEM, HBM, HBM], [VMEM] * 3, 14, moved=heavy // 2,
        scratch=[pltpu.SemaphoreType.DMA, pltpu.SemaphoreType.DMA((half // CHUNK,))],
    )(home, placed(latent, HBM), placed(cond_weights, HBM))
    serve8, serve2, serve1 = call(
        functools.partial(serve_kernel, capacity), "serve", (some_rows,) * 3,
        [SMEM] * 3 + [VMEM] * 2 + [ANY], [VMEM] * 3, 4, moved=4 * MIB,
    )(ask1, ask2, ask8, rows, before, left)
    from8 = passed(serve8, [(i, i + 4) for i in everyone if i >= 4 and i + 4 < devices])
    from2 = passed(serve2, [(i, i ^ 2) for i in everyone])
    from1 = passed(serve1, [(i, i // 4 * 4 + (i + 1) % 4) for i in everyone])
    later, held_w, held_f = call(
        late_kernel, "late",
        (
            shape((leaf_dev - half, samples, width), jnp.float32),
            shape(cond_weights.shape, jnp.bfloat16), shape(precision_factor.shape, jnp.bfloat16),
        ),
        [SMEM, VMEM, ANY, VMEM, HBM, HBM], [VMEM] * 3, 14, moved=heavy // 2,
        scratch=[
            pltpu.SemaphoreType.DMA(((leaf_dev - half) // CHUNK,)), pltpu.SemaphoreType.DMA
        ],
        aliases={3: 1},
    )(home, rows, before, held_w, placed(cond_weights, HBM), placed(precision_factor, HBM))
    back, low, out8, out4, out2, out1 = call(
        functools.partial(remote_kernel, capacity), "remote",
        (all_rows, shape((leaf_dev + 8, samples, width), jnp.bfloat16)) + (sent,) * 4,
        [SMEM] * 2 + [VMEM] * 9, [VMEM] * 6, 8, moved=heavy,
        scratch=[VMEM((leaf_dev + 8, samples, width), jnp.float32)],
    )(asked, slots, asked, left, later, before, from2, from8, from1, held_w, held_f)
    returned = [
        passed(x, [(i, i - reach) for i in everyone if i >= reach])
        for reach, x in ((8, out8), (4, out4), (2, out2), (1, out1))
    ]
    (part,) = call(
        home_kernel, "home", (all_rows,), [SMEM] + [VMEM] * 3, [VMEM], 6, moved=heavy,
        scratch=[VMEM((leaf_dev + 8, samples, width), jnp.float32)],
    )(home, back, low, held_w)
    lists = (4, 4 * SLOTS)
    (gradient,) = call(
        functools.partial(add_kernel, capacity, (3, 2, 1, 0)), "add", (all_rows,), [VMEM] * 5,
        [VMEM], 6, moved=4 * MIB,
        scratch=[VMEM(lists, jnp.int32), SMEM(lists, jnp.int32), pltpu.SemaphoreType.DMA],
    )(part, *returned)
    return gradient


def solution(mesh):
    return jax.shard_map(
        per_device,
        mesh=mesh,
        in_specs=(
            P(("groups", "kx"), None, None),
            P(("groups", "kx"), None),
            P(("groups", "kx"), None, None, None),
            P(("groups", "kx"), None, None),
        ),
        out_specs=P(("groups", "kx"), None, None),
        check_vma=False,
    )
```

```python
import functools

import jax
import jax.numpy as jnp
from jax import lax
from jax.experimental import pallas as pl
from jax.experimental.pallas import tpu as pltpu
from jax.sharding import PartitionSpec as P

SLOTS = 32
PART = 16
LEAVES = 40
MIB = 2**20
BY_ROWS = (((1,), (1,)), ((), ()))
VMEM, SMEM, HBM, ANY = pltpu.VMEM, pltpu.SMEM, pltpu.HBM, pl.ANY


def fetched(weights, held, sem, n):
    part = pl.ds(n * PART, PART)
    return pltpu.make_async_copy(weights.at[part], held.at[part], sem)


def index_kernel(
    lists, latent, weights, asked, slots, home, rows, held_w, row_sem, w_sem
):
    fan, leaf_dev = lists.shape
    fetches = (
        pltpu.make_async_copy(latent, rows.at[pl.ds(0, leaf_dev)], row_sem),
        fetched(weights, held_w, w_sem, 0),
    )
    for fetch in fetches:
        fetch.start()
    rows[leaf_dev] = jnp.zeros(latent.shape[1:], latent.dtype)
    me = lax.axis_index("kx")
    behind = me * leaf_dev - lists[...]
    kind = (
        (behind > 0).astype(jnp.int32)
        + (behind > leaf_dev).astype(jnp.int32)
        + (behind > 2 * leaf_dev).astype(jnp.int32)
        + (behind > 4 * leaf_dev).astype(jnp.int32)
    )
    reach = jnp.where(kind == 4, 8, jnp.where(kind == 3, 4, kind))
    row = reach * leaf_dev - behind
    home[...] = jnp.where(kind == 0, row, leaf_dev)

    def grid(shape, dim):
        return lax.broadcasted_iota(jnp.int32, shape, dim)

    def low(x):
        return x.astype(jnp.float32).astype(jnp.bfloat16)

    every = 4 * fan
    mask = jnp.concatenate([(kind == o).astype(jnp.float32) for o in range(1, 5)], axis=0)
    earlier = low(grid((leaf_dev, leaf_dev), 0) < grid((leaf_dev, leaf_dev), 1))
    a, b = grid((every, every), 0), grid((every, every), 1)
    above = (b < a)
    for o in range(1, 4):
        above = above & ((a < o * fan) | (b >= o * fan))
    within = jnp.dot(low(mask), earlier, preferred_element_type=jnp.float32)
    base = jnp.sum(
        jnp.dot(low(above), low(mask), preferred_element_type=jnp.float32), axis=1, keepdims=True
    )
    place = jnp.where(mask > 0.0, within + base, -1.0)
    slot = grid((SLOTS, leaf_dev), 0).astype(jnp.float32)
    leaf = grid((1, leaf_dev), 1).astype(jnp.float32)
    ones = jnp.ones((1, leaf_dev), jnp.float32)
    total = jnp.zeros((8, 4 * SLOTS), jnp.float32)
    for k in range(fan):
        hit = jnp.concatenate(
            [(place[o * fan + k : o * fan + k + 1] == slot).astype(jnp.float32) for o in range(4)],
            axis=0,
        )
        facts = jnp.concatenate(
            [row[k : k + 1].astype(jnp.float32), leaf, k * ones, ones]
            + [jnp.zeros((4, leaf_dev), jnp.float32)], axis=0,
        )
        total = total + lax.dot_general(
            low(facts), low(hit), BY_ROWS, preferred_element_type=jnp.float32
        )
    asked[...] = total[0:1].astype(jnp.int32)
    slots[0:1] = jnp.where(total[3:4] > 0.0, total[1:2], float(leaf_dev)).astype(jnp.int32)
    slots[1:2] = total[2:3].astype(jnp.int32)
    for fetch in fetches:
        fetch.wait()


def beside(xs):
    return jnp.concatenate(xs, axis=1)


def below(xs):
    return jnp.concatenate(xs, axis=0)


def paired(x, y, left, right, by_rows=False):
    samples = x.shape[0]
    if by_rows:
        wide = left.shape[0]
        both = lax.dot_general(
            below([x, y]), below([left, right]), BY_ROWS, preferred_element_type=jnp.float32
        )
    else:
        wide = left.shape[1]
        both = jnp.dot(below([x, y]), beside([left, right]), preferred_element_type=jnp.float32)
    return both[:samples, :wide], both[samples:, wide:]


def local_means(home, rows, held, left, first, leaves):
    fan, width = held.shape[1], held.shape[2]
    for i in leaves:
        mean = jnp.dot(
            beside([rows[home[k, i]] for k in range(fan)]),
            held[i].reshape(fan * width, width), preferred_element_type=jnp.float32,
        )
        left[i - first] = rows[i].astype(jnp.float32) - mean


def early_kernel(home, rows, held_part, weights, left, held_w, w_sem):
    parts = left.shape[0] // PART
    fetches = [fetched(weights, held_w, w_sem.at[n], n + 1) for n in range(parts)]
    for fetch in fetches:
        fetch.start()
    for n in range(parts):
        if n > 0:
            fetches[n - 1].wait()
        held = held_w if n > 0 else held_part
        local_means(home, rows, held, left, 0, range(n * PART, (n + 1) * PART))
    fetches[-1].wait()


def late_kernel(home, rows, before, held_part, weights, factor, left, held_w, held_f, w_sem, f_sem):
    parts, first = left.shape[0] // PART, weights.shape[0] - left.shape[0]
    fetches = [fetched(weights, held_w, w_sem.at[n - 1], first // PART + n) for n in range(1, parts)]
    fetch_factor = pltpu.make_async_copy(factor, held_f, f_sem)
    for fetch in fetches:
        fetch.start()
    fetch_factor.start()
    for n in range(parts):
        if n > 0:
            fetches[n - 1].wait()
        at = first + n * PART
        held = held_w if n > 0 else held_part
        local_means(home, rows, held, left, first, range(at, at + PART))
    fetch_factor.wait()


def serve_kernel(capacity, ask1, ask2, ask8, latent, before, left, out8, out2, out1):
    me = lax.axis_index("kx")
    def pick(o, ask, rows, out):
        for r in range(capacity):
            out[r] = rows[ask[0, o * SLOTS + r]]

    pick(3, ask8, before, out8)
    for o, ask, out, bits in ((1, ask2, out2, 2), (0, ask1, out1, 3)):
        relays = lax.bitwise_and(me, bits) == bits

        @pl.when(relays)
        def _():
            pick(o, ask, before, out)

        @pl.when(jnp.logical_not(relays))
        def _():
            pick(o, ask, latent, out)


def asker(slots, weights, o, r):
    i = slots[0, o * SLOTS + r]
    return i, weights[jnp.minimum(i, weights.shape[0] - 1), slots[1, o * SLOTS + r]]


def remote_terms(capacity, slots, asked_row, low, weights, outs):
    listed = jnp.broadcast_to(asked_row[...].astype(jnp.float32), low.shape[1:])
    for o, out in outs:
        for r in range(0, capacity, 2):
            (i, w), (j, v) = asker(slots, weights, o, r), asker(slots, weights, o, r + 1)
            for at, x in zip((r, r + 1), paired(low[i], low[j], w, v, True)):
                out[at] = x.astype(out.dtype)
        out[capacity] = listed.astype(out.dtype)


def remote_kernel(
    capacity, asked, slots, asked_row, left, later, before, from2, from8, from1,
    weights, factor, back, low, out8, out4, out2, out1, resid,
):
    leaf_dev, half = back.shape[0], left.shape[0]
    resid[pl.ds(0, half)] = left[...]
    resid[pl.ds(half, leaf_dev - half)] = later[...]
    resid[leaf_dev] = jnp.zeros(left.shape[1:], left.dtype)
    low[leaf_dev] = jnp.zeros(left.shape[1:], low.dtype)

    for o, rows in ((2, before), (3, from8), (1, from2), (0, from1)):
        found = []
        for r in range(0, capacity, 2):
            (i, w), (j, v) = asker(slots, weights, o, r), asker(slots, weights, o, r + 1)
            at = (asked[0, o * SLOTS + r], asked[0, o * SLOTS + r + 1]) if o == 2 else (r, r + 1)
            found += zip((i, j), paired(rows[at[0]], rows[at[1]], w, v))
        for i, mean in found:
            resid[i] = resid[i] - mean

    def leaves(c, carry):
        pairs = [c * LEAVES + u for u in range(0, LEAVES, 2)]
        innov = [
            paired(
                resid[i].astype(jnp.bfloat16), resid[i + 1].astype(jnp.bfloat16),
                factor[i], factor[i + 1],
            )
            for i in pairs
        ]
        for i, (x, y) in zip(pairs, innov):
            both = paired(
                x.astype(jnp.bfloat16), y.astype(jnp.bfloat16), factor[i], factor[i + 1], True
            )
            for j, z in zip((i, i + 1), both):
                back[j] = z
                low[j] = z.astype(jnp.bfloat16)
        return carry

    lax.fori_loop(0, leaf_dev // LEAVES, leaves, 0)
    remote_terms(
        capacity, slots, asked_row, low, weights, ((3, out8), (2, out4), (1, out2), (0, out1))
    )


def home_kernel(home, back, low, weights, part, acc):
    leaf_dev = back.shape[0]
    fan, width = weights.shape[1], weights.shape[2]
    acc[pl.ds(0, leaf_dev)] = -back[...]
    acc[leaf_dev] = jnp.zeros(back.shape[1:], back.dtype)

    def some(c, carry):
        found = []
        for u in range(LEAVES):
            i = c * LEAVES + u
            found.append((i, lax.dot_general(
                low[i], weights[i].reshape(fan * width, width), BY_ROWS,
                preferred_element_type=jnp.float32,
            )))
        for i, x in found:
            for k in range(fan):
                j = home[k, i]
                acc[j] = acc[j] + x[:, k * width : (k + 1) * width]
        return carry

    lax.fori_loop(0, leaf_dev // LEAVES, some, 0)
    part[...] = acc[pl.ds(0, leaf_dev)]


def add_kernel(capacity, part, back8, ring, back4, back2, relayed, out, listed, wanted, sem):
    last = lax.bitwise_and(lax.axis_index("kx"), 3) == 3

    def back1(r):
        return jnp.where(last, relayed[r].astype(jnp.float32), ring[r].astype(jnp.float32))

    returned = [(3, back8), (2, back4), (1, back2)]
    returned = [(o, lambda r, x=x: x[r].astype(jnp.float32)) for o, x in returned] + [(0, back1)]
    for o, row in returned:
        listed[o : o + 1] = row(capacity)[0:1].astype(jnp.int32)
    fetch = pltpu.make_async_copy(listed, wanted, sem)
    fetch.start()
    out[...] = part[...]
    fetch.wait()
    for o, row in returned:
        for r in range(capacity):
            j = wanted[o, o * SLOTS + r]
            out[j] = out[j] + row(r)


def call(body, name, out_shape, ins, outs, limit, flops=0, moved=0, scratch=(), aliases={}):
    spec = lambda space: pl.BlockSpec(memory_space=space)
    return pl.pallas_call(
        body,
        out_shape=out_shape,
        in_specs=[spec(space) for space in ins],
        out_specs=tuple(spec(space) for space in outs),
        scratch_shapes=scratch,
        input_output_aliases=aliases,
        compiler_params=pltpu.CompilerParams(vmem_limit_bytes=limit * MIB),
        cost_estimate=pl.CostEstimate(flops=flops, bytes_accessed=moved, transcendentals=0),
        name=name,
    )


def placed(x, space):
    return pltpu.with_memory_space_constraint(x, space)


def per_device(latent, cond_lists, cond_weights, precision_factor):
    devices = lax.axis_size("kx")
    leaf_dev, samples, width = latent.shape
    fan = cond_lists.shape[1]
    capacity = fan * leaf_dev // 8
    everyone = range(devices)
    shape = jax.ShapeDtypeStruct
    some_rows = shape((capacity, samples, width), jnp.bfloat16)
    sent = shape((capacity + 1, samples, width), jnp.bfloat16)
    all_rows = shape(latent.shape, jnp.float32)
    one_list = shape((1, 4 * SLOTS), jnp.int32)
    heavy = cond_weights.size * 2

    def passed(x, route):
        return lax.ppermute(x, "kx", route)

    before = passed(latent, [(i, i + 4) for i in everyone if i + 4 < devices])
    held = shape(cond_weights.shape, jnp.bfloat16)
    weights = placed(cond_weights, HBM)
    dma = pltpu.SemaphoreType.DMA
    asked, slots, home, rows, held_w = call(
        index_kernel, "index",
        (
            one_list, shape((2, 4 * SLOTS), jnp.int32), shape((fan, leaf_dev), jnp.int32),
            shape((leaf_dev + 8, samples, width), jnp.bfloat16), held,
        ),
        [VMEM, HBM, HBM], [VMEM] * 5, 14, moved=2 * MIB, scratch=[dma, dma],
    )(placed(cond_lists.T, HBM), placed(latent, HBM), weights)
    ask8 = passed(asked, [(i, i - 4) for i in everyone if i >= 4])
    ask2 = passed(asked, [(i, i ^ 2) for i in everyone])
    ask1 = passed(asked, [(i, i // 4 * 4 + (i + 3) % 4) for i in everyone])
    most = -(-leaf_dev // (2 * PART)) * PART
    left, held_w = call(
        early_kernel, "early", (shape((most, samples, width), jnp.float32), held),
        [SMEM, VMEM, VMEM, HBM], [VMEM] * 2, 14, moved=heavy // 2,
        scratch=[dma((most // PART,))], aliases={2: 1},
    )(home, rows, held_w, weights)
    serve8, serve2, serve1 = call(
        functools.partial(serve_kernel, capacity), "serve", (some_rows,) * 3,
        [SMEM] * 3 + [VMEM] * 2 + [ANY], [VMEM] * 3, 4, moved=4 * MIB,
    )(ask1, ask2, ask8, rows, before, left)
    from8 = passed(serve8, [(i, i + 4) for i in everyone if i >= 4 and i + 4 < devices])
    from2 = passed(serve2, [(i, i ^ 2) for i in everyone])
    from1 = passed(serve1, [(i, i // 4 * 4 + (i + 1) % 4) for i in everyone])
    later, held_w, held_f = call(
        late_kernel, "late",
        (
            shape((leaf_dev - most, samples, width), jnp.float32), held,
            shape(precision_factor.shape, jnp.bfloat16),
        ),
        [SMEM, VMEM, ANY, VMEM, HBM, HBM], [VMEM] * 3, 14, moved=heavy // 2,
        scratch=[dma(((leaf_dev - most) // PART - 1,)), dma], aliases={3: 1},
    )(home, rows, before, held_w, weights, placed(precision_factor, HBM))
    back, low, out8, out4, out2, out1 = call(
        functools.partial(remote_kernel, capacity), "remote",
        (all_rows, shape((leaf_dev + 8, samples, width), jnp.bfloat16)) + (sent,) * 4,
        [SMEM] * 2 + [VMEM] * 9, [VMEM] * 6, 8, moved=heavy,
        scratch=[VMEM((leaf_dev + 8, samples, width), jnp.float32)],
    )(asked, slots, asked, left, later, before, from2, from8, from1, held_w, held_f)
    def back_by(x, reach):
        return passed(x, [(i, i - reach) for i in everyone if i >= reach])

    ring = passed(out1, [(i, i // 4 * 4 + (i + 3) % 4) for i in everyone])
    back8, back4, back2 = back_by(out8, 8), back_by(out4, 4), back_by(out2, 2)
    relayed = passed(ring, [(i, i - 4) for i in everyone if i >= 4 and i % 4 == 3])
    (part,) = call(
        home_kernel, "home", (all_rows,), [SMEM] + [VMEM] * 3, [VMEM], 6, moved=heavy,
        scratch=[VMEM((leaf_dev + 8, samples, width), jnp.float32)],
    )(home, back, low, held_w)
    lists = (4, 4 * SLOTS)
    (gradient,) = call(
        functools.partial(add_kernel, capacity), "add", (all_rows,), [VMEM] * 6,
        [VMEM], 6, moved=4 * MIB, scratch=[VMEM(lists, jnp.int32), SMEM(lists, jnp.int32), dma],
    )(part, back8, ring, back4, back2, relayed)
    return gradient


def solution(mesh):
    return jax.shard_map(
        per_device,
        mesh=mesh,
        in_specs=(
            P(("groups", "kx"), None, None),
            P(("groups", "kx"), None),
            P(("groups", "kx"), None, None, None),
            P(("groups", "kx"), None, None),
        ),
        out_specs=P(("groups", "kx"), None, None),
        check_vma=False,
    )
```

```python
import functools

import jax
import jax.numpy as jnp
from jax import lax
from jax.experimental import pallas as pl
from jax.experimental.pallas import tpu as pltpu
from jax.sharding import PartitionSpec as P

SLOTS = 32
PART = 16
LEAVES = 40
MIB = 2**20
BY_ROWS = (((1,), (1,)), ((), ()))
VMEM, SMEM, HBM, ANY = pltpu.VMEM, pltpu.SMEM, pltpu.HBM, pl.ANY


def index_kernel(
    lists, latent, asked, slots, home, rows, row_sem
):
    fan, leaf_dev = lists.shape
    fetch = pltpu.make_async_copy(latent, rows.at[pl.ds(0, leaf_dev)], row_sem)
    fetch.start()
    rows[leaf_dev] = jnp.zeros(latent.shape[1:], latent.dtype)
    me = lax.axis_index("kx")
    behind = me * leaf_dev - lists[...]
    kind = (
        (behind > 0).astype(jnp.int32)
        + (behind > leaf_dev).astype(jnp.int32)
        + (behind > 2 * leaf_dev).astype(jnp.int32)
        + (behind > 4 * leaf_dev).astype(jnp.int32)
    )
    reach = jnp.where(kind == 4, 8, jnp.where(kind == 3, 4, kind))
    row = reach * leaf_dev - behind
    home[...] = jnp.where(kind == 0, row, leaf_dev)

    def grid(shape, dim):
        return lax.broadcasted_iota(jnp.int32, shape, dim)

    def low(x):
        return x.astype(jnp.float32).astype(jnp.bfloat16)

    every = 4 * fan
    mask = jnp.concatenate([(kind == o).astype(jnp.float32) for o in range(1, 5)], axis=0)
    earlier = low(grid((leaf_dev, leaf_dev), 0) < grid((leaf_dev, leaf_dev), 1))
    a, b = grid((every, every), 0), grid((every, every), 1)
    above = (b < a)
    for o in range(1, 4):
        above = above & ((a < o * fan) | (b >= o * fan))
    within = jnp.dot(low(mask), earlier, preferred_element_type=jnp.float32)
    base = jnp.sum(
        jnp.dot(low(above), low(mask), preferred_element_type=jnp.float32), axis=1, keepdims=True
    )
    place = jnp.where(mask > 0.0, within + base, -1.0)
    slot = grid((SLOTS, leaf_dev), 0).astype(jnp.float32)
    leaf = grid((1, leaf_dev), 1).astype(jnp.float32)
    ones = jnp.ones((1, leaf_dev), jnp.float32)
    total = jnp.zeros((8, 4 * SLOTS), jnp.float32)
    for k in range(fan):
        hit = jnp.concatenate(
            [(place[o * fan + k : o * fan + k + 1] == slot).astype(jnp.float32) for o in range(4)],
            axis=0,
        )
        facts = jnp.concatenate(
            [row[k : k + 1].astype(jnp.float32), leaf, k * ones, ones]
            + [jnp.zeros((4, leaf_dev), jnp.float32)], axis=0,
        )
        total = total + lax.dot_general(
            low(facts), low(hit), BY_ROWS, preferred_element_type=jnp.float32
        )
    asked[...] = total[0:1].astype(jnp.int32)
    slots[0:1] = jnp.where(total[3:4] > 0.0, total[1:2], float(leaf_dev)).astype(jnp.int32)
    slots[1:2] = total[2:3].astype(jnp.int32)
    fetch.wait()


def beside(xs):
    return jnp.concatenate(xs, axis=1)


def below(xs):
    return jnp.concatenate(xs, axis=0)


def paired(x, y, left, right, by_rows=False):
    samples = x.shape[0]
    if by_rows:
        wide = left.shape[0]
        both = lax.dot_general(
            below([x, y]), below([left, right]), BY_ROWS, preferred_element_type=jnp.float32
        )
    else:
        wide = left.shape[1]
        both = jnp.dot(below([x, y]), beside([left, right]), preferred_element_type=jnp.float32)
    return both[:samples, :wide], both[samples:, wide:]


def local_means(home, rows, held, left, first, leaves):
    fan, width = held.shape[1], held.shape[2]
    for i in leaves:
        mean = jnp.dot(
            beside([rows[home[k, i]] for k in range(fan)]),
            held[i].reshape(fan * width, width), preferred_element_type=jnp.float32,
        )
        left[i - first] = rows[i].astype(jnp.float32) - mean


def early_kernel(home, rows, weights, left, held, sem):
    parts = [pl.ds(at, PART) for at in range(0, left.shape[0], PART)]
    fetches = [
        pltpu.make_async_copy(weights.at[p], held.at[p], sem.at[n]) for n, p in enumerate(parts)
    ]
    for fetch in fetches:
        fetch.start()
    for n, fetch in enumerate(fetches):
        fetch.wait()
        local_means(home, rows, held, left, 0, range(n * PART, (n + 1) * PART))


def late_kernel(home, rows, before, weights, left):
    leaf_dev = weights.shape[0]
    first = leaf_dev - left.shape[0]
    local_means(home, rows, weights, left, first, range(first, leaf_dev))


def serve_kernel(capacity, ask1, ask2, ask8, latent, before, left, out8, out2, out1):
    me = lax.axis_index("kx")
    def pick(o, ask, rows, out):
        for r in range(capacity):
            out[r] = rows[ask[0, o * SLOTS + r]]

    pick(3, ask8, before, out8)
    for o, ask, out, bits in ((1, ask2, out2, 2), (0, ask1, out1, 3)):
        relays = lax.bitwise_and(me, bits) == bits

        @pl.when(relays)
        def _():
            pick(o, ask, before, out)

        @pl.when(jnp.logical_not(relays))
        def _():
            pick(o, ask, latent, out)


def asker(slots, weights, o, r):
    i = slots[0, o * SLOTS + r]
    return i, weights[jnp.minimum(i, weights.shape[0] - 1), slots[1, o * SLOTS + r]]


def remote_terms(capacity, slots, asked_row, low, weights, outs):
    listed = jnp.broadcast_to(asked_row[...].astype(jnp.float32), low.shape[1:])
    for o, out in outs:
        for r in range(0, capacity, 2):
            (i, w), (j, v) = asker(slots, weights, o, r), asker(slots, weights, o, r + 1)
            for at, x in zip((r, r + 1), paired(low[i], low[j], w, v, True)):
                out[at] = x.astype(out.dtype)
        out[capacity] = listed.astype(out.dtype)


def remote_kernel(
    capacity, asked, slots, asked_row, left, later, before, from2, from8, from1,
    weights, factor, back, low, out8, out4, out2, out1, resid,
):
    leaf_dev, half = back.shape[0], left.shape[0]
    resid[pl.ds(0, half)] = left[...]
    resid[pl.ds(half, leaf_dev - half)] = later[...]
    resid[leaf_dev] = jnp.zeros(left.shape[1:], left.dtype)
    low[leaf_dev] = jnp.zeros(left.shape[1:], low.dtype)

    for o, rows in ((2, before), (3, from8), (1, from2), (0, from1)):
        found = []
        for r in range(0, capacity, 2):
            (i, w), (j, v) = asker(slots, weights, o, r), asker(slots, weights, o, r + 1)
            at = (asked[0, o * SLOTS + r], asked[0, o * SLOTS + r + 1]) if o == 2 else (r, r + 1)
            found += zip((i, j), paired(rows[at[0]], rows[at[1]], w, v))
        for i, mean in found:
            resid[i] = resid[i] - mean

    def leaves(c, carry):
        pairs = [c * LEAVES + u for u in range(0, LEAVES, 2)]
        innov = [
            paired(
                resid[i].astype(jnp.bfloat16), resid[i + 1].astype(jnp.bfloat16),
                factor[i], factor[i + 1],
            )
            for i in pairs
        ]
        for i, (x, y) in zip(pairs, innov):
            both = paired(
                x.astype(jnp.bfloat16), y.astype(jnp.bfloat16), factor[i], factor[i + 1], True
            )
            for j, z in zip((i, i + 1), both):
                back[j] = z
                low[j] = z.astype(jnp.bfloat16)
        return carry

    lax.fori_loop(0, leaf_dev // LEAVES, leaves, 0)
    remote_terms(
        capacity, slots, asked_row, low, weights, ((3, out8), (2, out4), (1, out2), (0, out1))
    )


def home_kernel(home, back, low, weights, part, acc):
    leaf_dev = back.shape[0]
    fan, width = weights.shape[1], weights.shape[2]
    acc[pl.ds(0, leaf_dev)] = -back[...]
    acc[leaf_dev] = jnp.zeros(back.shape[1:], back.dtype)

    def some(c, carry):
        found = []
        for u in range(LEAVES):
            i = c * LEAVES + u
            found.append((i, lax.dot_general(
                low[i], weights[i].reshape(fan * width, width), BY_ROWS,
                preferred_element_type=jnp.float32,
            )))
        for i, x in found:
            for k in range(fan):
                j = home[k, i]
                acc[j] = acc[j] + x[:, k * width : (k + 1) * width]
        return carry

    lax.fori_loop(0, leaf_dev // LEAVES, some, 0)
    part[...] = acc[pl.ds(0, leaf_dev)]


def add_kernel(capacity, part, back8, ring, back4, back2, relayed, out, listed, wanted, sem):
    last = lax.bitwise_and(lax.axis_index("kx"), 3) == 3

    def back1(r):
        return jnp.where(last, relayed[r].astype(jnp.float32), ring[r].astype(jnp.float32))

    returned = [(3, back8), (2, back4), (1, back2)]
    returned = [(o, lambda r, x=x: x[r].astype(jnp.float32)) for o, x in returned] + [(0, back1)]
    for o, row in returned:
        listed[o : o + 1] = row(capacity)[0:1].astype(jnp.int32)
    fetch = pltpu.make_async_copy(listed, wanted, sem)
    fetch.start()
    out[...] = part[...]
    fetch.wait()
    for o, row in returned:
        for r in range(capacity):
            j = wanted[o, o * SLOTS + r]
            out[j] = out[j] + row(r)


def call(body, name, out_shape, ins, outs, limit, flops=0, moved=0, scratch=(), aliases={}):
    spec = lambda space: pl.BlockSpec(memory_space=space)
    return pl.pallas_call(
        body,
        out_shape=out_shape,
        in_specs=[spec(space) for space in ins],
        out_specs=tuple(spec(space) for space in outs),
        scratch_shapes=scratch,
        input_output_aliases=aliases,
        compiler_params=pltpu.CompilerParams(vmem_limit_bytes=limit * MIB),
        cost_estimate=pl.CostEstimate(flops=flops, bytes_accessed=moved, transcendentals=0),
        name=name,
    )


def placed(x, space):
    return pltpu.with_memory_space_constraint(x, space)


def per_device(latent, cond_lists, cond_weights, precision_factor):
    devices = lax.axis_size("kx")
    leaf_dev, samples, width = latent.shape
    fan = cond_lists.shape[1]
    capacity = fan * leaf_dev // 8
    everyone = range(devices)
    shape = jax.ShapeDtypeStruct
    some_rows = shape((capacity, samples, width), jnp.bfloat16)
    sent = shape((capacity + 1, samples, width), jnp.bfloat16)
    all_rows = shape(latent.shape, jnp.float32)
    one_list = shape((1, 4 * SLOTS), jnp.int32)
    heavy = cond_weights.size * 2

    def passed(x, route):
        return lax.ppermute(x, "kx", route)

    before = passed(latent, [(i, i + 4) for i in everyone if i + 4 < devices])
    weights, factor = placed(cond_weights, VMEM), placed(precision_factor, VMEM)
    dma = pltpu.SemaphoreType.DMA
    asked, slots, home, rows = call(
        index_kernel, "index",
        (
            one_list, shape((2, 4 * SLOTS), jnp.int32), shape((fan, leaf_dev), jnp.int32),
            shape((leaf_dev + 8, samples, width), jnp.bfloat16),
        ),
        [VMEM, HBM], [VMEM] * 4, 4, moved=2 * MIB, scratch=[dma],
    )(placed(cond_lists.T, HBM), placed(latent, HBM))
    ask8 = passed(asked, [(i, i - 4) for i in everyone if i >= 4])
    ask2 = passed(asked, [(i, i ^ 2) for i in everyone])
    ask1 = passed(asked, [(i, i // 4 * 4 + (i + 3) % 4) for i in everyone])
    most = 2 * leaf_dev // 5 // PART * PART
    (left,) = call(
        early_kernel, "early", (shape((most, samples, width), jnp.float32),),
        [SMEM, VMEM, HBM], [VMEM], 6, moved=heavy // 2,
        scratch=[VMEM((most,) + cond_weights.shape[1:], jnp.bfloat16), dma((most // PART,))],
    )(home, rows, placed(cond_weights, HBM))
    serve8, serve2, serve1 = call(
        functools.partial(serve_kernel, capacity), "serve", (some_rows,) * 3,
        [SMEM] * 3 + [VMEM] * 2 + [ANY], [VMEM] * 3, 4, moved=4 * MIB,
    )(ask1, ask2, ask8, rows, before, left)
    from8 = passed(serve8, [(i, i + 4) for i in everyone if i >= 4 and i + 4 < devices])
    from2 = passed(serve2, [(i, i ^ 2) for i in everyone])
    from1 = passed(serve1, [(i, i // 4 * 4 + (i + 1) % 4) for i in everyone])
    (later,) = call(
        late_kernel, "late", (shape((leaf_dev - most, samples, width), jnp.float32),),
        [SMEM, VMEM, ANY, VMEM], [VMEM], 4, moved=heavy // 2,
    )(home, rows, before, weights)
    back, low, out8, out4, out2, out1 = call(
        functools.partial(remote_kernel, capacity), "remote",
        (all_rows, shape((leaf_dev + 8, samples, width), jnp.bfloat16)) + (sent,) * 4,
        [SMEM] * 2 + [VMEM] * 9, [VMEM] * 6, 8, moved=heavy,
        scratch=[VMEM((leaf_dev + 8, samples, width), jnp.float32)],
    )(asked, slots, asked, left, later, before, from2, from8, from1, weights, factor)
    def back_by(x, reach):
        return passed(x, [(i, i - reach) for i in everyone if i >= reach])

    ring = passed(out1, [(i, i // 4 * 4 + (i + 3) % 4) for i in everyone])
    back8, back4, back2 = back_by(out8, 8), back_by(out4, 4), back_by(out2, 2)
    relayed = passed(ring, [(i, i - 4) for i in everyone if i >= 4 and i % 4 == 3])
    (part,) = call(
        home_kernel, "home", (all_rows,), [SMEM] + [VMEM] * 3, [VMEM], 6, moved=heavy,
        scratch=[VMEM((leaf_dev + 8, samples, width), jnp.float32)],
    )(home, back, low, weights)
    lists = (4, 4 * SLOTS)
    (gradient,) = call(
        functools.partial(add_kernel, capacity), "add", (all_rows,), [VMEM] * 6,
        [VMEM], 6, moved=4 * MIB, scratch=[VMEM(lists, jnp.int32), SMEM(lists, jnp.int32), dma],
    )(part, back8, ring, back4, back2, relayed)
    return gradient


def solution(mesh):
    return jax.shard_map(
        per_device,
        mesh=mesh,
        in_specs=(
            P(("groups", "kx"), None, None),
            P(("groups", "kx"), None),
            P(("groups", "kx"), None, None, None),
            P(("groups", "kx"), None, None),
        ),
        out_specs=P(("groups", "kx"), None, None),
        check_vma=False,
    )
```

```python
import functools

import jax
import jax.numpy as jnp
from jax import lax
from jax.experimental import pallas as pl
from jax.experimental.pallas import tpu as pltpu
from jax.sharding import PartitionSpec as P

SLOTS = 32
LEAVES = 40
MIB = 2**20
BY_ROWS = (((1,), (1,)), ((), ()))
VMEM, SMEM, HBM, ANY = pltpu.VMEM, pltpu.SMEM, pltpu.HBM, pl.ANY


def index_kernel(lists, latent, weights, asked, slots, home):
    fan, leaf_dev = lists.shape
    me = lax.axis_index("kx")
    behind = me * leaf_dev - lists[...]
    kind = (
        (behind > 0).astype(jnp.int32)
        + (behind > leaf_dev).astype(jnp.int32)
        + (behind > 2 * leaf_dev).astype(jnp.int32)
        + (behind > 4 * leaf_dev).astype(jnp.int32)
    )
    reach = jnp.where(kind == 4, 8, jnp.where(kind == 3, 4, kind))
    row = reach * leaf_dev - behind
    home[...] = jnp.where(kind == 0, row, leaf_dev)

    def grid(shape, dim):
        return lax.broadcasted_iota(jnp.int32, shape, dim)

    def low(x):
        return x.astype(jnp.float32).astype(jnp.bfloat16)

    every = 4 * fan
    mask = jnp.concatenate([(kind == o).astype(jnp.float32) for o in range(1, 5)], axis=0)
    earlier = low(grid((leaf_dev, leaf_dev), 0) < grid((leaf_dev, leaf_dev), 1))
    a, b = grid((every, every), 0), grid((every, every), 1)
    above = (b < a)
    for o in range(1, 4):
        above = above & ((a < o * fan) | (b >= o * fan))
    within = jnp.dot(low(mask), earlier, preferred_element_type=jnp.float32)
    base = jnp.sum(
        jnp.dot(low(above), low(mask), preferred_element_type=jnp.float32), axis=1, keepdims=True
    )
    place = jnp.where(mask > 0.0, within + base, -1.0)
    slot = grid((SLOTS, leaf_dev), 0).astype(jnp.float32)
    leaf = grid((1, leaf_dev), 1).astype(jnp.float32)
    ones = jnp.ones((1, leaf_dev), jnp.float32)
    total = jnp.zeros((8, 4 * SLOTS), jnp.float32)
    for k in range(fan):
        hit = jnp.concatenate(
            [(place[o * fan + k : o * fan + k + 1] == slot).astype(jnp.float32) for o in range(4)],
            axis=0,
        )
        facts = jnp.concatenate(
            [row[k : k + 1].astype(jnp.float32), leaf, k * ones, ones]
            + [jnp.zeros((4, leaf_dev), jnp.float32)], axis=0,
        )
        total = total + lax.dot_general(
            low(facts), low(hit), BY_ROWS, preferred_element_type=jnp.float32
        )
    asked[...] = total[0:1].astype(jnp.int32)
    slots[0:1] = jnp.where(total[3:4] > 0.0, total[1:2], float(leaf_dev)).astype(jnp.int32)
    slots[1:2] = total[2:3].astype(jnp.int32)


def beside(xs):
    return jnp.concatenate(xs, axis=1)


def below(xs):
    return jnp.concatenate(xs, axis=0)


def paired(x, y, left, right, by_rows=False):
    samples = x.shape[0]
    if by_rows:
        wide = left.shape[0]
        both = lax.dot_general(
            below([x, y]), below([left, right]), BY_ROWS, preferred_element_type=jnp.float32
        )
    else:
        wide = left.shape[1]
        both = jnp.dot(below([x, y]), beside([left, right]), preferred_element_type=jnp.float32)
    return both[:samples, :wide], both[samples:, wide:]


def local_kernel(home, latent, before, weights, left, rows):
    leaf_dev, fan, width = latent.shape[0], weights.shape[1], weights.shape[2]
    rows[pl.ds(0, leaf_dev)] = latent[...]
    rows[leaf_dev] = jnp.zeros(latent.shape[1:], latent.dtype)

    def some(c, carry):
        for u in range(LEAVES):
            i = c * LEAVES + u
            mean = jnp.dot(
                beside([rows[home[k, i]] for k in range(fan)]),
                weights[i].reshape(fan * width, width), preferred_element_type=jnp.float32,
            )
            left[i] = latent[i].astype(jnp.float32) - mean
        return carry

    lax.fori_loop(0, leaf_dev // LEAVES, some, 0)


def serve_kernel(capacity, ask1, ask2, ask8, latent, before, out8, out2, out1):
    me = lax.axis_index("kx")
    def pick(o, ask, rows, out):
        for r in range(capacity):
            out[r] = rows[ask[0, o * SLOTS + r]]

    pick(3, ask8, before, out8)
    for o, ask, out, bits in ((1, ask2, out2, 2), (0, ask1, out1, 3)):
        relays = lax.bitwise_and(me, bits) == bits

        @pl.when(relays)
        def _():
            pick(o, ask, before, out)

        @pl.when(jnp.logical_not(relays))
        def _():
            pick(o, ask, latent, out)


def asker(slots, weights, o, r):
    i = slots[0, o * SLOTS + r]
    return i, weights[jnp.minimum(i, weights.shape[0] - 1), slots[1, o * SLOTS + r]]


def remote_terms(capacity, slots, asked_row, low, weights, outs):
    listed = jnp.broadcast_to(asked_row[...].astype(jnp.float32), low.shape[1:])
    for o, out in outs:
        for r in range(0, capacity, 2):
            (i, w), (j, v) = asker(slots, weights, o, r), asker(slots, weights, o, r + 1)
            for at, x in zip((r, r + 1), paired(low[i], low[j], w, v, True)):
                out[at] = x.astype(out.dtype)
        out[capacity] = listed.astype(out.dtype)


def remote_kernel(
    capacity, asked, slots, asked_row, left, before, from2, from8, from1,
    weights, factor, back, low, out8, out4, out2, out1, resid,
):
    leaf_dev = back.shape[0]
    resid[pl.ds(0, leaf_dev)] = left[...]
    resid[leaf_dev] = jnp.zeros(left.shape[1:], left.dtype)
    low[leaf_dev] = jnp.zeros(left.shape[1:], low.dtype)

    for o, rows in ((2, before), (3, from8), (1, from2), (0, from1)):
        found = []
        for r in range(0, capacity, 2):
            (i, w), (j, v) = asker(slots, weights, o, r), asker(slots, weights, o, r + 1)
            at = (asked[0, o * SLOTS + r], asked[0, o * SLOTS + r + 1]) if o == 2 else (r, r + 1)
            found += zip((i, j), paired(rows[at[0]], rows[at[1]], w, v))
        for i, mean in found:
            resid[i] = resid[i] - mean

    def leaves(c, carry):
        pairs = [c * LEAVES + u for u in range(0, LEAVES, 2)]
        innov = [
            paired(
                resid[i].astype(jnp.bfloat16), resid[i + 1].astype(jnp.bfloat16),
                factor[i], factor[i + 1],
            )
            for i in pairs
        ]
        for i, (x, y) in zip(pairs, innov):
            both = paired(
                x.astype(jnp.bfloat16), y.astype(jnp.bfloat16), factor[i], factor[i + 1], True
            )
            for j, z in zip((i, i + 1), both):
                back[j] = z
                low[j] = z.astype(jnp.bfloat16)
        return carry

    lax.fori_loop(0, leaf_dev // LEAVES, leaves, 0)
    remote_terms(
        capacity, slots, asked_row, low, weights, ((3, out8), (2, out4), (1, out2), (0, out1))
    )


def home_kernel(home, back, low, weights, part, acc):
    leaf_dev = back.shape[0]
    fan, width = weights.shape[1], weights.shape[2]
    acc[pl.ds(0, leaf_dev)] = -back[...]
    acc[leaf_dev] = jnp.zeros(back.shape[1:], back.dtype)

    def some(c, carry):
        found = []
        for u in range(LEAVES):
            i = c * LEAVES + u
            found.append((i, lax.dot_general(
                low[i], weights[i].reshape(fan * width, width), BY_ROWS,
                preferred_element_type=jnp.float32,
            )))
        for i, x in found:
            for k in range(fan):
                j = home[k, i]
                acc[j] = acc[j] + x[:, k * width : (k + 1) * width]
        return carry

    lax.fori_loop(0, leaf_dev // LEAVES, some, 0)
    part[...] = acc[pl.ds(0, leaf_dev)]


def add_kernel(capacity, part, back8, ring, back4, back2, relayed, out, listed, wanted, sem):
    last = lax.bitwise_and(lax.axis_index("kx"), 3) == 3

    def back1(r):
        return jnp.where(last, relayed[r].astype(jnp.float32), ring[r].astype(jnp.float32))

    returned = [(3, back8), (2, back4), (1, back2)]
    returned = [(o, lambda r, x=x: x[r].astype(jnp.float32)) for o, x in returned] + [(0, back1)]
    for o, row in returned:
        listed[o : o + 1] = row(capacity)[0:1].astype(jnp.int32)
    fetch = pltpu.make_async_copy(listed, wanted, sem)
    fetch.start()
    out[...] = part[...]
    fetch.wait()
    for o, row in returned:
        for r in range(capacity):
            j = wanted[o, o * SLOTS + r]
            out[j] = out[j] + row(r)


def call(body, name, out_shape, ins, outs, limit, flops=0, moved=0, scratch=(), aliases={}):
    spec = lambda space: pl.BlockSpec(memory_space=space)
    return pl.pallas_call(
        body,
        out_shape=out_shape,
        in_specs=[spec(space) for space in ins],
        out_specs=tuple(spec(space) for space in outs),
        scratch_shapes=scratch,
        input_output_aliases=aliases,
        compiler_params=pltpu.CompilerParams(vmem_limit_bytes=limit * MIB),
        cost_estimate=pl.CostEstimate(flops=flops, bytes_accessed=moved, transcendentals=0),
        name=name,
    )


def placed(x, space):
    return pltpu.with_memory_space_constraint(x, space)


def per_device(latent, cond_lists, cond_weights, precision_factor):
    devices = lax.axis_size("kx")
    leaf_dev, samples, width = latent.shape
    fan = cond_lists.shape[1]
    capacity = fan * leaf_dev // 8
    everyone = range(devices)
    shape = jax.ShapeDtypeStruct
    some_rows = shape((capacity, samples, width), jnp.bfloat16)
    sent = shape((capacity + 1, samples, width), jnp.bfloat16)
    all_rows = shape(latent.shape, jnp.float32)
    one_list = shape((1, 4 * SLOTS), jnp.int32)
    heavy = cond_weights.size * 2

    def passed(x, route):
        return lax.ppermute(x, "kx", route)

    before = passed(latent, [(i, i + 4) for i in everyone if i + 4 < devices])
    weights, factor = placed(cond_weights, VMEM), placed(precision_factor, VMEM)
    held_l = placed(latent, VMEM)
    asked, slots, home = call(
        index_kernel, "index",
        (one_list, shape((2, 4 * SLOTS), jnp.int32), shape((fan, leaf_dev), jnp.int32)),
        [VMEM, HBM, HBM], [VMEM] * 3, 4, moved=2 * MIB,
    )(placed(cond_lists.T, HBM), placed(latent, HBM), placed(cond_weights, HBM))
    ask8 = passed(asked, [(i, i - 4) for i in everyone if i >= 4])
    ask2 = passed(asked, [(i, i ^ 2) for i in everyone])
    ask1 = passed(asked, [(i, i // 4 * 4 + (i + 3) % 4) for i in everyone])
    serve8, serve2, serve1 = call(
        functools.partial(serve_kernel, capacity), "serve", (some_rows,) * 3,
        [SMEM] * 3 + [VMEM] * 2, [VMEM] * 3, 4, moved=4 * MIB,
    )(ask1, ask2, ask8, held_l, before)
    from8 = passed(serve8, [(i, i + 4) for i in everyone if i >= 4 and i + 4 < devices])
    from2 = passed(serve2, [(i, i ^ 2) for i in everyone])
    from1 = passed(serve1, [(i, i // 4 * 4 + (i + 1) % 4) for i in everyone])
    (left,) = call(
        local_kernel, "local", (all_rows,), [SMEM, VMEM, ANY, VMEM], [VMEM], 6, moved=heavy,
        scratch=[VMEM((leaf_dev + 8, samples, width), jnp.bfloat16)],
    )(home, held_l, before, weights)
    back, low, out8, out4, out2, out1 = call(
        functools.partial(remote_kernel, capacity), "remote",
        (all_rows, shape((leaf_dev + 8, samples, width), jnp.bfloat16)) + (sent,) * 4,
        [SMEM] * 2 + [VMEM] * 8, [VMEM] * 6, 8, moved=heavy,
        scratch=[VMEM((leaf_dev + 8, samples, width), jnp.float32)],
    )(asked, slots, asked, left, before, from2, from8, from1, weights, factor)
    def back_by(x, reach):
        return passed(x, [(i, i - reach) for i in everyone if i >= reach])

    ring = passed(out1, [(i, i // 4 * 4 + (i + 3) % 4) for i in everyone])
    back8, back4, back2 = back_by(out8, 8), back_by(out4, 4), back_by(out2, 2)
    relayed = passed(ring, [(i, i - 4) for i in everyone if i >= 4 and i % 4 == 3])
    (part,) = call(
        home_kernel, "home", (all_rows,), [SMEM] + [VMEM] * 3, [VMEM], 6, moved=heavy,
        scratch=[VMEM((leaf_dev + 8, samples, width), jnp.float32)],
    )(home, back, low, weights)
    lists = (4, 4 * SLOTS)
    (gradient,) = call(
        functools.partial(add_kernel, capacity), "add", (all_rows,), [VMEM] * 6,
        [VMEM], 6, moved=4 * MIB, scratch=[VMEM(lists, jnp.int32), SMEM(lists, jnp.int32), pltpu.SemaphoreType.DMA],
    )(part, back8, ring, back4, back2, relayed)
    return gradient


def solution(mesh):
    return jax.shard_map(
        per_device,
        mesh=mesh,
        in_specs=(
            P(("groups", "kx"), None, None),
            P(("groups", "kx"), None),
            P(("groups", "kx"), None, None, None),
            P(("groups", "kx"), None, None),
        ),
        out_specs=P(("groups", "kx"), None, None),
        check_vma=False,
    )
```

```python
import functools

import jax
import jax.numpy as jnp
from jax import lax
from jax.experimental import pallas as pl
from jax.experimental.pallas import tpu as pltpu
from jax.sharding import PartitionSpec as P

SLOTS = 32
LEAVES = 80
MIB = 2**20
BY_ROWS = (((1,), (1,)), ((), ()))
VMEM, SMEM, HBM, ANY = pltpu.VMEM, pltpu.SMEM, pltpu.HBM, pl.ANY


def index_kernel(lists, latent, weights, asked, slots, home):
    fan, leaf_dev = lists.shape
    me = lax.axis_index("kx")
    behind = me * leaf_dev - lists[...]
    kind = (
        (behind > 0).astype(jnp.int32)
        + (behind > leaf_dev).astype(jnp.int32)
        + (behind > 2 * leaf_dev).astype(jnp.int32)
        + (behind > 4 * leaf_dev).astype(jnp.int32)
    )
    reach = jnp.where(kind == 4, 8, jnp.where(kind == 3, 4, kind))
    row = reach * leaf_dev - behind
    home[...] = jnp.where(kind == 0, row, leaf_dev)

    def grid(shape, dim):
        return lax.broadcasted_iota(jnp.int32, shape, dim)

    def low(x):
        return x.astype(jnp.float32).astype(jnp.bfloat16)

    every = 4 * fan
    mask = jnp.concatenate([(kind == o).astype(jnp.float32) for o in range(1, 5)], axis=0)
    earlier = low(grid((leaf_dev, leaf_dev), 0) < grid((leaf_dev, leaf_dev), 1))
    a, b = grid((every, every), 0), grid((every, every), 1)
    above = (b < a)
    for o in range(1, 4):
        above = above & ((a < o * fan) | (b >= o * fan))
    within = jnp.dot(low(mask), earlier, preferred_element_type=jnp.float32)
    base = jnp.sum(
        jnp.dot(low(above), low(mask), preferred_element_type=jnp.float32), axis=1, keepdims=True
    )
    place = jnp.where(mask > 0.0, within + base, -1.0)
    slot = grid((SLOTS, leaf_dev), 0).astype(jnp.float32)
    leaf = grid((1, leaf_dev), 1).astype(jnp.float32)
    ones = jnp.ones((1, leaf_dev), jnp.float32)
    total = jnp.zeros((8, 4 * SLOTS), jnp.float32)
    for k in range(fan):
        hit = jnp.concatenate(
            [(place[o * fan + k : o * fan + k + 1] == slot).astype(jnp.float32) for o in range(4)],
            axis=0,
        )
        facts = jnp.concatenate(
            [row[k : k + 1].astype(jnp.float32), leaf, k * ones, ones]
            + [jnp.zeros((4, leaf_dev), jnp.float32)], axis=0,
        )
        total = total + lax.dot_general(
            low(facts), low(hit), BY_ROWS, preferred_element_type=jnp.float32
        )
    asked[...] = total[0:1].astype(jnp.int32)
    slots[0:1] = jnp.where(total[3:4] > 0.0, total[1:2], float(leaf_dev)).astype(jnp.int32)
    slots[1:2] = total[2:3].astype(jnp.int32)


def beside(xs):
    return jnp.concatenate(xs, axis=1)


def below(xs):
    return jnp.concatenate(xs, axis=0)


def paired(x, y, left, right, by_rows=False):
    samples = x.shape[0]
    if by_rows:
        wide = left.shape[0]
        both = lax.dot_general(
            below([x, y]), below([left, right]), BY_ROWS, preferred_element_type=jnp.float32
        )
    else:
        wide = left.shape[1]
        both = jnp.dot(below([x, y]), beside([left, right]), preferred_element_type=jnp.float32)
    return both[:samples, :wide], both[samples:, wide:]


def local_kernel(home, latent, before, weights, left, rows):
    leaf_dev, fan, width = latent.shape[0], weights.shape[1], weights.shape[2]
    rows[pl.ds(0, leaf_dev)] = latent[...]
    rows[leaf_dev] = jnp.zeros(latent.shape[1:], latent.dtype)

    def some(c, carry):
        for u in range(LEAVES):
            i = c * LEAVES + u
            mean = jnp.dot(
                beside([rows[home[k, i]] for k in range(fan)]),
                weights[i].reshape(fan * width, width), preferred_element_type=jnp.float32,
            )
            left[i] = latent[i].astype(jnp.float32) - mean
        return carry

    lax.fori_loop(0, leaf_dev // LEAVES, some, 0)


def serve_kernel(capacity, ask1, ask2, ask8, latent, before, out8, out2, out1):
    me = lax.axis_index("kx")
    def pick(o, ask, rows, out):
        for r in range(capacity):
            out[r] = rows[ask[0, o * SLOTS + r]]

    pick(3, ask8, before, out8)
    for o, ask, out, bits in ((1, ask2, out2, 2), (0, ask1, out1, 3)):
        relays = lax.bitwise_and(me, bits) == bits

        @pl.when(relays)
        def _():
            pick(o, ask, before, out)

        @pl.when(jnp.logical_not(relays))
        def _():
            pick(o, ask, latent, out)


def asker(slots, weights, o, r):
    i = slots[0, o * SLOTS + r]
    return i, weights[jnp.minimum(i, weights.shape[0] - 1), slots[1, o * SLOTS + r]]


def remote_terms(capacity, slots, asked_row, low, weights, outs):
    listed = jnp.broadcast_to(asked_row[...].astype(jnp.float32), low.shape[1:])
    for o, out in outs:
        for r in range(0, capacity, 2):
            (i, w), (j, v) = asker(slots, weights, o, r), asker(slots, weights, o, r + 1)
            for at, x in zip((r, r + 1), paired(low[i], low[j], w, v, True)):
                out[at] = x.astype(out.dtype)
        out[capacity] = listed.astype(out.dtype)


def remote_kernel(
    capacity, asked, slots, asked_row, left, before, from2, from8, from1,
    weights, factor, back, low, out8, out4, out2, out1, resid,
):
    leaf_dev = back.shape[0]
    resid[pl.ds(0, leaf_dev)] = left[...]
    resid[leaf_dev] = jnp.zeros(left.shape[1:], left.dtype)
    low[leaf_dev] = jnp.zeros(left.shape[1:], low.dtype)

    for o, rows in ((2, before), (3, from8), (1, from2), (0, from1)):
        found = []
        for r in range(0, capacity, 2):
            (i, w), (j, v) = asker(slots, weights, o, r), asker(slots, weights, o, r + 1)
            at = (asked[0, o * SLOTS + r], asked[0, o * SLOTS + r + 1]) if o == 2 else (r, r + 1)
            found += zip((i, j), paired(rows[at[0]], rows[at[1]], w, v))
        for i, mean in found:
            resid[i] = resid[i] - mean

    def leaves(c, carry):
        pairs = [c * LEAVES + u for u in range(0, LEAVES, 2)]
        innov = [
            paired(
                resid[i].astype(jnp.bfloat16), resid[i + 1].astype(jnp.bfloat16),
                factor[i], factor[i + 1],
            )
            for i in pairs
        ]
        for i, (x, y) in zip(pairs, innov):
            both = paired(
                x.astype(jnp.bfloat16), y.astype(jnp.bfloat16), factor[i], factor[i + 1], True
            )
            for j, z in zip((i, i + 1), both):
                back[j] = z
                low[j] = z.astype(jnp.bfloat16)
        return carry

    lax.fori_loop(0, leaf_dev // LEAVES, leaves, 0)
    remote_terms(
        capacity, slots, asked_row, low, weights, ((3, out8), (2, out4), (1, out2), (0, out1))
    )


def home_kernel(home, back, low, weights, part, acc):
    leaf_dev = back.shape[0]
    fan, width = weights.shape[1], weights.shape[2]
    acc[pl.ds(0, leaf_dev)] = -back[...]
    acc[leaf_dev] = jnp.zeros(back.shape[1:], back.dtype)

    def some(c, carry):
        found = []
        for u in range(LEAVES):
            i = c * LEAVES + u
            found.append((i, lax.dot_general(
                low[i], weights[i].reshape(fan * width, width), BY_ROWS,
                preferred_element_type=jnp.float32,
            )))
        for i, x in found:
            for k in range(fan):
                j = home[k, i]
                acc[j] = acc[j] + x[:, k * width : (k + 1) * width]
        return carry

    lax.fori_loop(0, leaf_dev // LEAVES, some, 0)
    part[...] = acc[pl.ds(0, leaf_dev)]


def add_kernel(capacity, part, ring, back2, back8, back4, relayed, out, listed, wanted, sem):
    last = lax.bitwise_and(lax.axis_index("kx"), 3) == 3

    def back1(r):
        return jnp.where(last, relayed[r].astype(jnp.float32), ring[r].astype(jnp.float32))

    returned = [(3, back8), (2, back4), (1, back2)]
    returned = [(o, lambda r, x=x: x[r].astype(jnp.float32)) for o, x in returned] + [(0, back1)]
    for o, row in returned:
        listed[o : o + 1] = row(capacity)[0:1].astype(jnp.int32)
    fetch = pltpu.make_async_copy(listed, wanted, sem)
    fetch.start()
    out[...] = part[...]
    fetch.wait()
    for o, row in returned:
        for r in range(capacity):
            j = wanted[o, o * SLOTS + r]
            out[j] = out[j] + row(r)


def call(body, name, out_shape, ins, outs, limit, flops=0, moved=0, scratch=(), aliases={}):
    spec = lambda space: pl.BlockSpec(memory_space=space)
    return pl.pallas_call(
        body,
        out_shape=out_shape,
        in_specs=[spec(space) for space in ins],
        out_specs=tuple(spec(space) for space in outs),
        scratch_shapes=scratch,
        input_output_aliases=aliases,
        compiler_params=pltpu.CompilerParams(vmem_limit_bytes=limit * MIB),
        cost_estimate=pl.CostEstimate(flops=flops, bytes_accessed=moved, transcendentals=0),
        name=name,
    )


def placed(x, space):
    return pltpu.with_memory_space_constraint(x, space)


def per_device(latent, cond_lists, cond_weights, precision_factor):
    devices = lax.axis_size("kx")
    leaf_dev, samples, width = latent.shape
    fan = cond_lists.shape[1]
    capacity = fan * leaf_dev // 8
    everyone = range(devices)
    shape = jax.ShapeDtypeStruct
    some_rows = shape((capacity, samples, width), jnp.bfloat16)
    sent = shape((capacity + 1, samples, width), jnp.bfloat16)
    all_rows = shape(latent.shape, jnp.float32)
    one_list = shape((1, 4 * SLOTS), jnp.int32)
    heavy = cond_weights.size * 2

    def passed(x, route):
        return lax.ppermute(x, "kx", route)

    before = passed(latent, [(i, i + 4) for i in everyone if i + 4 < devices])
    weights, factor = placed(cond_weights, VMEM), placed(precision_factor, VMEM)
    held_l = placed(latent, VMEM)
    asked, slots, home = call(
        index_kernel, "index",
        (one_list, shape((2, 4 * SLOTS), jnp.int32), shape((fan, leaf_dev), jnp.int32)),
        [VMEM, HBM, HBM], [VMEM] * 3, 4, moved=2 * MIB,
    )(placed(cond_lists.T, HBM), placed(latent, HBM), placed(cond_weights, HBM))
    ask8 = passed(asked, [(i, i - 4) for i in everyone if i >= 4])
    ask2 = passed(asked, [(i, i ^ 2) for i in everyone])
    ask1 = passed(asked, [(i, i // 4 * 4 + (i + 3) % 4) for i in everyone])
    serve8, serve2, serve1 = call(
        functools.partial(serve_kernel, capacity), "serve", (some_rows,) * 3,
        [SMEM] * 3 + [VMEM] * 2, [VMEM] * 3, 4, moved=4 * MIB,
    )(ask1, ask2, ask8, held_l, before)
    from8 = passed(serve8, [(i, i + 4) for i in everyone if i >= 4 and i + 4 < devices])
    from2 = passed(serve2, [(i, i ^ 2) for i in everyone])
    from1 = passed(serve1, [(i, i // 4 * 4 + (i + 1) % 4) for i in everyone])
    (left,) = call(
        local_kernel, "local", (all_rows,), [SMEM, VMEM, ANY, VMEM], [VMEM], 6, moved=heavy,
        scratch=[VMEM((leaf_dev + 8, samples, width), jnp.bfloat16)],
    )(home, held_l, before, weights)
    back, low, out8, out4, out2, out1 = call(
        functools.partial(remote_kernel, capacity), "remote",
        (all_rows, shape((leaf_dev + 8, samples, width), jnp.bfloat16)) + (sent,) * 4,
        [SMEM] * 2 + [VMEM] * 8, [VMEM] * 6, 8, moved=heavy,
        scratch=[VMEM((leaf_dev + 8, samples, width), jnp.float32)],
    )(asked, slots, asked, left, before, from2, from8, from1, weights, factor)
    def back_by(x, reach):
        return passed(x, [(i, i - reach) for i in everyone if i >= reach])

    ring = passed(out1, [(i, i // 4 * 4 + (i + 3) % 4) for i in everyone])
    back8, back4, back2 = back_by(out8, 8), back_by(out4, 4), back_by(out2, 2)
    relayed = passed(ring, [(i, i - 4) for i in everyone if i >= 4 and i % 4 == 3])
    (part,) = call(
        home_kernel, "home", (all_rows,), [SMEM] + [VMEM] * 3, [VMEM], 6, moved=heavy,
        scratch=[VMEM((leaf_dev + 8, samples, width), jnp.float32)],
    )(home, back, low, weights)
    lists = (4, 4 * SLOTS)
    (gradient,) = call(
        functools.partial(add_kernel, capacity), "add", (all_rows,), [VMEM] * 6,
        [VMEM], 6, moved=4 * MIB, scratch=[VMEM(lists, jnp.int32), SMEM(lists, jnp.int32), pltpu.SemaphoreType.DMA],
    )(part, ring, back2, back8, back4, relayed)
    return gradient


def solution(mesh):
    return jax.shard_map(
        per_device,
        mesh=mesh,
        in_specs=(
            P(("groups", "kx"), None, None),
            P(("groups", "kx"), None),
            P(("groups", "kx"), None, None, None),
            P(("groups", "kx"), None, None),
        ),
        out_specs=P(("groups", "kx"), None, None),
        check_vma=False,
    )
```

```python
import functools

import jax
import jax.numpy as jnp
from jax import lax
from jax.experimental import pallas as pl
from jax.experimental.pallas import tpu as pltpu
from jax.sharding import PartitionSpec as P

SLOTS = 32
LEAVES = 80
MIB = 2**20
BY_ROWS = (((1,), (1,)), ((), ()))
VMEM, SMEM, HBM, ANY = pltpu.VMEM, pltpu.SMEM, pltpu.HBM, pl.ANY


def index_kernel(lists, latent, weights, asked, slots, home):
    fan, leaf_dev = lists.shape
    me = lax.axis_index("kx")
    behind = me * leaf_dev - lists[...]
    kind = (
        (behind > 0).astype(jnp.int32)
        + (behind > leaf_dev).astype(jnp.int32)
        + (behind > 2 * leaf_dev).astype(jnp.int32)
        + (behind > 4 * leaf_dev).astype(jnp.int32)
    )
    reach = jnp.where(kind == 4, 8, jnp.where(kind == 3, 4, kind))
    row = reach * leaf_dev - behind
    home[...] = jnp.where(kind == 0, row, leaf_dev)

    def grid(shape, dim):
        return lax.broadcasted_iota(jnp.int32, shape, dim)

    def low(x):
        return x.astype(jnp.float32).astype(jnp.bfloat16)

    every = 4 * fan
    mask = jnp.concatenate([(kind == o).astype(jnp.float32) for o in range(1, 5)], axis=0)
    earlier = low(grid((leaf_dev, leaf_dev), 0) < grid((leaf_dev, leaf_dev), 1))
    a, b = grid((every, every), 0), grid((every, every), 1)
    above = (b < a)
    for o in range(1, 4):
        above = above & ((a < o * fan) | (b >= o * fan))
    within = jnp.dot(low(mask), earlier, preferred_element_type=jnp.float32)
    base = jnp.sum(
        jnp.dot(low(above), low(mask), preferred_element_type=jnp.float32), axis=1, keepdims=True
    )
    place = jnp.where(mask > 0.0, within + base, -1.0)
    slot = grid((SLOTS, leaf_dev), 0).astype(jnp.float32)
    leaf = grid((1, leaf_dev), 1).astype(jnp.float32)
    ones = jnp.ones((1, leaf_dev), jnp.float32)
    total = jnp.zeros((8, 4 * SLOTS), jnp.float32)
    for k in range(fan):
        hit = jnp.concatenate(
            [(place[o * fan + k : o * fan + k + 1] == slot).astype(jnp.float32) for o in range(4)],
            axis=0,
        )
        facts = jnp.concatenate(
            [row[k : k + 1].astype(jnp.float32), leaf, k * ones, ones]
            + [jnp.zeros((4, leaf_dev), jnp.float32)], axis=0,
        )
        total = total + lax.dot_general(
            low(facts), low(hit), BY_ROWS, preferred_element_type=jnp.float32
        )
    asked[...] = total[0:1].astype(jnp.int32)
    slots[0:1] = jnp.where(total[3:4] > 0.0, total[1:2], float(leaf_dev)).astype(jnp.int32)
    slots[1:2] = total[2:3].astype(jnp.int32)


def beside(xs):
    return jnp.concatenate(xs, axis=1)


def below(xs):
    return jnp.concatenate(xs, axis=0)


def paired(x, y, left, right, by_rows=False):
    samples = x.shape[0]
    if by_rows:
        wide = left.shape[0]
        both = lax.dot_general(
            below([x, y]), below([left, right]), BY_ROWS, preferred_element_type=jnp.float32
        )
    else:
        wide = left.shape[1]
        both = jnp.dot(below([x, y]), beside([left, right]), preferred_element_type=jnp.float32)
    return both[:samples, :wide], both[samples:, wide:]


def local_kernel(home, latent, before, weights, left, rows):
    leaf_dev, fan, width = latent.shape[0], weights.shape[1], weights.shape[2]
    rows[pl.ds(0, leaf_dev)] = latent[...]
    rows[leaf_dev] = jnp.zeros(latent.shape[1:], latent.dtype)

    def some(c, carry):
        for u in range(LEAVES):
            i = c * LEAVES + u
            mean = jnp.dot(
                beside([rows[home[k, i]] for k in range(fan)]),
                weights[i].reshape(fan * width, width), preferred_element_type=jnp.float32,
            )
            left[i] = latent[i].astype(jnp.float32) - mean
        return carry

    lax.fori_loop(0, leaf_dev // LEAVES, some, 0)


def serve_kernel(capacity, ask1, ask2, ask8, latent, before, out8, out2, out1):
    me = lax.axis_index("kx")
    def pick(o, ask, rows, out):
        for r in range(capacity):
            out[r] = rows[ask[0, o * SLOTS + r]]

    pick(3, ask8, before, out8)
    for o, ask, out, bits in ((1, ask2, out2, 2), (0, ask1, out1, 3)):
        relays = lax.bitwise_and(me, bits) == bits

        @pl.when(relays)
        def _():
            pick(o, ask, before, out)

        @pl.when(jnp.logical_not(relays))
        def _():
            pick(o, ask, latent, out)


def asker(slots, weights, o, r):
    i = slots[0, o * SLOTS + r]
    return i, weights[jnp.minimum(i, weights.shape[0] - 1), slots[1, o * SLOTS + r]]


def remote_terms(capacity, slots, asked_row, low, weights, outs):
    listed = jnp.broadcast_to(asked_row[...].astype(jnp.float32), low.shape[1:])
    for o, out in outs:
        for r in range(0, capacity, 2):
            (i, w), (j, v) = asker(slots, weights, o, r), asker(slots, weights, o, r + 1)
            for at, x in zip((r, r + 1), paired(low[i], low[j], w, v, True)):
                out[at] = x.astype(out.dtype)
        out[capacity] = listed.astype(out.dtype)


def remote_kernel(
    capacity, asked, slots, asked_row, left, before, from2, from1, from8,
    weights, factor, back, low, out8, out4, out2, out1, resid,
):
    leaf_dev = back.shape[0]
    resid[pl.ds(0, leaf_dev)] = left[...]
    resid[leaf_dev] = jnp.zeros(left.shape[1:], left.dtype)
    low[leaf_dev] = jnp.zeros(left.shape[1:], low.dtype)

    for o, rows in ((2, before), (3, from8), (1, from2), (0, from1)):
        found = []
        for r in range(0, capacity, 2):
            (i, w), (j, v) = asker(slots, weights, o, r), asker(slots, weights, o, r + 1)
            at = (asked[0, o * SLOTS + r], asked[0, o * SLOTS + r + 1]) if o == 2 else (r, r + 1)
            found += zip((i, j), paired(rows[at[0]], rows[at[1]], w, v))
        for i, mean in found:
            resid[i] = resid[i] - mean

    def leaves(c, carry):
        pairs = [c * LEAVES + u for u in range(0, LEAVES, 2)]
        innov = [
            paired(
                resid[i].astype(jnp.bfloat16), resid[i + 1].astype(jnp.bfloat16),
                factor[i], factor[i + 1],
            )
            for i in pairs
        ]
        for i, (x, y) in zip(pairs, innov):
            both = paired(
                x.astype(jnp.bfloat16), y.astype(jnp.bfloat16), factor[i], factor[i + 1], True
            )
            for j, z in zip((i, i + 1), both):
                back[j] = z
                low[j] = z.astype(jnp.bfloat16)
        return carry

    lax.fori_loop(0, leaf_dev // LEAVES, leaves, 0)
    remote_terms(
        capacity, slots, asked_row, low, weights, ((3, out8), (2, out4), (1, out2), (0, out1))
    )


def home_kernel(home, back, low, weights, part, acc):
    leaf_dev = back.shape[0]
    fan, width = weights.shape[1], weights.shape[2]
    acc[pl.ds(0, leaf_dev)] = -back[...]
    acc[leaf_dev] = jnp.zeros(back.shape[1:], back.dtype)

    def some(c, carry):
        found = []
        for u in range(LEAVES):
            i = c * LEAVES + u
            found.append((i, lax.dot_general(
                low[i], weights[i].reshape(fan * width, width), BY_ROWS,
                preferred_element_type=jnp.float32,
            )))
        for i, x in found:
            for k in range(fan):
                j = home[k, i]
                acc[j] = acc[j] + x[:, k * width : (k + 1) * width]
        return carry

    lax.fori_loop(0, leaf_dev // LEAVES, some, 0)
    part[...] = acc[pl.ds(0, leaf_dev)]


def add_kernel(capacity, part, back8, ring, back4, back2, relayed, out, listed, wanted, sem):
    last = lax.bitwise_and(lax.axis_index("kx"), 3) == 3

    def back1(r):
        return jnp.where(last, relayed[r].astype(jnp.float32), ring[r].astype(jnp.float32))

    returned = [(3, back8), (2, back4), (1, back2)]
    returned = [(o, lambda r, x=x: x[r].astype(jnp.float32)) for o, x in returned] + [(0, back1)]
    for o, row in returned:
        listed[o : o + 1] = row(capacity)[0:1].astype(jnp.int32)
    fetch = pltpu.make_async_copy(listed, wanted, sem)
    fetch.start()
    out[...] = part[...]
    fetch.wait()
    for o, row in returned:
        for r in range(capacity):
            j = wanted[o, o * SLOTS + r]
            out[j] = out[j] + row(r)


def call(body, name, out_shape, ins, outs, limit, flops=0, moved=0, scratch=(), aliases={}):
    spec = lambda space: pl.BlockSpec(memory_space=space)
    return pl.pallas_call(
        body,
        out_shape=out_shape,
        in_specs=[spec(space) for space in ins],
        out_specs=tuple(spec(space) for space in outs),
        scratch_shapes=scratch,
        input_output_aliases=aliases,
        compiler_params=pltpu.CompilerParams(vmem_limit_bytes=limit * MIB),
        cost_estimate=pl.CostEstimate(flops=flops, bytes_accessed=moved, transcendentals=0),
        name=name,
    )


def placed(x, space):
    return pltpu.with_memory_space_constraint(x, space)


def per_device(latent, cond_lists, cond_weights, precision_factor):
    devices = lax.axis_size("kx")
    leaf_dev, samples, width = latent.shape
    fan = cond_lists.shape[1]
    capacity = fan * leaf_dev // 8
    everyone = range(devices)
    shape = jax.ShapeDtypeStruct
    some_rows = shape((capacity, samples, width), jnp.bfloat16)
    sent = shape((capacity + 1, samples, width), jnp.bfloat16)
    all_rows = shape(latent.shape, jnp.float32)
    one_list = shape((1, 4 * SLOTS), jnp.int32)
    heavy = cond_weights.size * 2

    def passed(x, route):
        return lax.ppermute(x, "kx", route)

    before = passed(latent, [(i, i + 4) for i in everyone if i + 4 < devices])
    weights, factor = placed(cond_weights, VMEM), placed(precision_factor, VMEM)
    held_l = placed(latent, VMEM)
    asked, slots, home = call(
        index_kernel, "index",
        (one_list, shape((2, 4 * SLOTS), jnp.int32), shape((fan, leaf_dev), jnp.int32)),
        [VMEM, HBM, HBM], [VMEM] * 3, 4, moved=2 * MIB,
    )(placed(cond_lists.T, HBM), placed(latent, HBM), placed(cond_weights, HBM))
    ask8 = passed(asked, [(i, i - 4) for i in everyone if i >= 4])
    ask2 = passed(asked, [(i, i ^ 2) for i in everyone])
    ask1 = passed(asked, [(i, i // 4 * 4 + (i + 3) % 4) for i in everyone])
    serve8, serve2, serve1 = call(
        functools.partial(serve_kernel, capacity), "serve", (some_rows,) * 3,
        [SMEM] * 3 + [VMEM] * 2, [VMEM] * 3, 4, moved=4 * MIB,
    )(ask1, ask2, ask8, held_l, before)
    from8 = passed(serve8, [(i, i + 4) for i in everyone if i >= 4 and i + 4 < devices])
    from2 = passed(serve2, [(i, i ^ 2) for i in everyone])
    from1 = passed(serve1, [(i, i // 4 * 4 + (i + 1) % 4) for i in everyone])
    (left,) = call(
        local_kernel, "local", (all_rows,), [SMEM, VMEM, ANY, VMEM], [VMEM], 6, moved=heavy,
        scratch=[VMEM((leaf_dev + 8, samples, width), jnp.bfloat16)],
    )(home, held_l, before, weights)
    back, low, out8, out4, out2, out1 = call(
        functools.partial(remote_kernel, capacity), "remote",
        (all_rows, shape((leaf_dev + 8, samples, width), jnp.bfloat16)) + (sent,) * 4,
        [SMEM] * 2 + [VMEM] * 8, [VMEM] * 6, 8, moved=heavy,
        scratch=[VMEM((leaf_dev + 8, samples, width), jnp.float32)],
    )(asked, slots, asked, left, before, from2, from1, from8, weights, factor)
    def back_by(x, reach):
        return passed(x, [(i, i - reach) for i in everyone if i >= reach])

    ring = passed(out1, [(i, i // 4 * 4 + (i + 3) % 4) for i in everyone])
    back8, back4, back2 = back_by(out8, 8), back_by(out4, 4), back_by(out2, 2)
    relayed = passed(ring, [(i, i - 4) for i in everyone if i >= 4 and i % 4 == 3])
    (part,) = call(
        home_kernel, "home", (all_rows,), [SMEM] + [VMEM] * 3, [VMEM], 6, moved=heavy,
        scratch=[VMEM((leaf_dev + 8, samples, width), jnp.float32)],
    )(home, back, low, weights)
    lists = (4, 4 * SLOTS)
    (gradient,) = call(
        functools.partial(add_kernel, capacity), "add", (all_rows,), [VMEM] * 6,
        [VMEM], 6, moved=4 * MIB, scratch=[VMEM(lists, jnp.int32), SMEM(lists, jnp.int32), pltpu.SemaphoreType.DMA],
    )(part, back8, ring, back4, back2, relayed)
    return gradient


def solution(mesh):
    return jax.shard_map(
        per_device,
        mesh=mesh,
        in_specs=(
            P(("groups", "kx"), None, None),
            P(("groups", "kx"), None),
            P(("groups", "kx"), None, None, None),
            P(("groups", "kx"), None, None),
        ),
        out_specs=P(("groups", "kx"), None, None),
        check_vma=False,
    )
```

```python
import functools

import jax
import jax.numpy as jnp
from jax import lax
from jax.experimental import pallas as pl
from jax.experimental.pallas import tpu as pltpu
from jax.sharding import PartitionSpec as P

SLOTS = 32
LEAVES = 80
MIB = 2**20
BY_ROWS = (((1,), (1,)), ((), ()))
VMEM, SMEM, HBM, ANY = pltpu.VMEM, pltpu.SMEM, pltpu.HBM, pl.ANY


def index_kernel(lists, latent, weights, asked, slots, home):
    fan, leaf_dev = lists.shape
    me = lax.axis_index("kx")
    behind = me * leaf_dev - lists[...]
    kind = (
        (behind > 0).astype(jnp.int32)
        + (behind > leaf_dev).astype(jnp.int32)
        + (behind > 2 * leaf_dev).astype(jnp.int32)
        + (behind > 4 * leaf_dev).astype(jnp.int32)
    )
    reach = jnp.where(kind == 4, 8, jnp.where(kind == 3, 4, kind))
    row = reach * leaf_dev - behind
    home[...] = jnp.where(kind == 0, row, leaf_dev)

    def grid(shape, dim):
        return lax.broadcasted_iota(jnp.int32, shape, dim)

    def low(x):
        return x.astype(jnp.float32).astype(jnp.bfloat16)

    every = 4 * fan
    mask = jnp.concatenate([(kind == o).astype(jnp.float32) for o in range(1, 5)], axis=0)
    earlier = low(grid((leaf_dev, leaf_dev), 0) < grid((leaf_dev, leaf_dev), 1))
    a, b = grid((every, every), 0), grid((every, every), 1)
    above = (b < a)
    for o in range(1, 4):
        above = above & ((a < o * fan) | (b >= o * fan))
    within = jnp.dot(low(mask), earlier, preferred_element_type=jnp.float32)
    base = jnp.sum(
        jnp.dot(low(above), low(mask), preferred_element_type=jnp.float32), axis=1, keepdims=True
    )
    place = jnp.where(mask > 0.0, within + base, -1.0)
    slot = grid((SLOTS, leaf_dev), 0).astype(jnp.float32)
    leaf = grid((1, leaf_dev), 1).astype(jnp.float32)
    ones = jnp.ones((1, leaf_dev), jnp.float32)
    total = jnp.zeros((8, 4 * SLOTS), jnp.float32)
    for k in range(fan):
        hit = jnp.concatenate(
            [(place[o * fan + k : o * fan + k + 1] == slot).astype(jnp.float32) for o in range(4)],
            axis=0,
        )
        facts = jnp.concatenate(
            [row[k : k + 1].astype(jnp.float32), leaf, k * ones, ones]
            + [jnp.zeros((4, leaf_dev), jnp.float32)], axis=0,
        )
        total = total + lax.dot_general(
            low(facts), low(hit), BY_ROWS, preferred_element_type=jnp.float32
        )
    asked[...] = total[0:1].astype(jnp.int32)
    slots[0:1] = jnp.where(total[3:4] > 0.0, total[1:2], float(leaf_dev)).astype(jnp.int32)
    slots[1:2] = total[2:3].astype(jnp.int32)


def beside(xs):
    return jnp.concatenate(xs, axis=1)


def below(xs):
    return jnp.concatenate(xs, axis=0)


def paired(x, y, left, right, by_rows=False):
    samples = x.shape[0]
    if by_rows:
        wide = left.shape[0]
        both = lax.dot_general(
            below([x, y]), below([left, right]), BY_ROWS, preferred_element_type=jnp.float32
        )
    else:
        wide = left.shape[1]
        both = jnp.dot(below([x, y]), beside([left, right]), preferred_element_type=jnp.float32)
    return both[:samples, :wide], both[samples:, wide:]


def local_kernel(home, latent, before, weights, left, rows):
    leaf_dev, fan, width = latent.shape[0], weights.shape[1], weights.shape[2]
    rows[pl.ds(0, leaf_dev)] = latent[...]
    rows[leaf_dev] = jnp.zeros(latent.shape[1:], latent.dtype)

    def some(c, carry):
        for u in range(LEAVES):
            i = c * LEAVES + u
            mean = jnp.dot(
                beside([rows[home[k, i]] for k in range(fan)]),
                weights[i].reshape(fan * width, width), preferred_element_type=jnp.float32,
            )
            left[i] = latent[i].astype(jnp.float32) - mean
        return carry

    lax.fori_loop(0, leaf_dev // LEAVES, some, 0)


def serve_kernel(capacity, ask1, ask2, ask8, latent, before, out8, out2, out1):
    me = lax.axis_index("kx")
    def pick(o, ask, rows, out):
        for r in range(capacity):
            out[r] = rows[ask[0, o * SLOTS + r]]

    pick(3, ask8, before, out8)
    for o, ask, out, bits in ((1, ask2, out2, 2), (0, ask1, out1, 3)):
        relays = lax.bitwise_and(me, bits) == bits

        @pl.when(relays)
        def _():
            pick(o, ask, before, out)

        @pl.when(jnp.logical_not(relays))
        def _():
            pick(o, ask, latent, out)


def asker(slots, weights, o, r):
    i = slots[0, o * SLOTS + r]
    return i, weights[jnp.minimum(i, weights.shape[0] - 1), slots[1, o * SLOTS + r]]


def remote_terms(capacity, slots, asked_row, low, weights, outs):
    listed = jnp.broadcast_to(asked_row[...].astype(jnp.float32), low.shape[1:])
    for o, out in outs:
        for r in range(0, capacity, 2):
            (i, w), (j, v) = asker(slots, weights, o, r), asker(slots, weights, o, r + 1)
            for at, x in zip((r, r + 1), paired(low[i], low[j], w, v, True)):
                out[at] = x.astype(out.dtype)
        out[capacity] = listed.astype(out.dtype)


def remote_kernel(
    capacity, asked, slots, asked_row, left, before, from2, from1, from8,
    weights, factor, back, low, out8, out4, out2, out1, resid,
):
    leaf_dev = back.shape[0]
    resid[pl.ds(0, leaf_dev)] = left[...]
    resid[leaf_dev] = jnp.zeros(left.shape[1:], left.dtype)
    low[leaf_dev] = jnp.zeros(left.shape[1:], low.dtype)

    for o, rows in ((2, before), (3, from8), (1, from2), (0, from1)):
        found = []
        for r in range(0, capacity, 2):
            (i, w), (j, v) = asker(slots, weights, o, r), asker(slots, weights, o, r + 1)
            at = (asked[0, o * SLOTS + r], asked[0, o * SLOTS + r + 1]) if o == 2 else (r, r + 1)
            found += zip((i, j), paired(rows[at[0]], rows[at[1]], w, v))
        for i, mean in found:
            resid[i] = resid[i] - mean

    def leaves(c, carry):
        pairs = [c * LEAVES + u for u in range(0, LEAVES, 2)]
        innov = [
            paired(
                resid[i].astype(jnp.bfloat16), resid[i + 1].astype(jnp.bfloat16),
                factor[i], factor[i + 1],
            )
            for i in pairs
        ]
        for i, (x, y) in zip(pairs, innov):
            both = paired(
                x.astype(jnp.bfloat16), y.astype(jnp.bfloat16), factor[i], factor[i + 1], True
            )
            for j, z in zip((i, i + 1), both):
                back[j] = z
                low[j] = z.astype(jnp.bfloat16)
        return carry

    lax.fori_loop(0, leaf_dev // LEAVES, leaves, 0)
    remote_terms(
        capacity, slots, asked_row, low, weights, ((3, out8), (2, out4), (1, out2), (0, out1))
    )


def home_kernel(home, back, low, weights, part, acc):
    leaf_dev = back.shape[0]
    fan, width = weights.shape[1], weights.shape[2]
    acc[pl.ds(0, leaf_dev)] = -back[...]
    acc[leaf_dev] = jnp.zeros(back.shape[1:], back.dtype)

    def some(c, carry):
        found = []
        for u in range(LEAVES):
            i = c * LEAVES + u
            found.append((i, lax.dot_general(
                low[i], weights[i].reshape(fan * width, width), BY_ROWS,
                preferred_element_type=jnp.float32,
            )))
        for i, x in found:
            for k in range(fan):
                j = home[k, i]
                acc[j] = acc[j] + x[:, k * width : (k + 1) * width]
        return carry

    lax.fori_loop(0, leaf_dev // LEAVES, some, 0)
    part[...] = acc[pl.ds(0, leaf_dev)]


def add_rows(capacity, returned, part, out, listed, wanted, sem):
    for n, (_, row) in enumerate(returned):
        listed[n : n + 1] = row(capacity)[0:1].astype(jnp.int32)
    fetch = pltpu.make_async_copy(listed, wanted, sem)
    fetch.start()
    out[...] = part[...]
    fetch.wait()
    for n, (o, row) in enumerate(returned):
        for r in range(capacity):
            j = wanted[n, o * SLOTS + r]
            out[j] = out[j] + row(r)


def far_kernel(capacity, part, back8, back4, out, listed, wanted, sem):
    returned = [(o, lambda r, x=x: x[r].astype(jnp.float32)) for o, x in ((3, back8), (2, back4))]
    add_rows(capacity, returned, part, out, listed, wanted, sem)


def add_kernel(capacity, part, ring, back2, relayed, out, listed, wanted, sem):
    last = lax.bitwise_and(lax.axis_index("kx"), 3) == 3

    def back1(r):
        return jnp.where(last, relayed[r].astype(jnp.float32), ring[r].astype(jnp.float32))

    returned = [(1, lambda r: back2[r].astype(jnp.float32)), (0, back1)]
    add_rows(capacity, returned, part, out, listed, wanted, sem)


def call(body, name, out_shape, ins, outs, limit, flops=0, moved=0, scratch=(), aliases={}):
    spec = lambda space: pl.BlockSpec(memory_space=space)
    return pl.pallas_call(
        body,
        out_shape=out_shape,
        in_specs=[spec(space) for space in ins],
        out_specs=tuple(spec(space) for space in outs),
        scratch_shapes=scratch,
        input_output_aliases=aliases,
        compiler_params=pltpu.CompilerParams(vmem_limit_bytes=limit * MIB),
        cost_estimate=pl.CostEstimate(flops=flops, bytes_accessed=moved, transcendentals=0),
        name=name,
    )


def placed(x, space):
    return pltpu.with_memory_space_constraint(x, space)


def per_device(latent, cond_lists, cond_weights, precision_factor):
    devices = lax.axis_size("kx")
    leaf_dev, samples, width = latent.shape
    fan = cond_lists.shape[1]
    capacity = fan * leaf_dev // 8
    everyone = range(devices)
    shape = jax.ShapeDtypeStruct
    some_rows = shape((capacity, samples, width), jnp.bfloat16)
    sent = shape((capacity + 1, samples, width), jnp.bfloat16)
    all_rows = shape(latent.shape, jnp.float32)
    one_list = shape((1, 4 * SLOTS), jnp.int32)
    heavy = cond_weights.size * 2

    def passed(x, route):
        return lax.ppermute(x, "kx", route)

    before = passed(latent, [(i, i + 4) for i in everyone if i + 4 < devices])
    weights, factor = placed(cond_weights, VMEM), placed(precision_factor, VMEM)
    held_l = placed(latent, VMEM)
    asked, slots, home = call(
        index_kernel, "index",
        (one_list, shape((2, 4 * SLOTS), jnp.int32), shape((fan, leaf_dev), jnp.int32)),
        [VMEM, HBM, HBM], [VMEM] * 3, 4, moved=2 * MIB,
    )(placed(cond_lists.T, HBM), placed(latent, HBM), placed(cond_weights, HBM))
    ask8 = passed(asked, [(i, i - 4) for i in everyone if i >= 4])
    ask2 = passed(asked, [(i, i ^ 2) for i in everyone])
    ask1 = passed(asked, [(i, i // 4 * 4 + (i + 3) % 4) for i in everyone])
    serve8, serve2, serve1 = call(
        functools.partial(serve_kernel, capacity), "serve", (some_rows,) * 3,
        [SMEM] * 3 + [VMEM] * 2, [VMEM] * 3, 4, moved=4 * MIB,
    )(ask1, ask2, ask8, held_l, before)
    from8 = passed(serve8, [(i, i + 4) for i in everyone if i >= 4 and i + 4 < devices])
    from2 = passed(serve2, [(i, i ^ 2) for i in everyone])
    from1 = passed(serve1, [(i, i // 4 * 4 + (i + 1) % 4) for i in everyone])
    (left,) = call(
        local_kernel, "local", (all_rows,), [SMEM, VMEM, ANY, VMEM], [VMEM], 6, moved=heavy,
        scratch=[VMEM((leaf_dev + 8, samples, width), jnp.bfloat16)],
    )(home, held_l, before, weights)
    back, low, out8, out4, out2, out1 = call(
        functools.partial(remote_kernel, capacity), "remote",
        (all_rows, shape((leaf_dev + 8, samples, width), jnp.bfloat16)) + (sent,) * 4,
        [SMEM] * 2 + [VMEM] * 8, [VMEM] * 6, 8, moved=heavy,
        scratch=[VMEM((leaf_dev + 8, samples, width), jnp.float32)],
    )(asked, slots, asked, left, before, from2, from1, from8, weights, factor)
    def back_by(x, reach):
        return passed(x, [(i, i - reach) for i in everyone if i >= reach])

    ring = passed(out1, [(i, i // 4 * 4 + (i + 3) % 4) for i in everyone])
    back8, back4, back2 = back_by(out8, 8), back_by(out4, 4), back_by(out2, 2)
    relayed = passed(ring, [(i, i - 4) for i in everyone if i >= 4 and i % 4 == 3])
    (part,) = call(
        home_kernel, "home", (all_rows,), [SMEM] + [VMEM] * 3, [VMEM], 6, moved=heavy,
        scratch=[VMEM((leaf_dev + 8, samples, width), jnp.float32)],
    )(home, back, low, weights)
    lists = (2, 4 * SLOTS)
    scratch = [VMEM(lists, jnp.int32), SMEM(lists, jnp.int32), pltpu.SemaphoreType.DMA]
    (part,) = call(
        functools.partial(far_kernel, capacity), "far", (all_rows,), [VMEM] * 3, [VMEM], 6,
        moved=2 * MIB, scratch=scratch,
    )(part, back8, back4)
    (gradient,) = call(
        functools.partial(add_kernel, capacity), "add", (all_rows,), [VMEM] * 4, [VMEM], 6,
        moved=2 * MIB, scratch=scratch,
    )(part, ring, back2, relayed)
    return gradient


def solution(mesh):
    return jax.shard_map(
        per_device,
        mesh=mesh,
        in_specs=(
            P(("groups", "kx"), None, None),
            P(("groups", "kx"), None),
            P(("groups", "kx"), None, None, None),
            P(("groups", "kx"), None, None),
        ),
        out_specs=P(("groups", "kx"), None, None),
        check_vma=False,
    )
```

```python
import functools

import jax
import jax.numpy as jnp
from jax import lax
from jax.experimental import pallas as pl
from jax.experimental.pallas import tpu as pltpu
from jax.sharding import PartitionSpec as P

SLOTS = 32
LEAVES = 80
MIB = 2**20
BY_ROWS = (((1,), (1,)), ((), ()))
VMEM, SMEM, HBM, ANY = pltpu.VMEM, pltpu.SMEM, pltpu.HBM, pl.ANY


def index_kernel(lists, latent, weights, asked, slots, home):
    fan, leaf_dev = lists.shape
    me = lax.axis_index("kx")
    behind = me * leaf_dev - lists[...]
    kind = (
        (behind > 0).astype(jnp.int32)
        + (behind > leaf_dev).astype(jnp.int32)
        + (behind > 2 * leaf_dev).astype(jnp.int32)
        + (behind > 4 * leaf_dev).astype(jnp.int32)
    )
    reach = jnp.where(kind == 4, 8, jnp.where(kind == 3, 4, kind))
    row = reach * leaf_dev - behind
    home[...] = jnp.where(kind == 0, row, leaf_dev)

    def grid(shape, dim):
        return lax.broadcasted_iota(jnp.int32, shape, dim)

    def low(x):
        return x.astype(jnp.float32).astype(jnp.bfloat16)

    every = 4 * fan
    mask = jnp.concatenate([(kind == o).astype(jnp.float32) for o in range(1, 5)], axis=0)
    earlier = low(grid((leaf_dev, leaf_dev), 0) < grid((leaf_dev, leaf_dev), 1))
    a, b = grid((every, every), 0), grid((every, every), 1)
    above = (b < a)
    for o in range(1, 4):
        above = above & ((a < o * fan) | (b >= o * fan))
    within = jnp.dot(low(mask), earlier, preferred_element_type=jnp.float32)
    base = jnp.sum(
        jnp.dot(low(above), low(mask), preferred_element_type=jnp.float32), axis=1, keepdims=True
    )
    place = jnp.where(mask > 0.0, within + base, -1.0)
    slot = grid((SLOTS, leaf_dev), 0).astype(jnp.float32)
    leaf = grid((1, leaf_dev), 1).astype(jnp.float32)
    ones = jnp.ones((1, leaf_dev), jnp.float32)
    total = jnp.zeros((8, 4 * SLOTS), jnp.float32)
    for k in range(fan):
        hit = jnp.concatenate(
            [(place[o * fan + k : o * fan + k + 1] == slot).astype(jnp.float32) for o in range(4)],
            axis=0,
        )
        facts = jnp.concatenate(
            [row[k : k + 1].astype(jnp.float32), leaf, k * ones, ones]
            + [jnp.zeros((4, leaf_dev), jnp.float32)], axis=0,
        )
        total = total + lax.dot_general(
            low(facts), low(hit), BY_ROWS, preferred_element_type=jnp.float32
        )
    asked[...] = total[0:1].astype(jnp.int32)
    slots[0:1] = jnp.where(total[3:4] > 0.0, total[1:2], float(leaf_dev)).astype(jnp.int32)
    slots[1:2] = total[2:3].astype(jnp.int32)


def beside(xs):
    return jnp.concatenate(xs, axis=1)


def below(xs):
    return jnp.concatenate(xs, axis=0)


def paired(x, y, left, right, by_rows=False):
    samples = x.shape[0]
    if by_rows:
        wide = left.shape[0]
        both = lax.dot_general(
            below([x, y]), below([left, right]), BY_ROWS, preferred_element_type=jnp.float32
        )
    else:
        wide = left.shape[1]
        both = jnp.dot(below([x, y]), beside([left, right]), preferred_element_type=jnp.float32)
    return both[:samples, :wide], both[samples:, wide:]


def local_kernel(home, latent, before, weights, left, rows):
    leaf_dev, fan, width = latent.shape[0], weights.shape[1], weights.shape[2]
    rows[pl.ds(0, leaf_dev)] = latent[...]
    rows[leaf_dev] = jnp.zeros(latent.shape[1:], latent.dtype)

    def some(c, carry):
        for u in range(LEAVES):
            i = c * LEAVES + u
            mean = jnp.dot(
                beside([rows[home[k, i]] for k in range(fan)]),
                weights[i].reshape(fan * width, width), preferred_element_type=jnp.float32,
            )
            left[i] = latent[i].astype(jnp.float32) - mean
        return carry

    lax.fori_loop(0, leaf_dev // LEAVES, some, 0)


def serve_kernel(capacity, ask1, ask2, ask8, latent, before, out8, out2, out1):
    me = lax.axis_index("kx")
    def pick(o, ask, rows, out):
        for r in range(capacity):
            out[r] = rows[ask[0, o * SLOTS + r]]

    pick(3, ask8, before, out8)
    for o, ask, out, bits in ((1, ask2, out2, 2), (0, ask1, out1, 3)):
        relays = lax.bitwise_and(me, bits) == bits

        @pl.when(relays)
        def _():
            pick(o, ask, before, out)

        @pl.when(jnp.logical_not(relays))
        def _():
            pick(o, ask, latent, out)


def asker(slots, weights, o, r):
    i = slots[0, o * SLOTS + r]
    return i, weights[jnp.minimum(i, weights.shape[0] - 1), slots[1, o * SLOTS + r]]


def remote_terms(capacity, slots, asked_row, low, weights, outs):
    listed = jnp.broadcast_to(asked_row[...].astype(jnp.float32), low.shape[1:])
    for o, out in outs:
        for r in range(0, capacity, 2):
            (i, w), (j, v) = asker(slots, weights, o, r), asker(slots, weights, o, r + 1)
            for at, x in zip((r, r + 1), paired(low[i], low[j], w, v, True)):
                out[at] = x.astype(out.dtype)
        out[capacity] = listed.astype(out.dtype)


def remote_kernel(
    capacity, asked, slots, asked_row, left, before, from2, from1, from8,
    weights, factor, back, low, out8, out4, out2, out1, resid,
):
    leaf_dev = back.shape[0]
    resid[pl.ds(0, leaf_dev)] = left[...]
    resid[leaf_dev] = jnp.zeros(left.shape[1:], left.dtype)
    low[leaf_dev] = jnp.zeros(left.shape[1:], low.dtype)

    for o, rows in ((2, before), (3, from8), (1, from2), (0, from1)):
        found = []
        for r in range(0, capacity, 2):
            (i, w), (j, v) = asker(slots, weights, o, r), asker(slots, weights, o, r + 1)
            at = (asked[0, o * SLOTS + r], asked[0, o * SLOTS + r + 1]) if o == 2 else (r, r + 1)
            found += zip((i, j), paired(rows[at[0]], rows[at[1]], w, v))
        for i, mean in found:
            resid[i] = resid[i] - mean

    def leaves(c, carry):
        pairs = [c * LEAVES + u for u in range(0, LEAVES, 2)]
        innov = [
            paired(
                resid[i].astype(jnp.bfloat16), resid[i + 1].astype(jnp.bfloat16),
                factor[i], factor[i + 1],
            )
            for i in pairs
        ]
        for i, (x, y) in zip(pairs, innov):
            both = paired(
                x.astype(jnp.bfloat16), y.astype(jnp.bfloat16), factor[i], factor[i + 1], True
            )
            for j, z in zip((i, i + 1), both):
                back[j] = z
                low[j] = z.astype(jnp.bfloat16)
        return carry

    lax.fori_loop(0, leaf_dev // LEAVES, leaves, 0)
    remote_terms(
        capacity, slots, asked_row, low, weights, ((3, out8), (2, out4), (1, out2), (0, out1))
    )


def home_kernel(home, back, low, weights, part, acc):
    leaf_dev = back.shape[0]
    fan, width = weights.shape[1], weights.shape[2]
    acc[pl.ds(0, leaf_dev)] = -back[...]
    acc[leaf_dev] = jnp.zeros(back.shape[1:], back.dtype)

    def some(c, carry):
        found = []
        for u in range(LEAVES):
            i = c * LEAVES + u
            found.append((i, lax.dot_general(
                low[i], weights[i].reshape(fan * width, width), BY_ROWS,
                preferred_element_type=jnp.float32,
            )))
        for i, x in found:
            for k in range(fan):
                j = home[k, i]
                acc[j] = acc[j] + x[:, k * width : (k + 1) * width]
        return carry

    lax.fori_loop(0, leaf_dev // LEAVES, some, 0)
    part[...] = acc[pl.ds(0, leaf_dev)]


def add_rows(capacity, returned, part, out, listed, wanted, sem):
    for n, (_, row) in enumerate(returned):
        listed[n : n + 1] = row(capacity)[0:1].astype(jnp.int32)
    fetch = pltpu.make_async_copy(listed, wanted, sem)
    fetch.start()
    out[...] = part[...]
    fetch.wait()
    for n, (o, row) in enumerate(returned):
        for r in range(capacity):
            j = wanted[n, o * SLOTS + r]
            out[j] = out[j] + row(r)


def far_kernel(capacity, part, back8, back2, out, listed, wanted, sem):
    returned = [(o, lambda r, x=x: x[r].astype(jnp.float32)) for o, x in ((3, back8), (1, back2))]
    add_rows(capacity, returned, part, out, listed, wanted, sem)


def add_kernel(capacity, part, ring, back4, relayed, out, listed, wanted, sem):
    last = lax.bitwise_and(lax.axis_index("kx"), 3) == 3

    def back1(r):
        return jnp.where(last, relayed[r].astype(jnp.float32), ring[r].astype(jnp.float32))

    returned = [(2, lambda r: back4[r].astype(jnp.float32)), (0, back1)]
    add_rows(capacity, returned, part, out, listed, wanted, sem)


def call(body, name, out_shape, ins, outs, limit, flops=0, moved=0, scratch=(), aliases={}):
    spec = lambda space: pl.BlockSpec(memory_space=space)
    return pl.pallas_call(
        body,
        out_shape=out_shape,
        in_specs=[spec(space) for space in ins],
        out_specs=tuple(spec(space) for space in outs),
        scratch_shapes=scratch,
        input_output_aliases=aliases,
        compiler_params=pltpu.CompilerParams(vmem_limit_bytes=limit * MIB),
        cost_estimate=pl.CostEstimate(flops=flops, bytes_accessed=moved, transcendentals=0),
        name=name,
    )


def placed(x, space):
    return pltpu.with_memory_space_constraint(x, space)


def per_device(latent, cond_lists, cond_weights, precision_factor):
    devices = lax.axis_size("kx")
    leaf_dev, samples, width = latent.shape
    fan = cond_lists.shape[1]
    capacity = fan * leaf_dev // 8
    everyone = range(devices)
    shape = jax.ShapeDtypeStruct
    some_rows = shape((capacity, samples, width), jnp.bfloat16)
    sent = shape((capacity + 1, samples, width), jnp.bfloat16)
    all_rows = shape(latent.shape, jnp.float32)
    one_list = shape((1, 4 * SLOTS), jnp.int32)
    heavy = cond_weights.size * 2

    def passed(x, route):
        return lax.ppermute(x, "kx", route)

    before = passed(latent, [(i, i + 4) for i in everyone if i + 4 < devices])
    weights, factor = placed(cond_weights, VMEM), placed(precision_factor, VMEM)
    held_l = placed(latent, VMEM)
    asked, slots, home = call(
        index_kernel, "index",
        (one_list, shape((2, 4 * SLOTS), jnp.int32), shape((fan, leaf_dev), jnp.int32)),
        [VMEM, HBM, HBM], [VMEM] * 3, 4, moved=2 * MIB,
    )(placed(cond_lists.T, HBM), placed(latent, HBM), placed(cond_weights, HBM))
    ask8 = passed(asked, [(i, i - 4) for i in everyone if i >= 4])
    ask2 = passed(asked, [(i, i ^ 2) for i in everyone])
    ask1 = passed(asked, [(i, i // 4 * 4 + (i + 3) % 4) for i in everyone])
    serve8, serve2, serve1 = call(
        functools.partial(serve_kernel, capacity), "serve", (some_rows,) * 3,
        [SMEM] * 3 + [VMEM] * 2, [VMEM] * 3, 4, moved=4 * MIB,
    )(ask1, ask2, ask8, held_l, before)
    from8 = passed(serve8, [(i, i + 4) for i in everyone if i >= 4 and i + 4 < devices])
    from2 = passed(serve2, [(i, i ^ 2) for i in everyone])
    from1 = passed(serve1, [(i, i // 4 * 4 + (i + 1) % 4) for i in everyone])
    (left,) = call(
        local_kernel, "local", (all_rows,), [SMEM, VMEM, ANY, VMEM], [VMEM], 6, moved=heavy,
        scratch=[VMEM((leaf_dev + 8, samples, width), jnp.bfloat16)],
    )(home, held_l, before, weights)
    back, low, out8, out4, out2, out1 = call(
        functools.partial(remote_kernel, capacity), "remote",
        (all_rows, shape((leaf_dev + 8, samples, width), jnp.bfloat16)) + (sent,) * 4,
        [SMEM] * 2 + [VMEM] * 8, [VMEM] * 6, 8, moved=heavy,
        scratch=[VMEM((leaf_dev + 8, samples, width), jnp.float32)],
    )(asked, slots, asked, left, before, from2, from1, from8, weights, factor)
    def back_by(x, reach):
        return passed(x, [(i, i - reach) for i in everyone if i >= reach])

    ring = passed(out1, [(i, i // 4 * 4 + (i + 3) % 4) for i in everyone])
    back8, back4, back2 = back_by(out8, 8), back_by(out4, 4), back_by(out2, 2)
    relayed = passed(ring, [(i, i - 4) for i in everyone if i >= 4 and i % 4 == 3])
    (part,) = call(
        home_kernel, "home", (all_rows,), [SMEM] + [VMEM] * 3, [VMEM], 6, moved=heavy,
        scratch=[VMEM((leaf_dev + 8, samples, width), jnp.float32)],
    )(home, back, low, weights)
    lists = (2, 4 * SLOTS)
    scratch = [VMEM(lists, jnp.int32), SMEM(lists, jnp.int32), pltpu.SemaphoreType.DMA]
    (part,) = call(
        functools.partial(far_kernel, capacity), "far", (all_rows,), [VMEM] * 3, [VMEM], 6,
        moved=2 * MIB, scratch=scratch,
    )(part, back8, back2)
    (gradient,) = call(
        functools.partial(add_kernel, capacity), "add", (all_rows,), [VMEM] * 4, [VMEM], 6,
        moved=2 * MIB, scratch=scratch,
    )(part, ring, back4, relayed)
    return gradient


def solution(mesh):
    return jax.shard_map(
        per_device,
        mesh=mesh,
        in_specs=(
            P(("groups", "kx"), None, None),
            P(("groups", "kx"), None),
            P(("groups", "kx"), None, None, None),
            P(("groups", "kx"), None, None),
        ),
        out_specs=P(("groups", "kx"), None, None),
        check_vma=False,
    )
```
